32 devices in a mesh: seq: 4 (over y, core), head: 4 (over z), role: 2 (over x).
Axes of the slice: x: 2, y: 2, z: 4, core: 2. Of those that a mesh axis runs over, the one named last changes fastest.
Arguments:
- prefill_queries: bfloat16 [2, 1024, 8192], P(None, 'seq', ('head', 'role')), may hold values from -64 to 64
- prefill_keys: bfloat16 [2, 1024, 1024], P(None, 'seq', ('head', 'role')), may hold values from -4 to 4
- prefill_values: bfloat16 [2, 1024, 1024], P(None, 'seq', ('head', 'role')), may hold values from -4 to 4
- prompt_len: int32 [2], replicated, may hold values from 512 to 1024, as said below
- assignment: int32 [16], P(('seq', 'role')), may hold values from 0 to 1
- cache_len: int32 [16], P(('seq', 'role')), may hold values from 8 to 1024, as said below
- cache_keys: bfloat16 [16, 1024, 1024], P(('seq', 'role'), None, 'head'), may hold values from -4 to 4
- cache_values: bfloat16 [16, 1024, 1024], P(('seq', 'role'), None, 'head'), may hold values from -4 to 4
- decode_queries: bfloat16 [4, 16, 8192], P(None, ('seq', 'role'), 'head'), may hold values from -64 to 64
- new_keys: bfloat16 [4, 16, 1024], P(None, ('seq', 'role'), 'head'), may hold values from -4 to 4
- new_values: bfloat16 [4, 16, 1024], P(None, ('seq', 'role'), 'head'), may hold values from -4 to 4
Outputs:
- prefill_out: bfloat16 [2, 1024, 8192], P(None, 'seq', ('head', 'role'))
- decode_out: bfloat16 [4, 16, 8192], P(None, ('seq', 'role'), 'head')
The draws below stay inside these ranges and needn't reach their ends.
Inputs may be any that keep to these rules, and one draw needn't show every extreme that they name: `prompt_len`: one prompt of every draw holds all 1024 positions. `cache_len`: the own cache of some decode row is full in every draw.
All inputs are finite; a program needn't handle non-finite values.
Results may differ from the reference program's by a relative error of at most 0.0038.
Values may be sent and summed in bfloat16 or wider, within the bound.
No kernel may reach another device: no remote copies, remote signals or barrier semaphores. Data moves between devices by JAX's collectives and lax.ppermute only.
A program may use at most 192 MiB of HBM per device.

```python
import jax
import jax.numpy as jnp
from jax import lax

Q_HEADS = 64
KV_HEADS = 8
D_HEAD = 128
PF_ROWS = 2
PF_LEN = 1024
DEC_ROWS = 16
CACHE = 1024
STEPS = 4


def prompt_key_base(key):
    key = jax.random.fold_in(key, 71)
    draw_shape = (PF_ROWS, PF_LEN, KV_HEADS, D_HEAD)
    drawn_draw = jnp.clip(jax.random.normal(key, draw_shape, jnp.float32), -4.0, 4.0)
    return drawn_draw


def cache_key_base(key):
    key = jax.random.fold_in(key, 73)
    draw_shape = (DEC_ROWS, CACHE, KV_HEADS, D_HEAD)
    drawn_draw = jnp.clip(jax.random.normal(key, draw_shape, jnp.float32), -4.0, 4.0)
    return drawn_draw


def draw_prefill_keys(key, part):
    drawn_draw = prompt_key_base(key)
    result = drawn_draw
    return result.reshape(PF_ROWS, PF_LEN, KV_HEADS * D_HEAD).astype(jnp.bfloat16)


def draw_prefill_queries(key, part):
    key = jax.random.fold_in(key, 5)
    draw_shape = (PF_ROWS, PF_LEN, KV_HEADS, Q_HEADS // KV_HEADS, D_HEAD)
    result = jnp.clip(2.0 * jax.random.normal(key, draw_shape, jnp.float32), -8.0, 8.0)
    return result.reshape(PF_ROWS, PF_LEN, Q_HEADS * D_HEAD).astype(jnp.bfloat16)


def draw_cache_keys(key, part):
    drawn_draw = cache_key_base(key)
    result = drawn_draw
    return result.reshape(DEC_ROWS, CACHE, KV_HEADS * D_HEAD).astype(jnp.bfloat16)


def draw_decode_queries(key, part):
    key = jax.random.fold_in(key, 9)
    draw_shape = (STEPS, DEC_ROWS, KV_HEADS, Q_HEADS // KV_HEADS, D_HEAD)
    result = jnp.clip(2.0 * jax.random.normal(key, draw_shape, jnp.float32), -8.0, 8.0)
    return result.reshape(STEPS, DEC_ROWS, Q_HEADS * D_HEAD).astype(jnp.bfloat16)


def draw_prompt_len(key, part):
    key = jax.random.fold_in(key, 11)
    lengths = jax.random.randint(key, (PF_ROWS,), PF_LEN // 2, PF_LEN + 1)
    full_row = jax.random.randint(jax.random.fold_in(key, 1), (), 0, PF_ROWS)
    return jnp.where(jnp.arange(PF_ROWS) == full_row, PF_LEN, lengths).astype(jnp.int32)


def draw_cache_len(key, part):
    key = jax.random.fold_in(key, 13)
    lengths = jax.random.randint(key, (DEC_ROWS,), 8, CACHE + 1)
    full_row = jax.random.randint(jax.random.fold_in(key, 1), (), 0, DEC_ROWS)
    return jnp.where(jnp.arange(DEC_ROWS) == full_row, CACHE, lengths).astype(jnp.int32)


def place_ends(array, key, low, high):
    longest = array.shape.index(max(array.shape))
    spots = []
    for shift in (0, 1):
        where = [jax.random.randint(jax.random.fold_in(key, axis), (), 0, length) for axis, length in enumerate(array.shape)]
        where[longest] = (where[longest] + shift) % array.shape[longest]
        spots.append(tuple(where))
    return array.at[spots[0]].set(low).at[spots[1]].set(high)


def steps_of(key, shape, cuts, least, high):
    factor_of, own = 1.0, jax.random.fold_in(key, 6)
    for dim, parts in cuts:
        draws = jnp.exp(jax.random.uniform(jax.random.fold_in(own, dim), (parts,), jnp.float32, least / len(cuts), high / len(cuts)))
        factor_of = factor_of * jnp.repeat(draws, shape[dim] // parts).reshape([-1 if axis == dim else 1 for axis in range(len(shape))])
    return factor_of


def bell_draw(own_key, dims, deviation, limit, split=(), held_as=jnp.bfloat16):
    gain = steps_of(own_key, dims, split, -0.22, 0.18) if split else 1.0
    values = jax.random.normal(own_key, dims, jnp.float32) * deviation * gain
    return jnp.minimum(jnp.maximum(values, -limit), limit).astype(held_as)


def setup_inputs(seed: int = 0) -> dict:
    streams_of = jax.random.split(jax.random.key(seed), 12)
    return {
        "prefill_queries": draw_prefill_queries(jax.random.fold_in(streams_of[11], 71), 0),
        "prefill_keys": draw_prefill_keys(jax.random.fold_in(streams_of[11], 71), 0),
        "prefill_values": bell_draw(streams_of[2], (PF_ROWS, PF_LEN, KV_HEADS * D_HEAD), 1.0, 4.0, ((1, 4), (2, 8))),
        "prompt_len": draw_prompt_len(jax.random.fold_in(streams_of[11], 71), 0),
        "assignment": place_ends(jax.random.randint(streams_of[4], (DEC_ROWS,), 0, PF_ROWS), jax.random.fold_in(streams_of[4], 1), 0, PF_ROWS - 1).astype(jnp.int32),
        "cache_len": draw_cache_len(jax.random.fold_in(streams_of[11], 71), 0),
        "cache_keys": draw_cache_keys(jax.random.fold_in(streams_of[11], 71), 0),
        "cache_values": bell_draw(streams_of[7], (DEC_ROWS, CACHE, KV_HEADS * D_HEAD), 1.0, 4.0, ((0, 8), (2, 4))),
        "decode_queries": draw_decode_queries(jax.random.fold_in(streams_of[11], 71), 0),
        "new_keys": bell_draw(streams_of[9], (STEPS, DEC_ROWS, KV_HEADS * D_HEAD), 1.0, 4.0, ((1, 8), (2, 4))),
        "new_values": bell_draw(streams_of[10], (STEPS, DEC_ROWS, KV_HEADS * D_HEAD), 1.0, 4.0, ((1, 8), (2, 4))),
    }


MASKED_SCORE = -1e30


def rounded(weights):
    return lax.optimization_barrier(weights.astype(jnp.bfloat16)).astype(jnp.float32)


def prefill_part(prefill_queries, prefill_keys, prefill_values, prompt_len):
    group_size = Q_HEADS // KV_HEADS
    score_scale = D_HEAD ** -0.5
    queries = prefill_queries.reshape(PF_ROWS, PF_LEN, KV_HEADS, group_size, D_HEAD).astype(jnp.float32)
    key_rows = prefill_keys.reshape(PF_ROWS, PF_LEN, KV_HEADS, D_HEAD).astype(jnp.float32)
    value_rows = prefill_values.reshape(PF_ROWS, PF_LEN, KV_HEADS, D_HEAD).astype(jnp.float32)
    position = jnp.arange(PF_LEN, dtype=jnp.int32)
    allowed = position[None, :] <= position[:, None]

    def one_head(items):
        head_queries, head_keys, head_values = items
        scores = jnp.einsum("rpgd,rkd->rgpk", head_queries, head_keys, precision=lax.Precision.HIGHEST) * score_scale
        scores = jnp.where(allowed, scores, MASKED_SCORE)
        top_score = jnp.max(scores, axis=-1)
        weights = jnp.where(allowed, jnp.exp(scores - top_score[..., None]), 0.0)
        weight_sum = jnp.sum(weights, axis=-1)
        summed = jnp.einsum("rgpk,rkd->rpgd", rounded(weights), head_values, precision=lax.Precision.HIGHEST)
        return summed / jnp.transpose(weight_sum, (0, 2, 1))[..., None]

    result = lax.map(one_head, (jnp.moveaxis(queries, 2, 0), jnp.moveaxis(key_rows, 2, 0), jnp.moveaxis(value_rows, 2, 0)))
    result = jnp.moveaxis(result, 0, 2)
    live_rows = position[None, :] < prompt_len[:, None]
    result = jnp.where(live_rows[:, :, None, None, None], result, 0.0)
    return result.reshape(PF_ROWS, PF_LEN, Q_HEADS * D_HEAD).astype(jnp.bfloat16)


def decode_part(prefill_keys, prefill_values, prompt_len, assignment, cache_len, cache_keys, cache_values, decode_queries, new_keys, new_values):
    group_size = Q_HEADS // KV_HEADS
    score_scale = D_HEAD ** -0.5
    prompt_keys = prefill_keys.reshape(PF_ROWS, PF_LEN, KV_HEADS, D_HEAD)
    prompt_values = prefill_values.reshape(PF_ROWS, PF_LEN, KV_HEADS, D_HEAD)
    prompt_pos = jnp.arange(PF_LEN, dtype=jnp.int32)
    cache_pos = jnp.arange(CACHE, dtype=jnp.int32)
    step_pos = jnp.arange(STEPS, dtype=jnp.int32)

    def one_row(items):
        which, own_len, own_keys, own_values, row_queries, row_new_keys, row_new_values = items
        chosen_keys = lax.dynamic_index_in_dim(prompt_keys, which, 0, keepdims=False)
        chosen_values = lax.dynamic_index_in_dim(prompt_values, which, 0, keepdims=False)
        chosen_len = lax.dynamic_index_in_dim(prompt_len, which, 0, keepdims=False)
        context_keys = jnp.concatenate([chosen_keys, own_keys.reshape(CACHE, KV_HEADS, D_HEAD), row_new_keys.reshape(STEPS, KV_HEADS, D_HEAD)], axis=0).astype(jnp.float32)
        context_values = jnp.concatenate([chosen_values, own_values.reshape(CACHE, KV_HEADS, D_HEAD), row_new_values.reshape(STEPS, KV_HEADS, D_HEAD)], axis=0).astype(jnp.float32)
        allowed = jnp.concatenate([
            jnp.broadcast_to(prompt_pos[None, :] < chosen_len, (STEPS, PF_LEN)),
            jnp.broadcast_to(cache_pos[None, :] < own_len, (STEPS, CACHE)),
            step_pos[None, :] <= step_pos[:, None]], axis=1)
        queries = row_queries.reshape(STEPS, KV_HEADS, group_size, D_HEAD).astype(jnp.float32)
        scores = jnp.einsum("tngd,knd->ngtk", queries, context_keys, precision=lax.Precision.HIGHEST) * score_scale
        scores = jnp.where(allowed, scores, MASKED_SCORE)
        top_score = jnp.max(scores, axis=-1)
        weights = jnp.where(allowed, jnp.exp(scores - top_score[..., None]), 0.0)
        weight_sum = jnp.sum(weights, axis=-1)
        summed = jnp.einsum("ngtk,knd->tngd", rounded(weights), context_values, precision=lax.Precision.HIGHEST)
        result = summed / jnp.transpose(weight_sum, (2, 0, 1))[..., None]
        return result.reshape(STEPS, Q_HEADS * D_HEAD)

    result = lax.map(one_row, (assignment, cache_len, cache_keys, cache_values, jnp.moveaxis(decode_queries, 1, 0), jnp.moveaxis(new_keys, 1, 0), jnp.moveaxis(new_values, 1, 0)))
    return jnp.moveaxis(result, 0, 1).astype(jnp.bfloat16)


def reference(prefill_queries, prefill_keys, prefill_values, prompt_len, assignment, cache_len, cache_keys, cache_values, decode_queries, new_keys, new_values):
    prefill_out = prefill_part(prefill_queries, prefill_keys, prefill_values, prompt_len)
    decode_out = decode_part(prefill_keys, prefill_values, prompt_len, assignment, cache_len, cache_keys, cache_values, decode_queries, new_keys, new_values)
    return (prefill_out, decode_out)
```

```python
import functools
import math

import jax
import jax.numpy as jnp
from jax import lax
from jax.experimental import pallas as pl
from jax.experimental.pallas import tpu as pltpu
from jax.sharding import PartitionSpec as P

D_HEAD = 128
MASKED_SCORE = -1e30
EXP2_SCALE = D_HEAD**-0.5 * math.log2(math.e)
VMEM_BYTES = 40 * 2**20
NT = (((1,), (1,)), ((), ()))


def scores_of(queries, keys):
    return lax.dot_general(queries, keys, NT, preferred_element_type=jnp.float32)


def weighted(weights, values):
    return jnp.dot(weights.astype(jnp.bfloat16), values, preferred_element_type=jnp.float32)


def eye_of(rows):
    shape = (rows, 128)
    return lax.broadcasted_iota(jnp.int32, shape, 0) == lax.broadcasted_iota(jnp.int32, shape, 1)


def column_to_row(column):
    spread = jnp.where(eye_of(column.shape[0]), column, 0.0)
    return jnp.sum(spread, axis=0, keepdims=True)


def row_to_column(row, rows):
    spread = jnp.where(eye_of(rows), jnp.broadcast_to(row, (rows, 128)), 0.0)
    return jnp.sum(spread, axis=1, keepdims=True)


def soft_parts(score_parts, masks, value_parts):
    masked = [jnp.where(mask, part * EXP2_SCALE, MASKED_SCORE) for part, mask in zip(score_parts, masks)]
    top = functools.reduce(jnp.maximum, [jnp.max(part, axis=1, keepdims=True) for part in masked])
    total = jnp.zeros_like(top)
    summed = jnp.zeros((top.shape[0], D_HEAD), jnp.float32)
    for part, mask, values in zip(masked, masks, value_parts):
        weights = jnp.where(mask, jnp.exp2(part - top), 0.0)
        total = total + jnp.sum(weights, axis=1, keepdims=True)
        summed = summed + weighted(weights, values)
    return summed, top, total


def pack_kernel(asg_ref, dq_ref, own_ref, other_ref, flat):
    steps, rows, columns = dq_ref.shape
    span = steps * rows
    for step in range(steps):
        flat[step * rows : (step + 1) * rows, :] = dq_ref[step].astype(jnp.float32)
    role = lax.axis_index("role")
    half = columns // 2
    group = half // D_HEAD
    row_index = lax.broadcasted_iota(jnp.int32, (span, 128), 0) % rows
    prompt = jnp.zeros((span, 128), jnp.float32)
    for row in range(rows):
        prompt = jnp.where(row_index == row, asg_ref[row].astype(jnp.float32), prompt)
    for out, kv in ((own_ref, role), (other_ref, 1 - role)):
        for pair in range(group // 2):
            two = [
                flat[:, pl.ds(pl.multiple_of(kv * half + (2 * pair + i) * D_HEAD, D_HEAD), D_HEAD)] for i in (0, 1)
            ]
            out[2 * span * pair : 2 * span * (pair + 1), :] = jnp.concatenate(two, axis=0).astype(jnp.bfloat16)
        out[span * group : span * (group + 2), :] = jnp.concatenate([prompt, prompt], axis=0).astype(jnp.bfloat16)


def cache_kernel(rows, steps, len_ref, own_ref, other_ref, ck_ref, cv_ref, nk_ref, nv_ref, sum_ref, top_ref, tot_ref, fk, fv):
    span = steps * rows
    queries = own_ref.shape[0] - 2 * span
    role = lax.axis_index("role")
    slots = ck_ref.shape[1]
    fk[...] = jnp.zeros_like(fk)
    fv[...] = jnp.zeros_like(fv)
    for step in range(steps):
        fk[step * rows : (step + 1) * rows, :] = nk_ref[step].astype(jnp.float32)
        fv[step * rows : (step + 1) * rows, :] = nv_ref[step].astype(jnp.float32)
    q_index = lax.broadcasted_iota(jnp.int32, (queries, 1), 0) % span
    q_step, q_row = q_index // rows, q_index % rows
    lane = lax.broadcasted_iota(jnp.int32, (queries, 128), 1)
    fresh_mask = (lane < span) & (lane % rows == q_row) & (lane // rows <= q_step)
    slot = lax.broadcasted_iota(jnp.int32, (queries, slots), 1)
    for index, (message, kv) in enumerate(((own_ref, role), (other_ref, 1 - role))):
        q = message[:queries, :]
        columns = pl.ds(pl.multiple_of(kv * D_HEAD, D_HEAD), D_HEAD)
        parts = [scores_of(q, fk[:, columns].astype(jnp.bfloat16))]
        masks = [fresh_mask]
        values = [fv[:, columns].astype(jnp.bfloat16)]
        for row in range(rows):
            parts.append(scores_of(q, ck_ref[row, :, columns]))
            masks.append((slot < len_ref[row]) & (q_row == row))
            values.append(cv_ref[row, :, columns])
        summed, top, total = soft_parts(parts, masks, values)
        sum_ref[index] = summed
        top_ref[index] = jnp.broadcast_to(top, (queries, 128))
        tot_ref[index] = jnp.broadcast_to(total, (queries, 128))


def jobs_over(q, prompt, plen_ref, chunks):
    parts, masks, values = [], [], []
    count = q.shape[0]
    for first, keys, vals in chunks:
        position = first + lax.broadcasted_iota(jnp.int32, (count, keys.shape[1]), 1)
        for row in range(keys.shape[0]):
            parts.append(scores_of(q, keys[row]))
            masks.append((position < plen_ref[row]) & (prompt == row))
            values.append(vals[row])
    return soft_parts(parts, masks, values)


def prompt_column(message, span, queries):
    eight = message[queries : queries + 2 * span, :].astype(jnp.float32)[:span, :1]
    return jnp.concatenate([eight] * (queries // span), axis=0)


def jobs_kernel(span, count, plen_ref, *refs):
    messages = refs[:count]
    k_own, v_own, k_near, v_near = refs[count : count + 4]
    outs = refs[count + 4 :]
    queries = messages[0].shape[0] - 2 * span
    seq = lax.axis_index("seq")
    length = k_own.shape[1]
    q = jnp.concatenate([m[:queries, :] for m in messages], axis=0)
    prompt = jnp.concatenate([prompt_column(m, span, queries) for m in messages], axis=0)
    near = seq + 1 - 2 * (seq % 2)
    summed, top, total = jobs_over(
        q, prompt, plen_ref, [(seq * length, k_own, v_own), (near * length, k_near, v_near)]
    )
    for index, out in enumerate(outs):
        rows = slice(index * queries, (index + 1) * queries)
        out[:queries, :] = summed[rows]
        out[queries : queries + 8, :] = jnp.concatenate(
            [column_to_row(top[rows]), column_to_row(total[rows]), jnp.zeros((6, 128), jnp.float32)], axis=0
        )


def local_kernel(q_ref, k_own, v_own, k_near, v_near, sum_ref, top_ref, tot_ref, ones):
    prompts, length, columns = q_ref.shape
    group = columns // D_HEAD
    seq = lax.axis_index("seq")
    ones[:, :, D_HEAD:] = jnp.ones((prompts, 2 * length, D_HEAD), jnp.bfloat16)
    ones[:, :length, :D_HEAD] = v_own[...]
    ones[:, length:, :D_HEAD] = v_near[...]
    causal = lax.broadcasted_iota(jnp.int32, (length, length), 1) <= lax.broadcasted_iota(
        jnp.int32, (length, length), 0
    )

    def run(with_near):
        for row in range(prompts):
            for head in range(group):
                cols = slice(head * D_HEAD, (head + 1) * D_HEAD)
                q = q_ref[row, :, cols]
                own = jnp.where(causal, scores_of(q, k_own[row]), MASKED_SCORE)
                top = jnp.max(own, axis=1, keepdims=True)
                if with_near:
                    near = scores_of(q, k_near[row])
                    top = jnp.maximum(top, jnp.max(near, axis=1, keepdims=True))
                top = top * EXP2_SCALE
                summed = weighted(jnp.exp2(own * EXP2_SCALE - top), ones[row, :length, :])
                if with_near:
                    summed = summed + weighted(jnp.exp2(near * EXP2_SCALE - top), ones[row, length:, :])
                sum_ref[row, :, cols] = summed[:, :D_HEAD]
                tot_ref[row, :, cols] = summed[:, D_HEAD:]
                top_ref[row, :, cols] = jnp.broadcast_to(top, (length, D_HEAD))

    @pl.when(seq % 2 == 0)
    def _():
        run(False)

    @pl.when(seq % 2 == 1)
    def _():
        run(True)


def far_scores_kernel(shift, q_ref, k_one, k_two, sum_in, top_in, tot_in, w_ref, sum_ref, top_ref, tot_ref):
    prompts, length, columns = q_ref.shape
    group = columns // D_HEAD

    @pl.when(lax.axis_index("seq") // 2 >= shift)
    def _():
        for row in range(prompts):
            for head in range(group):
                cols = slice(head * D_HEAD, (head + 1) * D_HEAD)
                q = q_ref[row, :, cols]
                one = scores_of(q, k_one[row])
                two = scores_of(q, k_two[row])
                new = jnp.maximum(jnp.max(one, axis=1, keepdims=True), jnp.max(two, axis=1, keepdims=True))
                old = top_in[row, :, cols]
                top = jnp.maximum(old, new * EXP2_SCALE)
                wide = jnp.concatenate([top] * (length // D_HEAD), axis=1)
                w_ref[row, head, :, :length] = jnp.exp2(one * EXP2_SCALE - wide).astype(jnp.bfloat16)
                w_ref[row, head, :, length:] = jnp.exp2(two * EXP2_SCALE - wide).astype(jnp.bfloat16)
                alpha = jnp.exp2(old - top)
                sum_ref[row, :, cols] = sum_in[row, :, cols] * alpha
                tot_ref[row, :, cols] = tot_in[row, :, cols] * alpha
                top_ref[row, :, cols] = top


def far_values_kernel(shift, last, span, n_other, n_own, *refs):
    plen_ref, w_ref, k_one, v_one, k_two, v_two, sum_in, tot_in, own_msg = refs[:9]
    rest = refs[9:]
    prompts, length, columns = sum_in.shape
    group = columns // D_HEAD
    seq = lax.axis_index("seq")
    role = lax.axis_index("role")
    pairs = lax.axis_size("seq") // 2
    outer = seq // 2
    queries = own_msg.shape[0] - 2 * span
    if last:
        cache_sum, cache_top, cache_tot = rest[:3]
        own_parts = rest[3 : 3 + n_own]
        other_parts = rest[3 + n_own : 3 + n_own + n_other]
        late_parts = rest[3 + n_own + n_other : -6]
        out_ref, dec_ref, late_ref, flat, ones_one, ones_two = rest[-6:]
    else:
        sum_ref, tot_ref, late_ref, ones_one, ones_two = rest

    def finish(row, cols, summed, total):
        if last:
            position = seq * length + lax.broadcasted_iota(jnp.int32, (length, D_HEAD), 0)
            result = jnp.where(position < plen_ref[row], summed / total, 0.0)
            out_ref[row, :, cols] = result.astype(jnp.bfloat16)
        else:
            sum_ref[row, :, cols] = summed
            tot_ref[row, :, cols] = total

    @pl.when(outer >= shift)
    def _():
        for ones, vals in ((ones_one, v_one), (ones_two, v_two)):
            ones[:, :, :D_HEAD] = vals[...]
            ones[:, :, D_HEAD:] = jnp.ones((prompts, length, D_HEAD), jnp.bfloat16)
        for row in range(prompts):
            for head in range(group):
                cols = slice(head * D_HEAD, (head + 1) * D_HEAD)
                far = jnp.dot(w_ref[row, head, :, :length], ones_one[row], preferred_element_type=jnp.float32)
                far = far + jnp.dot(w_ref[row, head, :, length:], ones_two[row], preferred_element_type=jnp.float32)
                finish(row, cols, sum_in[row, :, cols] + far[:, :D_HEAD], tot_in[row, :, cols] + far[:, D_HEAD:])
        near = 1 - 2 * (seq % 2)
        first = (seq - 2 * shift) * length
        summed, top, total = jobs_over(
            own_msg[:queries, :],
            prompt_column(own_msg, span, queries),
            plen_ref,
            [(first, k_one, v_one), (first + near * length, k_two, v_two)],
        )
        late_ref[:queries, :] = summed
        late_ref[queries : queries + 8, :] = jnp.concatenate(
            [column_to_row(top), column_to_row(total), jnp.zeros((6, 128), jnp.float32)], axis=0
        )

    @pl.when(outer < shift)
    def _():
        for row in range(prompts):
            for head in range(group):
                cols = slice(head * D_HEAD, (head + 1) * D_HEAD)
                finish(row, cols, sum_in[row, :, cols], tot_in[row, :, cols])
        late_ref[...] = jnp.zeros_like(late_ref)

    if not last:
        return
    half = group * D_HEAD
    lates = [(part, outer >= s + 1) for s, part in enumerate(list(late_parts) + [late_ref])]
    owns = [(own_parts[0], True)] + [(part, outer + s + 1 < pairs) for s, part in enumerate(own_parts[1:])]
    others = [(part, True) for part in other_parts]
    for index, (parts, kv) in enumerate(((owns + lates, role), (others, 1 - role))):
        sums, tops, tots = [cache_sum[index]], [cache_top[index][:, :1]], [cache_tot[index][:, :1]]
        for part, valid in parts:
            top = row_to_column(part[queries : queries + 1, :], queries)
            total = row_to_column(part[queries + 1 : queries + 2, :], queries)
            summed = part[:queries, :]
            if valid is not True:
                top = jnp.where(valid, top, MASKED_SCORE)
                total = jnp.where(valid, total, 0.0)
                summed = jnp.where(valid, summed, 0.0)
            sums.append(summed)
            tops.append(top)
            tots.append(total)
        high = functools.reduce(jnp.maximum, tops)
        factors = [jnp.exp2(top - high) for top in tops]
        summed = functools.reduce(jnp.add, [f * s for f, s in zip(factors, sums)])
        total = functools.reduce(jnp.add, [f * t for f, t in zip(factors, tots)])
        result = summed / total
        for head in range(group):
            start = pl.multiple_of(kv * half + head * D_HEAD, D_HEAD)
            flat[:, pl.ds(start, D_HEAD)] = result[head * span : (head + 1) * span]
    steps, rows, _ = dec_ref.shape
    for step in range(steps):
        dec_ref[step] = flat[step * rows : (step + 1) * rows, :].astype(jnp.bfloat16)


VMEM = pl.BlockSpec(memory_space=pltpu.VMEM)
SMEM = pl.BlockSpec(memory_space=pltpu.SMEM)


def call(kernel, args, outs, scratch=(), scalars=1, aliases=None, flops=0, moved=0):
    return pl.pallas_call(
        kernel,
        out_shape=outs,
        in_specs=[SMEM] * scalars + [VMEM] * (len(args) - scalars),
        out_specs=[VMEM] * len(outs),
        scratch_shapes=list(scratch),
        input_output_aliases=aliases or {},
        compiler_params=pltpu.CompilerParams(vmem_limit_bytes=VMEM_BYTES),
        cost_estimate=pl.CostEstimate(flops=flops, bytes_accessed=moved, transcendentals=0),
    )(*args)


def body(
    prefill_queries,
    prefill_keys,
    prefill_values,
    prompt_len,
    assignment,
    cache_len,
    cache_keys,
    cache_values,
    decode_queries,
    new_keys,
    new_values,
):
    seqs, roles = lax.axis_size("seq"), lax.axis_size("role")
    pairs = seqs // 2
    prompts, length, columns = prefill_queries.shape
    steps, rows, dec_columns = decode_queries.shape
    group = columns // D_HEAD
    span = steps * rows
    queries = group * span
    f32, bf16 = jnp.float32, jnp.bfloat16
    shape = jax.ShapeDtypeStruct

    swap = [(i, i ^ 1) for i in range(seqs)]

    def near(x):
        return lax.ppermute(x, "seq", swap)

    def forward(x, shift):
        return lax.ppermute(x, "seq", [(i, i + 2 * shift) for i in range(seqs - 2 * shift)])

    def back(x, shift):
        return lax.ppermute(x, "seq", [(i + 2 * shift, i) for i in range(seqs - 2 * shift)])

    def across(x, shift):
        moves = [
            (i * roles + r, (i + 2 * shift) % seqs * roles + (1 - r)) for i in range(seqs) for r in range(roles)
        ]
        return lax.ppermute(x, ("seq", "role"), moves)

    shifts = range(1, pairs)
    far_keys = [forward(prefill_keys, s) for s in shifts]
    far_values = [forward(prefill_values, s) for s in shifts]
    near_keys, near_values = near(prefill_keys), near(prefill_values)
    message = shape((queries + 2 * span, 128), bf16)
    own_msg, other_msg = call(
        pack_kernel, (assignment, decode_queries), [message] * 2, [pltpu.VMEM((span, dec_columns), f32)]
    )
    other_msgs = [across(other_msg, s) for s in range(pairs)]
    own_msgs = [forward(own_msg, s) for s in shifts]
    state = shape((2, queries, 128), f32)
    cache_parts = call(
        functools.partial(cache_kernel, rows, steps),
        (cache_len, own_msg, other_msg, cache_keys, cache_values, new_keys, new_values),
        [state] * 3,
        [pltpu.VMEM((128, 2 * D_HEAD), f32)] * 2,
    )
    messages = [own_msg] + other_msgs + own_msgs
    part = shape((queries + 8, 128), f32)
    parts = call(
        functools.partial(jobs_kernel, span, len(messages)),
        (prompt_len, *messages, prefill_keys, prefill_values, near_keys, near_values),
        [part] * len(messages),
    )
    other_parts = [across(p, -s) for s, p in enumerate(parts[1 : 1 + pairs])]
    own_parts = [parts[0]] + [back(p, s) for s, p in zip(shifts, parts[1 + pairs :])]
    run = shape((prompts, length, columns), f32)
    summed, top, total = call(
        local_kernel,
        (prefill_queries, prefill_keys, prefill_values, near_keys, near_values),
        [run] * 3,
        [pltpu.VMEM((prompts, 2 * length, 2 * D_HEAD), bf16)],
        scalars=0,
    )
    lates = []
    for index, shift in enumerate(shifts):
        last = shift == pairs - 1
        k_one, v_one = far_keys[index], far_values[index]
        k_two, v_two = near(k_one), near(v_one)
        weights, summed, top, total = call(
            functools.partial(far_scores_kernel, shift),
            (prefill_queries, k_one, k_two, summed, top, total),
            [shape((prompts, group, length, 2 * length), bf16)] + [run] * 3,
            scalars=0,
            aliases={3: 1, 4: 2, 5: 3},
        )
        args = (prompt_len, weights, k_one, v_one, k_two, v_two, summed, total, own_msg)
        ones = [pltpu.VMEM((prompts, length, 2 * D_HEAD), bf16)] * 2
        if last:
            prefill_out, decode_out, _ = call(
                functools.partial(far_values_kernel, shift, True, span, len(other_parts), len(own_parts)),
                (*args, *cache_parts, *own_parts, *other_parts, *lates),
                [shape(prefill_queries.shape, bf16), shape(decode_queries.shape, bf16), part],
                [pltpu.VMEM((span, dec_columns), f32)] + ones,
            )
        else:
            summed, total, late = call(
                functools.partial(far_values_kernel, shift, False, span, 0, 0),
                args,
                [run, run, part],
                ones,
                aliases={6: 0, 7: 1},
            )
            lates.append(late)
    return (prefill_out, decode_out)


def solution(mesh):
    in_specs = (
        P(None, "seq", ("head", "role")),
        P(None, "seq", ("head", "role")),
        P(None, "seq", ("head", "role")),
        P(),
        P(("seq", "role")),
        P(("seq", "role")),
        P(("seq", "role"), None, "head"),
        P(("seq", "role"), None, "head"),
        P(None, ("seq", "role"), "head"),
        P(None, ("seq", "role"), "head"),
        P(None, ("seq", "role"), "head"),
    )
    out_specs = (P(None, "seq", ("head", "role")), P(None, ("seq", "role"), "head"))
    return jax.shard_map(body, mesh=mesh, in_specs=in_specs, out_specs=out_specs, check_vma=False)
```

```python
import functools
import math

import jax
import jax.numpy as jnp
from jax import lax
from jax.experimental import pallas as pl
from jax.experimental.pallas import tpu as pltpu
from jax.sharding import PartitionSpec as P

D_HEAD = 128
MASKED_SCORE = -1e30
EXP2_SCALE = D_HEAD**-0.5 * math.log2(math.e)
VMEM_BYTES = 40 * 2**20
NT = (((1,), (1,)), ((), ()))


def scores_of(queries, keys):
    return lax.dot_general(queries, keys, NT, preferred_element_type=jnp.float32)


def weighted(weights, values):
    return jnp.dot(weights.astype(jnp.bfloat16), values, preferred_element_type=jnp.float32)


def eye_of(rows):
    shape = (rows, 128)
    return lax.broadcasted_iota(jnp.int32, shape, 0) == lax.broadcasted_iota(jnp.int32, shape, 1)


def column_to_row(column):
    spread = jnp.where(eye_of(column.shape[0]), column, 0.0)
    return jnp.sum(spread, axis=0, keepdims=True)


def row_to_column(row, rows):
    spread = jnp.where(eye_of(rows), jnp.broadcast_to(row, (rows, 128)), 0.0)
    return jnp.sum(spread, axis=1, keepdims=True)


def select_rows(index, parts):
    chosen = parts[-1]
    for number in range(len(parts) - 2, -1, -1):
        chosen = jnp.where(index == number, parts[number], chosen)
    return chosen


def lane_sum(x):
    tiles = [x[:, i : i + 128] for i in range(0, x.shape[1], 128)]
    return jnp.sum(functools.reduce(jnp.add, tiles), axis=1, keepdims=True)


def lane_max(x):
    tiles = [x[:, i : i + 128] for i in range(0, x.shape[1], 128)]
    return jnp.max(functools.reduce(jnp.maximum, tiles), axis=1, keepdims=True)


def pack_kernel(
    dq_hbm, asg_hbm, plen_hbm, clen_hbm, nk_hbm, nv_hbm, own_ref, other_ref, info_ref, nk_ref, nv_ref, dq, nk, nv, asg, plen, clen, flat, sems
):
    moves = [(dq_hbm, dq), (asg_hbm, asg), (plen_hbm, plen), (clen_hbm, clen), (nk_hbm, nk), (nv_hbm, nv)]
    copies = [pltpu.make_async_copy(a, b, sems.at[i]) for i, (a, b) in enumerate(moves)]
    for copy in copies:
        copy.start()
    steps, rows, columns = dq.shape
    span = steps * rows
    role = lax.axis_index("role")
    half = columns // 2
    group = half // D_HEAD
    row_index = lax.broadcasted_iota(jnp.int32, (span, 128), 0)
    nk_ref[...] = jnp.zeros_like(nk_ref)
    nv_ref[...] = jnp.zeros_like(nv_ref)
    for copy in copies:
        copy.wait()
    for step in range(steps):
        flat[step * rows : (step + 1) * rows, :] = dq[step].astype(jnp.float32)
        nk_ref[step * rows : (step + 1) * rows, :] = nk[step].astype(jnp.float32)
        nv_ref[step * rows : (step + 1) * rows, :] = nv[step].astype(jnp.float32)
    prompt = jnp.zeros((span, 128), jnp.float32)
    for row in range(rows):
        prompt = jnp.where(row_index % rows == row, asg[row].astype(jnp.float32), prompt)
    info = jnp.zeros((span, 128), jnp.int32)
    for row in range(plen.shape[0]):
        info = jnp.where(row_index == row, plen[row], info)
    for row in range(rows):
        info = jnp.where(row_index == 4 + row, clen[row], info)
    info_ref[...] = info
    for out, kv in ((own_ref, role), (other_ref, 1 - role)):
        for pair in range(group // 2):
            two = [
                flat[:, pl.ds(pl.multiple_of(kv * half + (2 * pair + i) * D_HEAD, D_HEAD), D_HEAD)] for i in (0, 1)
            ]
            out[2 * span * pair : 2 * span * (pair + 1), :] = jnp.concatenate(two, axis=0).astype(jnp.bfloat16)
        out[span * group : span * (group + 2), :] = jnp.concatenate([prompt, prompt], axis=0).astype(jnp.bfloat16)


def cache_kernel(rows, steps, info_ref, own_ref, other_ref, ck_ref, cv_ref, nk_ref, nv_ref, sum_ref, top_ref, tot_ref):
    span = steps * rows
    queries = own_ref.shape[0] - 2 * span
    role = lax.axis_index("role")
    slots = ck_ref.shape[1]
    q_index = lax.broadcasted_iota(jnp.int32, (queries, 1), 0) % span
    q_step, q_row = q_index // rows, q_index % rows
    lane = lax.broadcasted_iota(jnp.int32, (queries, 128), 1)
    fresh_mask = (lane < span) & (lane % rows == q_row) & (lane // rows <= q_step)
    limit = select_rows(q_row, [jnp.broadcast_to(info_ref[4 + r : 5 + r, :1], (queries, 1)) for r in range(rows)])
    live = lax.broadcasted_iota(jnp.int32, (queries, slots), 1) < limit
    for index, (message, kv) in enumerate(((own_ref, role), (other_ref, 1 - role))):
        q = message[:queries, :]
        columns = pl.ds(pl.multiple_of(kv * D_HEAD, D_HEAD), D_HEAD)
        fresh = scores_of(q, nk_ref[:, columns].astype(jnp.bfloat16))
        fresh = jnp.where(fresh_mask, fresh * EXP2_SCALE, MASKED_SCORE)
        old = select_rows(q_row, [scores_of(q, ck_ref[r, :, columns]) for r in range(rows)])
        old = jnp.where(live, old * EXP2_SCALE, MASKED_SCORE)
        top = jnp.maximum(lane_max(fresh), lane_max(old))
        fresh = jnp.exp2(fresh - top)
        old = jnp.exp2(old - top)
        total = lane_sum(fresh) + lane_sum(old)
        summed = weighted(fresh, nv_ref[:, columns].astype(jnp.bfloat16))
        for r in range(rows):
            summed = summed + weighted(jnp.where(q_row == r, old, 0.0), cv_ref[r, :, columns])
        sum_ref[index] = summed
        top_ref[index] = jnp.broadcast_to(top, (queries, 128))
        tot_ref[index] = jnp.broadcast_to(total, (queries, 128))


def jobs_kernel(span, count, *refs):
    messages = refs[:count]
    info_ref, k_own, v_own, k_near, v_near, _ = refs[count : count + 6]
    outs = refs[count + 6 : -1]
    wide = refs[-1]
    queries = messages[0].shape[0] - 2 * span
    seq = lax.axis_index("seq")
    prompts, length, _ = k_own.shape
    wide[:, :length, :D_HEAD] = v_own[...]
    wide[:, length:, :D_HEAD] = v_near[...]
    wide[:, :, D_HEAD:] = jnp.ones((prompts, 2 * length, D_HEAD), jnp.bfloat16)
    q = jnp.concatenate([m[:queries, :] for m in messages], axis=0)
    columns = []
    for m in messages:
        eight = m[queries : queries + 2 * span, :].astype(jnp.float32)[:span, :1]
        columns += [eight] * (queries // span)
    prompt = jnp.concatenate(columns, axis=0).astype(jnp.int32)
    limit = select_rows(prompt, [jnp.broadcast_to(info_ref[r : r + 1, :1], prompt.shape) for r in range(prompts)])
    parts = []
    for first, keys in ((seq * length, k_own), ((seq + 1 - 2 * (seq % 2)) * length, k_near)):
        position = first + lax.broadcasted_iota(jnp.int32, (q.shape[0], length), 1)
        part = select_rows(prompt, [scores_of(q, keys[r]) for r in range(prompts)])
        parts.append(jnp.where(position < limit, part * EXP2_SCALE, MASKED_SCORE))
    scores = jnp.concatenate(parts, axis=1)
    top = lane_max(scores)
    weights = jnp.exp2(scores - jnp.maximum(top, 0.5 * MASKED_SCORE))
    summed = jnp.zeros((q.shape[0], 2 * D_HEAD), jnp.float32)
    for r in range(prompts):
        summed = summed + weighted(jnp.where(prompt == r, weights, 0.0), wide[r])
    for index, out in enumerate(outs):
        rows = slice(index * queries, (index + 1) * queries)
        out[:queries, :] = summed[rows, :D_HEAD]
        out[queries : queries + 8, :] = jnp.concatenate(
            [column_to_row(top[rows]), column_to_row(summed[rows, D_HEAD:]), jnp.zeros((6, 128), jnp.float32)], axis=0
        )


def local_kernel(q_ref, k_own, k_near, wide, _, sum_ref, top_ref, tot_ref):
    prompts, length, columns = q_ref.shape
    group = columns // D_HEAD
    seq = lax.axis_index("seq")
    causal = lax.broadcasted_iota(jnp.int32, (length, length), 1) <= lax.broadcasted_iota(
        jnp.int32, (length, length), 0
    )

    def run(with_near):
        for row in range(prompts):
            for head in range(group):
                cols = slice(head * D_HEAD, (head + 1) * D_HEAD)
                q = q_ref[row, :, cols]
                scores = jnp.where(causal, scores_of(q, k_own[row]), MASKED_SCORE)
                if with_near:
                    scores = jnp.concatenate([scores, scores_of(q, k_near[row])], axis=1)
                top = jnp.max(scores, axis=1, keepdims=True) * EXP2_SCALE
                weights = jnp.exp2(scores * EXP2_SCALE - top)
                summed = weighted(weights, wide[row, : scores.shape[1], :])
                sum_ref[row, :, cols] = summed[:, :D_HEAD]
                tot_ref[row, :, cols] = summed[:, D_HEAD:]
                top_ref[row, :, cols] = jnp.broadcast_to(top, (length, D_HEAD))

    @pl.when(seq % 2 == 0)
    def _():
        run(False)

    @pl.when(seq % 2 == 1)
    def _():
        run(True)


def merge_kernel(span, n_own, n_other, group, *refs):
    cache_sum, cache_top, cache_tot = refs[:3]
    own_parts = refs[3 : 3 + n_own]
    other_parts = refs[3 + n_own : 3 + n_own + n_other]
    dec_ref, flat = refs[-2:]
    role = lax.axis_index("role")
    queries = group * span
    half = group * D_HEAD
    for index, (parts, kv) in enumerate(((own_parts, role), (other_parts, 1 - role))):
        sums, tops, tots = [cache_sum[index]], [cache_top[index][:, :1]], [cache_tot[index][:, :1]]
        for part in parts:
            sums.append(part[:queries, :])
            tops.append(row_to_column(part[queries : queries + 1, :], queries))
            tots.append(row_to_column(part[queries + 1 : queries + 2, :], queries))
        high = functools.reduce(jnp.maximum, tops)
        factors = [jnp.exp2(top - high) for top in tops]
        summed = functools.reduce(jnp.add, [f * s for f, s in zip(factors, sums)])
        total = functools.reduce(jnp.add, [f * t for f, t in zip(factors, tots)])
        result = summed / total
        for head in range(group):
            start = pl.multiple_of(kv * half + head * D_HEAD, D_HEAD)
            flat[:, pl.ds(start, D_HEAD)] = result[head * span : (head + 1) * span]
    steps, rows, _ = dec_ref.shape
    for step in range(steps):
        dec_ref[step] = flat[step * rows : (step + 1) * rows, :].astype(jnp.bfloat16)


def far_kernel(shift, last, info_ref, q_ref, k_one, v_one, k_two, v_two, sum_in, top_in, tot_in, _, *refs):
    prompts, length, columns = q_ref.shape
    group = columns // D_HEAD
    seq = lax.axis_index("seq")
    if last:
        out_hbm, out, wide, sems = refs
    else:
        sum_ref, top_ref, tot_ref, wide = refs

    def finish(row, cols, summed, top, total):
        if last:
            position = seq * length + lax.broadcasted_iota(jnp.int32, (length, D_HEAD), 0)
            live = position < info_ref[row : row + 1, :]
            out[row, :, cols] = jnp.where(live, summed / total, 0.0).astype(jnp.bfloat16)
        else:
            sum_ref[row, :, cols] = summed
            top_ref[row, :, cols] = top
            tot_ref[row, :, cols] = total

    def moves(row, part):
        wide_cols = slice(part * columns // 2, (part + 1) * columns // 2)
        return pltpu.make_async_copy(
            out.at[row, :, wide_cols], out_hbm.at[row, :, wide_cols], sems.at[row * 2 + part]
        )

    def run(with_far):
        for row in range(prompts):
            for head in range(group):
                cols = slice(head * D_HEAD, (head + 1) * D_HEAD)
                summed, total = sum_in[row, :, cols], tot_in[row, :, cols]
                top = top_in[row, :, cols]
                if with_far:
                    q = q_ref[row, :, cols]
                    scores = jnp.concatenate([scores_of(q, k_one[row]), scores_of(q, k_two[row])], axis=1)
                    new = jnp.maximum(top, jnp.max(scores, axis=1, keepdims=True) * EXP2_SCALE)
                    high = jnp.concatenate([new] * (2 * length // D_HEAD), axis=1)
                    far = weighted(jnp.exp2(scores * EXP2_SCALE - high), wide[row])
                    alpha = jnp.exp2(top - new)
                    summed = summed * alpha + far[:, :D_HEAD]
                    total = total * alpha + far[:, D_HEAD:]
                    top = new
                finish(row, cols, summed, top, total)
                if last and (head + 1) % (group // 2) == 0:
                    moves(row, (head + 1) // (group // 2) - 1).start()

    @pl.when(seq // 2 >= shift)
    def _():
        wide[:, :length, :D_HEAD] = v_one[...]
        wide[:, length:, :D_HEAD] = v_two[...]
        wide[:, :, D_HEAD:] = jnp.ones((prompts, 2 * length, D_HEAD), jnp.bfloat16)
        run(True)

    @pl.when(seq // 2 < shift)
    def _():
        run(False)

    if last:
        for row in range(prompts):
            for part in range(2):
                moves(row, part).wait()


VMEM = pl.BlockSpec(memory_space=pltpu.VMEM)
ANY = pl.BlockSpec(memory_space=pl.ANY)


def in_hbm(x):
    return pltpu.with_memory_space_constraint(x, pltpu.HBM)


def call(kernel, args, outs, scratch=(), specs=None, out_specs=None, us=1.0):
    return pl.pallas_call(
        kernel,
        out_shape=outs,
        in_specs=specs or [VMEM] * len(args),
        out_specs=out_specs or [VMEM] * len(outs),
        scratch_shapes=list(scratch),
        compiler_params=pltpu.CompilerParams(vmem_limit_bytes=VMEM_BYTES),
        cost_estimate=pl.CostEstimate(flops=int(us * 1.1e9), bytes_accessed=int(us * 3e6), transcendentals=0),
    )(*args)


def body(
    prefill_queries,
    prefill_keys,
    prefill_values,
    prompt_len,
    assignment,
    cache_len,
    cache_keys,
    cache_values,
    decode_queries,
    new_keys,
    new_values,
):
    seqs, roles = lax.axis_size("seq"), lax.axis_size("role")
    pairs = seqs // 2
    prompts, length, columns = prefill_queries.shape
    steps, rows, dec_columns = decode_queries.shape
    group = columns // D_HEAD
    span = steps * rows
    queries = group * span
    f32, bf16, i32 = jnp.float32, jnp.bfloat16, jnp.int32
    shape = jax.ShapeDtypeStruct

    def near(x):
        return lax.ppermute(x, "seq", [(i, i ^ 1) for i in range(seqs)])

    def forward(x, shift):
        return lax.ppermute(x, "seq", [(i, i + 2 * shift) for i in range(seqs - 2 * shift)])

    def around(x, shift, flip):
        moves = [
            (i * roles + r, (i + 2 * shift) % seqs * roles + (1 - r if flip else r))
            for i in range(seqs)
            for r in range(roles)
        ]
        return lax.ppermute(x, ("seq", "role"), moves)

    shifts = range(1, pairs)
    far_keys = [forward(prefill_keys, s) for s in shifts]
    far_values = [forward(prefill_values, s) for s in shifts]
    near_keys, near_values = near(prefill_keys), near(prefill_values)
    message = shape((queries + 2 * span, 128), bf16)
    small = [decode_queries, assignment, prompt_len, cache_len, new_keys, new_values]
    own_msg, other_msg, info, fresh_keys, fresh_values = call(
        pack_kernel,
        [in_hbm(x) for x in small],
        [message] * 2 + [shape((span, 128), i32)] + [shape((128, 2 * D_HEAD), f32)] * 2,
        [
            pltpu.VMEM(decode_queries.shape, bf16),
            pltpu.VMEM(new_keys.shape, bf16),
            pltpu.VMEM(new_values.shape, bf16),
            pltpu.SMEM(assignment.shape, i32),
            pltpu.SMEM(prompt_len.shape, i32),
            pltpu.SMEM(cache_len.shape, i32),
            pltpu.VMEM((span, dec_columns), f32),
            pltpu.SemaphoreType.DMA((6,)),
        ],
        specs=[ANY] * 6,
        us=1.0,
    )
    other_msgs = [around(other_msg, s, True) for s in range(pairs)]
    own_msgs = [own_msg] + [around(own_msg, s, False) for s in shifts]
    state = shape((2, queries, 128), f32)
    cache_parts = call(
        functools.partial(cache_kernel, rows, steps),
        (info, own_msg, other_msg, cache_keys, cache_values, fresh_keys, fresh_values),
        [state] * 3,
        us=1.2,
    )
    messages = own_msgs + other_msgs
    part = shape((queries + 8, 128), f32)
    *parts, wide = call(
        functools.partial(jobs_kernel, span, len(messages)),
        (*messages, info, prefill_keys, prefill_values, near_keys, near_values, cache_parts[0]),
        [part] * len(messages) + [shape((prompts, 2 * length, 2 * D_HEAD), bf16)],
        specs=[VMEM] * (len(messages) + 5) + [ANY],
        us=0.8,
    )
    own_parts = [parts[0]] + [around(parts[s], -s, False) for s in shifts]
    other_parts = [around(parts[pairs + s], -s, True) for s in range(pairs)]
    run = shape((prompts, length, columns), f32)
    summed, top, total = call(
        local_kernel,
        (prefill_queries, prefill_keys, near_keys, wide, parts[0]),
        [run] * 3,
        specs=[VMEM] * 4 + [ANY],
        us=2.5,
    )
    (decode_out,) = call(
        functools.partial(merge_kernel, span, len(own_parts), len(other_parts), group),
        (*cache_parts, *own_parts, *other_parts, total),
        [shape(decode_queries.shape, bf16)],
        [pltpu.VMEM((span, dec_columns), f32)],
        specs=[VMEM] * (3 + 2 * pairs) + [ANY],
        us=0.6,
    )
    for index, shift in enumerate(shifts):
        last = shift == pairs - 1
        k_one, v_one = far_keys[index], far_values[index]
        k_two, v_two = near(k_one), near(v_one)
        args = (info, prefill_queries, k_one, v_one, k_two, v_two, summed, top, total, decode_out)
        wide_scratch = pltpu.VMEM((prompts, 2 * length, 2 * D_HEAD), bf16)
        kernel = functools.partial(far_kernel, shift, last)
        specs = [VMEM] * (len(args) - 1) + [ANY]
        if last:
            (prefill_out,) = call(
                kernel,
                args,
                [shape(prefill_queries.shape, bf16)],
                [pltpu.VMEM(prefill_queries.shape, bf16), wide_scratch, pltpu.SemaphoreType.DMA((2 * prompts,))],
                specs=specs,
                out_specs=[ANY],
                us=3.0,
            )
        else:
            summed, top, total = call(kernel, args, [run] * 3, [wide_scratch], specs=specs, us=3.0)
    return (prefill_out, decode_out)


def solution(mesh):
    in_specs = (
        P(None, "seq", ("head", "role")),
        P(None, "seq", ("head", "role")),
        P(None, "seq", ("head", "role")),
        P(),
        P(("seq", "role")),
        P(("seq", "role")),
        P(("seq", "role"), None, "head"),
        P(("seq", "role"), None, "head"),
        P(None, ("seq", "role"), "head"),
        P(None, ("seq", "role"), "head"),
        P(None, ("seq", "role"), "head"),
    )
    out_specs = (P(None, "seq", ("head", "role")), P(None, ("seq", "role"), "head"))
    return jax.shard_map(body, mesh=mesh, in_specs=in_specs, out_specs=out_specs, check_vma=False)
```

```python
import functools
import math

import jax
import jax.numpy as jnp
from jax import lax
from jax.experimental import pallas as pl
from jax.experimental.pallas import tpu as pltpu
from jax.sharding import PartitionSpec as P

D_HEAD = 128
MASKED_SCORE = -1e30
EXP2_SCALE = D_HEAD**-0.5 * math.log2(math.e)
VMEM_BYTES = 40 * 2**20
NT = (((1,), (1,)), ((), ()))


def scores_of(queries, keys):
    return lax.dot_general(queries, keys, NT, preferred_element_type=jnp.float32)


def weighted(weights, values):
    return jnp.dot(weights.astype(jnp.bfloat16), values, preferred_element_type=jnp.float32)


def eye_of(rows):
    shape = (rows, 128)
    return lax.broadcasted_iota(jnp.int32, shape, 0) == lax.broadcasted_iota(jnp.int32, shape, 1)


def column_to_row(column):
    spread = jnp.where(eye_of(column.shape[0]), column, 0.0)
    return jnp.sum(spread, axis=0, keepdims=True)


def row_to_column(row, rows):
    spread = jnp.where(eye_of(rows), jnp.broadcast_to(row, (rows, 128)), 0.0)
    return jnp.sum(spread, axis=1, keepdims=True)


def select_rows(index, parts):
    chosen = parts[-1]
    for number in range(len(parts) - 2, -1, -1):
        chosen = jnp.where(index == number, parts[number], chosen)
    return chosen


def lane_sum(x):
    tiles = [x[:, i : i + 128] for i in range(0, x.shape[1], 128)]
    return jnp.sum(functools.reduce(jnp.add, tiles), axis=1, keepdims=True)


def lane_max(x):
    tiles = [x[:, i : i + 128] for i in range(0, x.shape[1], 128)]
    return jnp.max(functools.reduce(jnp.maximum, tiles), axis=1, keepdims=True)


def own_kernel(
    dq_hbm, asg_hbm, plen_hbm, clen_hbm, nk_hbm, nv_hbm, ck_hbm, cv_hbm,
    own_ref, other_ref, info_ref, sum_ref, top_ref, tot_ref,
    dq, nk, nv, asg, plen, clen, flat, fk, fv, ck_ref, cv_ref, sems,
):
    moves = [(dq_hbm, dq), (nk_hbm, nk), (nv_hbm, nv), (asg_hbm, asg), (plen_hbm, plen), (clen_hbm, clen)]
    role = lax.axis_index("role")
    for kv in (role, 1 - role):
        cols = pl.ds(pl.multiple_of(kv * D_HEAD, D_HEAD), D_HEAD)
        moves += [(ck_hbm.at[:, :, cols], ck_ref.at[:, :, cols]), (cv_hbm.at[:, :, cols], cv_ref.at[:, :, cols])]
    copies = [pltpu.make_async_copy(a, b, sems.at[i]) for i, (a, b) in enumerate(moves)]
    for copy in copies:
        copy.start()
    steps, rows, columns = dq.shape
    span = steps * rows
    half = columns // 2
    group = half // D_HEAD
    queries = group * span
    slots = ck_ref.shape[1]
    fk[...] = jnp.zeros_like(fk)
    fv[...] = jnp.zeros_like(fv)
    for copy in copies[:6]:
        copy.wait()
    for step in range(steps):
        at = slice(step * rows, (step + 1) * rows)
        flat[at, :] = dq[step].astype(jnp.float32)
        fk[at, :] = nk[step].astype(jnp.float32)
        fv[at, :] = nv[step].astype(jnp.float32)
    row_index = lax.broadcasted_iota(jnp.int32, (span, 128), 0)
    prompt = jnp.zeros((span, 128), jnp.float32)
    for row in range(rows):
        prompt = jnp.where(row_index % rows == row, asg[row].astype(jnp.float32), prompt)
    info = jnp.zeros((span, 128), jnp.int32)
    for row in range(plen.shape[0]):
        info = jnp.where(row_index == row, plen[row], info)
    info_ref[...] = info

    q_index = lax.broadcasted_iota(jnp.int32, (queries, 1), 0) % span
    q_step, q_row = q_index // rows, q_index % rows
    lane = lax.broadcasted_iota(jnp.int32, (queries, 128), 1)
    fresh_mask = (lane < span) & (lane % rows == q_row) & (lane // rows <= q_step)
    limit = select_rows(q_row, [clen[r] for r in range(rows)])
    live = lax.broadcasted_iota(jnp.int32, (queries, slots), 1) < limit
    for index, (out, kv) in enumerate(((own_ref, role), (other_ref, 1 - role))):
        heads = [flat[:, pl.ds(pl.multiple_of(kv * half + i * D_HEAD, D_HEAD), D_HEAD)] for i in range(group)]
        q = jnp.concatenate(heads, axis=0).astype(jnp.bfloat16)
        out[:queries, :] = q
        out[queries : queries + 2 * span, :] = jnp.concatenate([prompt, prompt], axis=0).astype(jnp.bfloat16)
        cols = pl.ds(pl.multiple_of(kv * D_HEAD, D_HEAD), D_HEAD)
        fresh = scores_of(q, fk[:, cols].astype(jnp.bfloat16))
        fresh = jnp.where(fresh_mask, fresh * EXP2_SCALE, MASKED_SCORE)
        copies[6 + 2 * index].wait()
        old = select_rows(q_row, [scores_of(q, ck_ref[r, :, cols]) for r in range(rows)])
        old = jnp.where(live, old * EXP2_SCALE, MASKED_SCORE)
        top = jnp.maximum(lane_max(fresh), lane_max(old))
        fresh = jnp.exp2(fresh - top)
        old = jnp.exp2(old - top)
        total = lane_sum(fresh) + lane_sum(old)
        summed = weighted(fresh, fv[:, cols].astype(jnp.bfloat16))
        copies[7 + 2 * index].wait()
        for r in range(rows):
            summed = summed + weighted(jnp.where(q_row == r, old, 0.0), cv_ref[r, :, cols])
        sum_ref[index] = summed
        top_ref[index] = jnp.broadcast_to(top, (queries, 128))
        tot_ref[index] = jnp.broadcast_to(total, (queries, 128))


def prompt_kernel(span, *refs):
    messages, info_ref = refs[:2], refs[2]
    chunk_refs, outs = refs[3:-3], refs[-2:]
    queries = messages[0].shape[0] - 2 * span
    seqs, seq = lax.axis_size("seq"), lax.axis_index("seq")
    prompts, length, _ = chunk_refs[0].shape
    q = jnp.concatenate([m[:queries, :] for m in messages], axis=0)
    columns = []
    for m in messages:
        eight = m[queries : queries + 2 * span, :].astype(jnp.float32)[:span, :1]
        columns += [eight] * (queries // span)
    prompt = jnp.concatenate(columns, axis=0).astype(jnp.int32)
    limit = select_rows(prompt, [jnp.broadcast_to(info_ref[r : r + 1, :1], prompt.shape) for r in range(prompts)])
    parts = []
    for index in range(seqs):
        base = (seq + seqs - 2 * (index // 2)) % seqs
        chunk = base + (index % 2) * (1 - 2 * (seq % 2))
        keys = chunk_refs[2 * index]
        position = chunk * length + lax.broadcasted_iota(jnp.int32, (q.shape[0], length), 1)
        part = select_rows(prompt, [scores_of(q, keys[r]) for r in range(prompts)])
        parts.append(jnp.where(position < limit, part * EXP2_SCALE, MASKED_SCORE))
    top = lane_max(jnp.concatenate(parts, axis=1))
    summed = jnp.zeros((q.shape[0], D_HEAD), jnp.float32)
    total = jnp.zeros((q.shape[0], 1), jnp.float32)
    for index, part in enumerate(parts):
        weights = jnp.exp2(part - top)
        total = total + lane_sum(weights)
        for r in range(prompts):
            summed = summed + weighted(jnp.where(prompt == r, weights, 0.0), chunk_refs[2 * index + 1][r])
    for index, out in enumerate(outs):
        rows = slice(index * queries, (index + 1) * queries)
        out[:queries, :] = summed[rows]
        out[queries : queries + 8, :] = jnp.concatenate(
            [column_to_row(top[rows]), column_to_row(total[rows]), jnp.zeros((6, 128), jnp.float32)], axis=0
        )


def local_kernel(row, q_ref, k_own, v_own, k_near, v_near, _, sum_ref, top_ref, tot_ref, wide):
    _, length, columns = q_ref.shape
    group = columns // D_HEAD
    seq = lax.axis_index("seq")
    wide[:length, :D_HEAD] = v_own[row]
    wide[length:, :D_HEAD] = v_near[row]
    wide[:, D_HEAD:] = jnp.ones((2 * length, D_HEAD), jnp.bfloat16)
    causal = lax.broadcasted_iota(jnp.int32, (length, length), 1) <= lax.broadcasted_iota(
        jnp.int32, (length, length), 0
    )

    def run(with_near):
        for head in range(group):
            cols = slice(head * D_HEAD, (head + 1) * D_HEAD)
            q = q_ref[row, :, cols]
            scores = jnp.where(causal, scores_of(q, k_own[row]), MASKED_SCORE)
            if with_near:
                scores = jnp.concatenate([scores, scores_of(q, k_near[row])], axis=1)
            top = jnp.max(scores, axis=1, keepdims=True) * EXP2_SCALE
            summed = weighted(jnp.exp2(scores * EXP2_SCALE - top), wide[: scores.shape[1], :])
            sum_ref[:, cols] = summed[:, :D_HEAD]
            tot_ref[:, cols] = summed[:, D_HEAD:]
            top_ref[:, cols] = jnp.broadcast_to(top, (length, D_HEAD))

    @pl.when(seq % 2 == 0)
    def _():
        run(False)

    @pl.when(seq % 2 == 1)
    def _():
        run(True)


def merge_rows(span, cache, own_part, other_part, dec, flat):
    steps, rows, columns = dec.shape
    half = columns // 2
    group = half // D_HEAD
    queries = group * span
    role = lax.axis_index("role")
    for index, (part, kv) in enumerate(((own_part, role), (other_part, 1 - role))):
        top = row_to_column(part[queries : queries + 1, :], queries)
        total = row_to_column(part[queries + 1 : queries + 2, :], queries)
        cache_sum, cache_top, cache_tot = (ref[index] for ref in cache)
        high = jnp.maximum(top, cache_top)
        one, two = jnp.exp2(cache_top - high), jnp.exp2(top - high)
        result = (one * cache_sum + two * part[:queries, :]) / (one * cache_tot + two * total)
        for head in range(group):
            start = pl.multiple_of(kv * half + head * D_HEAD, D_HEAD)
            flat[:, pl.ds(start, D_HEAD)] = result[head * span : (head + 1) * span]
    for step in range(steps):
        dec[step] = flat[step * rows : (step + 1) * rows, :].astype(jnp.bfloat16)


def far_kernel(shift, row, last, final, span, info_ref, q_ref, k_one, v_one, k_two, v_two, sum_in, top_in, tot_in, *refs):
    _, length, columns = q_ref.shape
    group = columns // D_HEAD
    seq = lax.axis_index("seq")
    if final:
        _, *cache, own_part, other_part, out_hbm, dec_hbm, wide, out, sems, dec, flat = refs
        merge_rows(span, cache, own_part, other_part, dec, flat)
        dec_copy = pltpu.make_async_copy(dec, dec_hbm, sems.at[group])
        dec_copy.start()
    elif last:
        out_hbm, wide, out, sems = refs[-4:]
    else:
        sum_ref, top_ref, tot_ref, wide = refs[-4:]

    def move(head):
        cols = slice(head * D_HEAD, (head + 1) * D_HEAD)
        return pltpu.make_async_copy(out.at[:, cols], out_hbm.at[row, :, cols], sems.at[head])

    def run(with_far):
        position = seq * length + lax.broadcasted_iota(jnp.int32, (length, D_HEAD), 0)
        live = position < info_ref[row : row + 1, :]
        for head in range(group):
            cols = slice(head * D_HEAD, (head + 1) * D_HEAD)
            summed, total, top = sum_in[:, cols], tot_in[:, cols], top_in[:, cols]
            if with_far:
                q = q_ref[row, :, cols]
                scores = jnp.concatenate([scores_of(q, k_one[row]), scores_of(q, k_two[row])], axis=1)
                new = jnp.maximum(top, jnp.max(scores, axis=1, keepdims=True) * EXP2_SCALE)
                high = jnp.concatenate([new] * (2 * length // D_HEAD), axis=1)
                far = weighted(jnp.exp2(scores * EXP2_SCALE - high), wide[...])
                alpha = jnp.exp2(top - new)
                summed = summed * alpha + far[:, :D_HEAD]
                total = total * alpha + far[:, D_HEAD:]
                top = new
            if last:
                out[:, cols] = jnp.where(live, summed / total, 0.0).astype(jnp.bfloat16)
                move(head).start()
            else:
                sum_ref[:, cols], top_ref[:, cols], tot_ref[:, cols] = summed, top, total

    @pl.when(seq // 2 >= shift)
    def _():
        wide[:length, :D_HEAD] = v_one[row]
        wide[length:, :D_HEAD] = v_two[row]
        wide[:, D_HEAD:] = jnp.ones((2 * length, D_HEAD), jnp.bfloat16)
        run(True)

    @pl.when(seq // 2 < shift)
    def _():
        run(False)

    if last:
        for head in range(group):
            move(head).wait()
    if final:
        dec_copy.wait()


VMEM = pl.BlockSpec(memory_space=pltpu.VMEM)
ANY = pl.BlockSpec(memory_space=pl.ANY)


def in_hbm(x):
    return pltpu.with_memory_space_constraint(x, pltpu.HBM)


def call(kernel, args, outs, scratch=(), specs=None, out_specs=None, aliases=None, us=1.0):
    return pl.pallas_call(
        kernel,
        out_shape=outs,
        in_specs=specs or [VMEM] * len(args),
        out_specs=out_specs or [VMEM] * len(outs),
        scratch_shapes=list(scratch),
        input_output_aliases=aliases or {},
        compiler_params=pltpu.CompilerParams(vmem_limit_bytes=VMEM_BYTES),
        cost_estimate=pl.CostEstimate(flops=int(us * 1.1e9), bytes_accessed=int(us * 3e6), transcendentals=0),
    )(*args)


def body(
    prefill_queries,
    prefill_keys,
    prefill_values,
    prompt_len,
    assignment,
    cache_len,
    cache_keys,
    cache_values,
    decode_queries,
    new_keys,
    new_values,
):
    seqs = lax.axis_size("seq")
    prompts, length, columns = prefill_queries.shape
    steps, rows, dec_columns = decode_queries.shape
    group = columns // D_HEAD
    span = steps * rows
    queries = group * span
    f32, bf16, i32 = jnp.float32, jnp.bfloat16, jnp.int32
    shape = jax.ShapeDtypeStruct
    after = lax.optimization_barrier

    def near(x):
        return lax.ppermute(x, "seq", [(i, i ^ 1) for i in range(seqs)])

    def around(x, shift):
        return lax.ppermute(x, "seq", [(i, (i + 2 * shift) % seqs) for i in range(seqs)])

    def partner(x):
        return lax.ppermute(x, "role", [(0, 1), (1, 0)])

    shifts = range(1, seqs // 2)
    far_keys = [around(prefill_keys, s) for s in shifts]
    far_values = [around(prefill_values, s) for s in shifts]
    near_keys, near_values = near(prefill_keys), near(prefill_values)
    message = shape((queries + 2 * span, 128), bf16)
    state = shape((2, queries, 128), f32)
    small = [decode_queries, assignment, prompt_len, cache_len, new_keys, new_values]
    own_msg, other_msg, info, *cache = call(
        own_kernel,
        [in_hbm(x) for x in small + [cache_keys, cache_values]],
        [message] * 2 + [shape((span, 128), i32)] + [state] * 3,
        [
            pltpu.VMEM(decode_queries.shape, bf16),
            pltpu.VMEM(new_keys.shape, bf16),
            pltpu.VMEM(new_values.shape, bf16),
            pltpu.SMEM(assignment.shape, i32),
            pltpu.SMEM(prompt_len.shape, i32),
            pltpu.SMEM(cache_len.shape, i32),
            pltpu.VMEM((span, dec_columns), f32),
            pltpu.VMEM((128, 2 * D_HEAD), f32),
            pltpu.VMEM((128, 2 * D_HEAD), f32),
            pltpu.VMEM(cache_keys.shape, bf16),
            pltpu.VMEM(cache_values.shape, bf16),
            pltpu.SemaphoreType.DMA((len(small) + 4,)),
        ],
        specs=[ANY] * (len(small) + 2),
        us=1.7,
    )
    partner_msg = partner(other_msg)
    far_keys, info = after((far_keys, info))
    far_near_keys = [near(k) for k in far_keys]
    run = shape((length, columns), f32)
    states = []
    marker = info
    for row in range(prompts):
        states.append(
            call(
                functools.partial(local_kernel, row),
                (prefill_queries, prefill_keys, prefill_values, near_keys, near_values, marker),
                [run] * 3,
                [pltpu.VMEM((2 * length, 2 * D_HEAD), bf16)],
                specs=[VMEM] * 5 + [ANY],
                us=1.3,
            )
        )
        marker = states[-1][0]
        if row == 0:
            far_values, marker = after((far_values, marker))
    far_near_values = [near(v) for v in far_values]
    chunks = [prefill_keys, prefill_values, near_keys, near_values]
    for quad in zip(far_keys, far_values, far_near_keys, far_near_values):
        chunks += quad
    part = shape((queries + 8, 128), f32)
    own_part, partner_part = call(
        functools.partial(prompt_kernel, span),
        (own_msg, partner_msg, info, *chunks, marker),
        [part] * 2,
        specs=[VMEM] * (3 + len(chunks)) + [ANY],
        us=0.9,
    )
    other_part = partner(partner_part)
    marker = own_part
    wide = pltpu.VMEM((2 * length, 2 * D_HEAD), bf16)
    out = None
    for index, shift in enumerate(shifts):
        last = index == len(shifts) - 1
        far = chunks[4 * (index + 1) : 4 * (index + 2)]
        for row in range(prompts):
            final = last and row == prompts - 1
            args = [info, prefill_queries, *far, *states[row], marker if out is None else out]
            specs = [VMEM] * (len(args) - 1) + [ANY]
            outs, out_specs, scratch, aliases = [run] * 3, [VMEM] * 3, [wide], {}
            if last:
                outs, out_specs = [shape(prefill_queries.shape, bf16)], [ANY]
                scratch += [pltpu.VMEM((length, columns), bf16), pltpu.SemaphoreType.DMA((group + 1,))]
                aliases = {} if out is None else {len(args) - 1: 0}
            if final:
                args += [*cache, own_part, other_part]
                specs += [VMEM] * 5
                outs.append(shape(decode_queries.shape, bf16))
                out_specs.append(ANY)
                scratch += [pltpu.VMEM(decode_queries.shape, bf16), pltpu.VMEM((span, dec_columns), f32)]
            result = call(
                functools.partial(far_kernel, shift, row, last, final, span),
                args, outs, scratch, specs=specs, out_specs=out_specs, aliases=aliases, us=1.7,
            )
            if last:
                out = result[0]
            else:
                states[row] = result
                marker = result[0]
    return (out, result[1])


def solution(mesh):
    in_specs = (
        P(None, "seq", ("head", "role")),
        P(None, "seq", ("head", "role")),
        P(None, "seq", ("head", "role")),
        P(),
        P(("seq", "role")),
        P(("seq", "role")),
        P(("seq", "role"), None, "head"),
        P(("seq", "role"), None, "head"),
        P(None, ("seq", "role"), "head"),
        P(None, ("seq", "role"), "head"),
        P(None, ("seq", "role"), "head"),
    )
    out_specs = (P(None, "seq", ("head", "role")), P(None, ("seq", "role"), "head"))
    return jax.shard_map(body, mesh=mesh, in_specs=in_specs, out_specs=out_specs, check_vma=False)
```

```python
import functools
import math

import jax
import jax.numpy as jnp
from jax import lax
from jax.experimental import pallas as pl
from jax.experimental.pallas import tpu as pltpu
from jax.sharding import PartitionSpec as P

D_HEAD = 128
MASKED_SCORE = -1e30
EXP2_SCALE = D_HEAD**-0.5 * math.log2(math.e)
VMEM_BYTES = 40 * 2**20
SUM_LIMIT = 2.0**100
NT = (((1,), (1,)), ((), ()))


def scores_of(queries, keys):
    return lax.dot_general(queries, keys, NT, preferred_element_type=jnp.float32)


def weighted(weights, values):
    return jnp.dot(weights.astype(jnp.bfloat16), values, preferred_element_type=jnp.float32)


def eye_of(rows):
    shape = (rows, 128)
    return lax.broadcasted_iota(jnp.int32, shape, 0) == lax.broadcasted_iota(jnp.int32, shape, 1)


def column_to_row(column):
    spread = jnp.where(eye_of(column.shape[0]), column, 0.0)
    return jnp.sum(spread, axis=0, keepdims=True)


def row_to_column(row, rows):
    spread = jnp.where(eye_of(rows), jnp.broadcast_to(row, (rows, 128)), 0.0)
    return jnp.sum(spread, axis=1, keepdims=True)


def select_rows(index, parts):
    chosen = parts[-1]
    for number in range(len(parts) - 2, -1, -1):
        chosen = jnp.where(index == number, parts[number], chosen)
    return chosen


def lane_sum(x):
    tiles = [x[:, i : i + 128] for i in range(0, x.shape[1], 128)]
    return jnp.sum(functools.reduce(jnp.add, tiles), axis=1, keepdims=True)


def lane_max(x):
    tiles = [x[:, i : i + 128] for i in range(0, x.shape[1], 128)]
    return jnp.max(functools.reduce(jnp.maximum, tiles), axis=1, keepdims=True)


def first_kernel(_, out_ref):
    out_ref[...] = jnp.zeros_like(out_ref)


def own_kernel(
    asg_hbm, plen_hbm, clen_hbm, dq, nk, nv, ck_ref, cv_ref, _,
    own_ref, other_ref, info_ref, sum_ref, top_ref, tot_ref, asg, plen, clen, flat, fk, fv, sems,
):
    moves = [(asg_hbm, asg), (plen_hbm, plen), (clen_hbm, clen)]
    copies = [pltpu.make_async_copy(a, b, sems.at[i]) for i, (a, b) in enumerate(moves)]
    for copy in copies:
        copy.start()
    role = lax.axis_index("role")
    steps, rows, columns = dq.shape
    span = steps * rows
    half = columns // 2
    group = half // D_HEAD
    queries = group * span
    slots = ck_ref.shape[1]
    fk[...] = jnp.zeros_like(fk)
    fv[...] = jnp.zeros_like(fv)
    for step in range(steps):
        at = slice(step * rows, (step + 1) * rows)
        flat[at, :] = dq[step].astype(jnp.float32)
        fk[at, :] = nk[step].astype(jnp.float32)
        fv[at, :] = nv[step].astype(jnp.float32)
    q_index = lax.broadcasted_iota(jnp.int32, (queries, 1), 0) % span
    q_step, q_row = q_index // rows, q_index % rows
    lane = lax.broadcasted_iota(jnp.int32, (queries, 128), 1)
    fresh_mask = (lane < span) & (lane % rows == q_row) & (lane // rows <= q_step)
    sides = ((own_ref, role), (other_ref, 1 - role))
    slices = [pl.ds(pl.multiple_of(kv * D_HEAD, D_HEAD), D_HEAD) for _, kv in sides]
    scores = []
    for (out, kv), cols in zip(sides, slices):
        heads = [flat[:, pl.ds(pl.multiple_of(kv * half + i * D_HEAD, D_HEAD), D_HEAD)] for i in range(group)]
        q = jnp.concatenate(heads, axis=0).astype(jnp.bfloat16)
        out[:queries, :] = q
        fresh = scores_of(q, fk[:, cols].astype(jnp.bfloat16))
        fresh = jnp.where(fresh_mask, fresh * EXP2_SCALE, MASKED_SCORE)
        scores.append((fresh, select_rows(q_row, [scores_of(q, ck_ref[r, :, cols]) for r in range(rows)])))
    for copy in copies:
        copy.wait()
    row_index = lax.broadcasted_iota(jnp.int32, (span, 128), 0)
    prompt = jnp.zeros((span, 128), jnp.float32)
    for row in range(rows):
        prompt = jnp.where(row_index % rows == row, asg[row].astype(jnp.float32), prompt)
    info = jnp.zeros((span, 128), jnp.int32)
    for row in range(plen.shape[0]):
        info = jnp.where(row_index == row, plen[row], info)
    info_ref[...] = info
    limit = select_rows(q_row, [clen[r] for r in range(rows)])
    live = lax.broadcasted_iota(jnp.int32, (queries, slots), 1) < limit
    for index, ((out, _), cols, (fresh, old)) in enumerate(zip(sides, slices, scores)):
        out[queries : queries + 2 * span, :] = jnp.concatenate([prompt, prompt], axis=0).astype(jnp.bfloat16)
        old = jnp.where(live, old * EXP2_SCALE, MASKED_SCORE)
        top = jnp.maximum(lane_max(fresh), lane_max(old))
        fresh = jnp.exp2(fresh - top)
        old = jnp.exp2(old - top)
        total = lane_sum(fresh) + lane_sum(old)
        summed = weighted(fresh, fv[:, cols].astype(jnp.bfloat16))
        for r in range(rows):
            summed = summed + weighted(jnp.where(q_row == r, old, 0.0), cv_ref[r, :, cols])
        sum_ref[index] = summed
        top_ref[index] = jnp.broadcast_to(top, (queries, 128))
        tot_ref[index] = jnp.broadcast_to(total, (queries, 128))


def prompt_kernel(span, *refs):
    messages, info_ref = refs[:2], refs[2]
    chunk_refs, outs = refs[3:-3], refs[-2:]
    queries = messages[0].shape[0] - 2 * span
    seqs, seq = lax.axis_size("seq"), lax.axis_index("seq")
    prompts, length, _ = chunk_refs[0].shape
    q = jnp.concatenate([m[:queries, :] for m in messages], axis=0)
    columns = []
    for m in messages:
        eight = m[queries : queries + 2 * span, :].astype(jnp.float32)[:span, :1]
        columns += [eight] * (queries // span)
    prompt = jnp.concatenate(columns, axis=0).astype(jnp.int32)
    limit = select_rows(prompt, [jnp.broadcast_to(info_ref[r : r + 1, :1], prompt.shape) for r in range(prompts)])
    parts = []
    for index in range(seqs):
        base = (seq + seqs - 2 * (index // 2)) % seqs
        chunk = base + (index % 2) * (1 - 2 * (seq % 2))
        keys = chunk_refs[2 * index]
        position = chunk * length + lax.broadcasted_iota(jnp.int32, (q.shape[0], length), 1)
        part = select_rows(prompt, [scores_of(q, keys[r]) for r in range(prompts)])
        parts.append(jnp.where(position < limit, part * EXP2_SCALE, MASKED_SCORE))
    top = lane_max(jnp.concatenate(parts, axis=1))
    summed = jnp.zeros((q.shape[0], D_HEAD), jnp.float32)
    total = jnp.zeros((q.shape[0], 1), jnp.float32)
    for index, part in enumerate(parts):
        weights = jnp.exp2(part - top)
        total = total + lane_sum(weights)
        for r in range(prompts):
            summed = summed + weighted(jnp.where(prompt == r, weights, 0.0), chunk_refs[2 * index + 1][r])
    for index, out in enumerate(outs):
        rows = slice(index * queries, (index + 1) * queries)
        out[:queries, :] = summed[rows]
        out[queries : queries + 8, :] = jnp.concatenate(
            [column_to_row(top[rows]), column_to_row(total[rows]), jnp.zeros((6, 128), jnp.float32)], axis=0
        )


def local_kernel(q_ref, k_own, v_own, k_near, v_near, _, *refs):
    outs, wide = refs[:-1], refs[-1]
    prompts, length, columns = q_ref.shape
    group = columns // D_HEAD
    seq = lax.axis_index("seq")
    wide[:, :length, :D_HEAD] = v_own[...]
    wide[:, length:, :D_HEAD] = v_near[...]
    wide[:, :, D_HEAD:] = jnp.ones((prompts, 2 * length, D_HEAD), jnp.bfloat16)
    causal = lax.broadcasted_iota(jnp.int32, (length, length), 1) <= lax.broadcasted_iota(
        jnp.int32, (length, length), 0
    )

    def run(with_near):
        for row in range(prompts):
            sum_ref, top_ref, tot_ref = outs[3 * row : 3 * row + 3]
            for head in range(group):
                cols = slice(head * D_HEAD, (head + 1) * D_HEAD)
                q = q_ref[row, :, cols]
                scores = jnp.where(causal, scores_of(q, k_own[row]), MASKED_SCORE)
                if with_near:
                    scores = jnp.concatenate([scores, scores_of(q, k_near[row])], axis=1)
                top = jnp.max(scores, axis=1, keepdims=True) * EXP2_SCALE
                summed = weighted(jnp.exp2(scores * EXP2_SCALE - top), wide[row, : scores.shape[1], :])
                sum_ref[:, cols] = summed[:, :D_HEAD]
                tot_ref[:, cols] = summed[:, D_HEAD:]
                top_ref[:, cols] = jnp.broadcast_to(top, (length, D_HEAD))

    @pl.when(seq % 2 == 0)
    def _():
        run(False)

    @pl.when(seq % 2 == 1)
    def _():
        run(True)


def merge_rows(span, cache, own_part, other_part, dec, flat):
    steps, rows, columns = dec.shape
    half = columns // 2
    group = half // D_HEAD
    queries = group * span
    role = lax.axis_index("role")
    for index, (part, kv) in enumerate(((own_part, role), (other_part, 1 - role))):
        top = row_to_column(part[queries : queries + 1, :], queries)
        total = row_to_column(part[queries + 1 : queries + 2, :], queries)
        cache_sum, cache_top, cache_tot = (ref[index] for ref in cache)
        high = jnp.maximum(top, cache_top)
        one, two = jnp.exp2(cache_top - high), jnp.exp2(top - high)
        result = (one * cache_sum + two * part[:queries, :]) / (one * cache_tot + two * total)
        for head in range(group):
            start = pl.multiple_of(kv * half + head * D_HEAD, D_HEAD)
            flat[:, pl.ds(start, D_HEAD)] = result[head * span : (head + 1) * span]
    for step in range(steps):
        dec[step] = flat[step * rows : (step + 1) * rows, :].astype(jnp.bfloat16)


def add_chunk(q, keys, wide, summed, total, top):
    scores = scores_of(q, keys)
    new = jnp.maximum(top, jnp.max(scores, axis=1, keepdims=True) * EXP2_SCALE)
    high = jnp.concatenate([new] * (scores.shape[1] // D_HEAD), axis=1)
    far = weighted(jnp.exp2(scores * EXP2_SCALE - high), wide)
    alpha = jnp.exp2(top - new)
    return summed * alpha + far[:, :D_HEAD], total * alpha + far[:, D_HEAD:], new


def add_chunk_at(q, keys, wide, summed, total, top):
    scores = scores_of(q, keys)
    high = jnp.concatenate([top] * (scores.shape[1] // D_HEAD), axis=1)
    far = weighted(jnp.exp2(scores * EXP2_SCALE - high), wide)
    return summed + far[:, :D_HEAD], total + far[:, D_HEAD:]


def widen(values, wide):
    wide[..., :D_HEAD] = values
    wide[..., D_HEAD:] = jnp.ones(values.shape, jnp.bfloat16)


def over_heads(q_ref, keys, wide, states, emit):
    prompts, length, columns = q_ref.shape
    blocks = [(row, slice(i, i + D_HEAD)) for row in range(prompts) for i in range(0, columns, D_HEAD)]
    worst = jnp.zeros((8, D_HEAD), jnp.float32)
    for row, cols in blocks:
        sum_ref, top_ref, tot_ref = states[3 * row : 3 * row + 3]
        top = top_ref[:, cols]
        summed, total = add_chunk_at(q_ref[row, :, cols], keys[row], wide[row], sum_ref[:, cols], tot_ref[:, cols], top)
        emit(row, cols, summed, total, top)
        for i in range(0, length, 8):
            worst = jnp.maximum(worst, total[i : i + 8])

    @pl.when(jnp.max(worst) > SUM_LIMIT)
    def _():
        for row, cols in blocks:
            sum_ref, top_ref, tot_ref = states[3 * row : 3 * row + 3]
            state = sum_ref[:, cols], tot_ref[:, cols], top_ref[:, cols]
            emit(row, cols, *add_chunk(q_ref[row, :, cols], keys[row], wide[row], *state))


def far_kernel(shift, q_ref, keys, values, _, *refs):
    states_in, states, wide = refs[: len(refs) // 2], refs[len(refs) // 2 : -1], refs[-1]

    def emit(row, cols, summed, total, top):
        for ref, value in zip(states[3 * row : 3 * row + 3], (summed, top, total)):
            ref[:, cols] = value

    @pl.when(lax.axis_index("seq") // 2 >= shift)
    def _():
        widen(values[...], wide)
        over_heads(q_ref, keys, wide, states_in, emit)

    @pl.when(lax.axis_index("seq") // 2 < shift)
    def _():
        for ref, value in zip(states, states_in):
            ref[...] = value[...]


def last_kernel(shift, info_ref, q_ref, keys, values, _, *refs):
    *states, out, wide = refs
    prompts, length, columns = q_ref.shape
    seq = lax.axis_index("seq")
    position = seq * length + lax.broadcasted_iota(jnp.int32, (length, D_HEAD), 0)

    def emit(row, cols, summed, total, top):
        live = position < info_ref[row : row + 1, :]
        out[row, :, cols] = jnp.where(live, summed / total, 0.0).astype(jnp.bfloat16)

    @pl.when(seq // 2 >= shift)
    def _():
        widen(values[...], wide)
        over_heads(q_ref, keys, wide, states, emit)

    @pl.when(seq // 2 < shift)
    def _():
        for row in range(prompts):
            sum_ref, _, tot_ref = states[3 * row : 3 * row + 3]
            for i in range(0, columns, D_HEAD):
                cols = slice(i, i + D_HEAD)
                emit(row, cols, sum_ref[:, cols], tot_ref[:, cols], None)


def finish_kernel(span, pre, cache_sum, cache_top, cache_tot, own_part, other_part, pre_hbm, dec_hbm, dec, flat, sems):
    copies = [pltpu.make_async_copy(pre, pre_hbm, sems.at[0]), pltpu.make_async_copy(dec, dec_hbm, sems.at[1])]
    copies[0].start()
    merge_rows(span, (cache_sum, cache_top, cache_tot), own_part, other_part, dec, flat)
    copies[1].start()
    for copy in copies:
        copy.wait()


VMEM = pl.BlockSpec(memory_space=pltpu.VMEM)
ANY = pl.BlockSpec(memory_space=pl.ANY)


def in_hbm(x):
    return pltpu.with_memory_space_constraint(x, pltpu.HBM)


def call(kernel, args, outs, scratch=(), specs=None, out_specs=None, aliases=None, us=1.0):
    return pl.pallas_call(
        kernel,
        out_shape=outs,
        in_specs=specs or [VMEM] * len(args),
        out_specs=out_specs or [VMEM] * len(outs),
        scratch_shapes=list(scratch),
        input_output_aliases=aliases or {},
        compiler_params=pltpu.CompilerParams(vmem_limit_bytes=VMEM_BYTES),
        cost_estimate=pl.CostEstimate(flops=int(us * 1.1e9), bytes_accessed=int(us * 3e6), transcendentals=0),
    )(*args)


def body(
    prefill_queries,
    prefill_keys,
    prefill_values,
    prompt_len,
    assignment,
    cache_len,
    cache_keys,
    cache_values,
    decode_queries,
    new_keys,
    new_values,
):
    seqs = lax.axis_size("seq")
    prompts, length, columns = prefill_queries.shape
    steps, rows, dec_columns = decode_queries.shape
    group = columns // D_HEAD
    span = steps * rows
    queries = group * span
    f32, bf16, i32 = jnp.float32, jnp.bfloat16, jnp.int32
    shape = jax.ShapeDtypeStruct
    after = lax.optimization_barrier

    def near(x):
        return lax.ppermute(x, "seq", [(i, i ^ 1) for i in range(seqs)])

    def around(x, shift):
        return lax.ppermute(x, "seq", [(i, (i + 2 * shift) % seqs) for i in range(seqs)])

    def partner(x):
        return lax.ppermute(x, "role", [(0, 1), (1, 0)])

    shifts = range(1, seqs // 2)
    far_keys = [around(prefill_keys, s) for s in shifts]
    far_values = [around(prefill_values, s) for s in shifts]
    (first,) = call(first_kernel, [in_hbm(prompt_len)], [shape((span, 128), f32)], specs=[ANY], us=3.0)
    own_keys, own_values, first = after((prefill_keys, prefill_values, first))
    near_keys, near_values = near(own_keys), near(own_values)
    message = shape((queries + 2 * span, 128), bf16)
    state = shape((2, queries, 128), f32)
    lengths = [assignment, prompt_len, cache_len]
    own_msg, other_msg, info, *cache = call(
        own_kernel,
        [in_hbm(x) for x in lengths] + [decode_queries, new_keys, new_values, cache_keys, cache_values, first],
        [message] * 2 + [shape((span, 128), i32)] + [state] * 3,
        [
            pltpu.SMEM(assignment.shape, i32),
            pltpu.SMEM(prompt_len.shape, i32),
            pltpu.SMEM(cache_len.shape, i32),
            pltpu.VMEM((span, dec_columns), f32),
            pltpu.VMEM((128, 2 * D_HEAD), f32),
            pltpu.VMEM((128, 2 * D_HEAD), f32),
            pltpu.SemaphoreType.DMA((len(lengths),)),
        ],
        specs=[ANY] * len(lengths) + [VMEM] * 5 + [ANY],
        us=1.3,
    )
    partner_msg = partner(other_msg)
    run = shape((length, columns), f32)
    states = call(
        local_kernel,
        (prefill_queries, prefill_keys, prefill_values, near_keys, near_values, info),
        [run] * (3 * prompts),
        [pltpu.VMEM((prompts, 2 * length, 2 * D_HEAD), bf16)],
        specs=[VMEM] * 5 + [ANY],
        us=2.9,
    )
    far_keys, partner_msg, states = after((far_keys, partner_msg, states))
    far_near_keys = [near(k) for k in far_keys]
    far_values, states = after((far_values, states))
    far_near_values = [near(v) for v in far_values]
    wide = pltpu.VMEM((prompts, length, 2 * D_HEAD), bf16)

    def far_step(shift, keys, values, states, marker):
        return call(
            functools.partial(far_kernel, shift),
            (prefill_queries, keys, values, marker, *states),
            [run] * len(states),
            [wide],
            specs=[VMEM] * 3 + [ANY] + [VMEM] * len(states),
            us=1.5,
        )

    marker = info
    for index, shift in enumerate(shifts):
        states = far_step(shift, far_keys[index], far_values[index], states, marker)
        if index < len(far_keys) - 1:
            states = far_step(shift, far_near_keys[index], far_near_values[index], states, marker)
    chunks = [prefill_keys, prefill_values, near_keys, near_values]
    for quad in zip(far_keys, far_values, far_near_keys, far_near_values):
        chunks += quad
    part = shape((queries + 8, 128), f32)
    own_part, partner_part = call(
        functools.partial(prompt_kernel, span),
        (own_msg, partner_msg, info, *chunks, states[0]),
        [part] * 2,
        specs=[VMEM] * (3 + len(chunks)) + [ANY],
        us=0.7,
    )
    other_part = partner(partner_part)
    (prefill_out,) = call(
        functools.partial(last_kernel, shifts[-1]),
        (info, prefill_queries, far_near_keys[-1], far_near_values[-1], own_part, *states),
        [shape(prefill_queries.shape, bf16)],
        [wide],
        specs=[VMEM] * 4 + [ANY] + [VMEM] * len(states),
        us=2.2,
    )
    return tuple(
        call(
            functools.partial(finish_kernel, span),
            (prefill_out, *cache, own_part, other_part),
            [shape(prefill_queries.shape, bf16), shape(decode_queries.shape, bf16)],
            [
                pltpu.VMEM(decode_queries.shape, bf16),
                pltpu.VMEM((span, dec_columns), f32),
                pltpu.SemaphoreType.DMA((2,)),
            ],
            out_specs=[ANY] * 2,
            us=1.0,
        )
    )


def solution(mesh):
    in_specs = (
        P(None, "seq", ("head", "role")),
        P(None, "seq", ("head", "role")),
        P(None, "seq", ("head", "role")),
        P(),
        P(("seq", "role")),
        P(("seq", "role")),
        P(("seq", "role"), None, "head"),
        P(("seq", "role"), None, "head"),
        P(None, ("seq", "role"), "head"),
        P(None, ("seq", "role"), "head"),
        P(None, ("seq", "role"), "head"),
    )
    out_specs = (P(None, "seq", ("head", "role")), P(None, ("seq", "role"), "head"))
    return jax.shard_map(body, mesh=mesh, in_specs=in_specs, out_specs=out_specs, check_vma=False)
```

```python
import functools
import math

import jax
import jax.numpy as jnp
from jax import lax
from jax.experimental import pallas as pl
from jax.experimental.pallas import tpu as pltpu
from jax.sharding import PartitionSpec as P

D_HEAD = 128
MASKED_SCORE = -1e30
EXP2_SCALE = D_HEAD**-0.5 * math.log2(math.e)
VMEM_BYTES = 40 * 2**20
SUM_LIMIT = 2.0**100
NT = (((1,), (1,)), ((), ()))


def scores_of(queries, keys):
    return lax.dot_general(queries, keys, NT, preferred_element_type=jnp.float32)


def weighted(weights, values):
    return jnp.dot(weights.astype(jnp.bfloat16), values, preferred_element_type=jnp.float32)


def eye_of(rows):
    shape = (rows, 128)
    return lax.broadcasted_iota(jnp.int32, shape, 0) == lax.broadcasted_iota(jnp.int32, shape, 1)


def column_to_row(column):
    spread = jnp.where(eye_of(column.shape[0]), column, 0.0)
    return jnp.sum(spread, axis=0, keepdims=True)


def row_to_column(row, rows):
    spread = jnp.where(eye_of(rows), jnp.broadcast_to(row, (rows, 128)), 0.0)
    return jnp.sum(spread, axis=1, keepdims=True)


def select_rows(index, parts):
    chosen = parts[-1]
    for number in range(len(parts) - 2, -1, -1):
        chosen = jnp.where(index == number, parts[number], chosen)
    return chosen


def lane_sum(x):
    tiles = [x[:, i : i + 128] for i in range(0, x.shape[1], 128)]
    return jnp.sum(functools.reduce(jnp.add, tiles), axis=1, keepdims=True)


def lane_max(x):
    tiles = [x[:, i : i + 128] for i in range(0, x.shape[1], 128)]
    return jnp.max(functools.reduce(jnp.maximum, tiles), axis=1, keepdims=True)


def first_kernel(_, out_ref):
    out_ref[...] = jnp.zeros_like(out_ref)


def own_kernel(
    asg, plen, clen, dq, nk, nv, ck_ref, cv_ref, _,
    own_ref, other_ref, info_ref, sum_ref, top_ref, tot_ref, flat, fk, fv,
):
    role = lax.axis_index("role")
    steps, rows, columns = dq.shape
    span = steps * rows
    half = columns // 2
    group = half // D_HEAD
    queries = group * span
    slots = ck_ref.shape[1]
    fk[...] = jnp.zeros_like(fk)
    fv[...] = jnp.zeros_like(fv)
    for step in range(steps):
        at = slice(step * rows, (step + 1) * rows)
        flat[at, :] = dq[step].astype(jnp.float32)
        fk[at, :] = nk[step].astype(jnp.float32)
        fv[at, :] = nv[step].astype(jnp.float32)
    q_index = lax.broadcasted_iota(jnp.int32, (queries, 1), 0) % span
    q_step, q_row = q_index // rows, q_index % rows
    lane = lax.broadcasted_iota(jnp.int32, (queries, 128), 1)
    fresh_mask = (lane < span) & (lane % rows == q_row) & (lane // rows <= q_step)
    sides = ((own_ref, role), (other_ref, 1 - role))
    slices = [pl.ds(pl.multiple_of(kv * D_HEAD, D_HEAD), D_HEAD) for _, kv in sides]
    scores = []
    for (out, kv), cols in zip(sides, slices):
        heads = [flat[:, pl.ds(pl.multiple_of(kv * half + i * D_HEAD, D_HEAD), D_HEAD)] for i in range(group)]
        q = jnp.concatenate(heads, axis=0).astype(jnp.bfloat16)
        out[:queries, :] = q
        fresh = scores_of(q, fk[:, cols].astype(jnp.bfloat16))
        fresh = jnp.where(fresh_mask, fresh * EXP2_SCALE, MASKED_SCORE)
        scores.append((fresh, select_rows(q_row, [scores_of(q, ck_ref[r, :, cols]) for r in range(rows)])))
    row_index = lax.broadcasted_iota(jnp.int32, (span, 128), 0)
    prompt = jnp.zeros((span, 128), jnp.float32)
    for row in range(rows):
        prompt = jnp.where(row_index % rows == row, asg[row].astype(jnp.float32), prompt)
    info = jnp.zeros((span, 128), jnp.int32)
    for row in range(plen.shape[0]):
        info = jnp.where(row_index == row, plen[row], info)
    info_ref[...] = info
    limit = select_rows(q_row, [clen[r] for r in range(rows)])
    live = lax.broadcasted_iota(jnp.int32, (queries, slots), 1) < limit
    for index, ((out, _), cols, (fresh, old)) in enumerate(zip(sides, slices, scores)):
        out[queries : queries + 2 * span, :] = jnp.concatenate([prompt, prompt], axis=0).astype(jnp.bfloat16)
        old = jnp.where(live, old * EXP2_SCALE, MASKED_SCORE)
        top = jnp.maximum(lane_max(fresh), lane_max(old))
        fresh = jnp.exp2(fresh - top)
        old = jnp.exp2(old - top)
        total = lane_sum(fresh) + lane_sum(old)
        summed = weighted(fresh, fv[:, cols].astype(jnp.bfloat16))
        for r in range(rows):
            summed = summed + weighted(jnp.where(q_row == r, old, 0.0), cv_ref[r, :, cols])
        sum_ref[index] = summed
        top_ref[index] = jnp.broadcast_to(top, (queries, 128))
        tot_ref[index] = jnp.broadcast_to(total, (queries, 128))


def prompt_kernel(span, *refs):
    messages, info_ref = refs[:2], refs[2]
    chunk_refs, outs = refs[3:-3], refs[-2:]
    queries = messages[0].shape[0] - 2 * span
    seqs, seq = lax.axis_size("seq"), lax.axis_index("seq")
    prompts, length, _ = chunk_refs[0].shape
    q = jnp.concatenate([m[:queries, :] for m in messages], axis=0)
    columns = []
    for m in messages:
        eight = m[queries : queries + 2 * span, :].astype(jnp.float32)[:span, :1]
        columns += [eight] * (queries // span)
    prompt = jnp.concatenate(columns, axis=0).astype(jnp.int32)
    limit = select_rows(prompt, [jnp.broadcast_to(info_ref[r : r + 1, :1], prompt.shape) for r in range(prompts)])
    parts = []
    for index in range(seqs):
        base = (seq + seqs - 2 * (index // 2)) % seqs
        chunk = base + (index % 2) * (1 - 2 * (seq % 2))
        keys = chunk_refs[2 * index]
        position = chunk * length + lax.broadcasted_iota(jnp.int32, (q.shape[0], length), 1)
        part = select_rows(prompt, [scores_of(q, keys[r]) for r in range(prompts)])
        parts.append(jnp.where(position < limit, part * EXP2_SCALE, MASKED_SCORE))
    top = lane_max(jnp.concatenate(parts, axis=1))
    summed = jnp.zeros((q.shape[0], D_HEAD), jnp.float32)
    total = jnp.zeros((q.shape[0], 1), jnp.float32)
    for index, part in enumerate(parts):
        weights = jnp.exp2(part - top)
        total = total + lane_sum(weights)
        for r in range(prompts):
            summed = summed + weighted(jnp.where(prompt == r, weights, 0.0), chunk_refs[2 * index + 1][r])
    for index, out in enumerate(outs):
        rows = slice(index * queries, (index + 1) * queries)
        out[:queries, :] = summed[rows]
        out[queries : queries + 8, :] = jnp.concatenate(
            [column_to_row(top[rows]), column_to_row(total[rows]), jnp.zeros((6, 128), jnp.float32)], axis=0
        )


def local_kernel(blocks, q_ref, k_own, v_own, k_near, v_near, _, *refs):
    outs, wide = refs[:-1], refs[-1]
    prompts, length, _ = q_ref.shape
    seq = lax.axis_index("seq")
    for row in sorted({row for row, _, _ in blocks}):
        wide[row, :length, :D_HEAD] = v_own[row]
        wide[row, length:, :D_HEAD] = v_near[row]
        wide[row, :, D_HEAD:] = jnp.ones((2 * length, D_HEAD), jnp.bfloat16)
    causal = lax.broadcasted_iota(jnp.int32, (length, length), 1) <= lax.broadcasted_iota(
        jnp.int32, (length, length), 0
    )

    def run(with_near):
        for index, (row, start, stop) in enumerate(blocks):
            sum_ref, top_ref, tot_ref = outs[3 * index : 3 * index + 3]
            for head in range(start, stop):
                cols = slice((head - start) * D_HEAD, (head - start + 1) * D_HEAD)
                q = q_ref[row, :, head * D_HEAD : (head + 1) * D_HEAD]
                scores = jnp.where(causal, scores_of(q, k_own[row]), MASKED_SCORE)
                if with_near:
                    scores = jnp.concatenate([scores, scores_of(q, k_near[row])], axis=1)
                top = jnp.max(scores, axis=1, keepdims=True) * EXP2_SCALE
                summed = weighted(jnp.exp2(scores * EXP2_SCALE - top), wide[row, : scores.shape[1], :])
                sum_ref[:, cols] = summed[:, :D_HEAD]
                tot_ref[:, cols] = summed[:, D_HEAD:]
                top_ref[:, cols] = jnp.broadcast_to(top, (length, D_HEAD))

    @pl.when(seq % 2 == 0)
    def _():
        run(False)

    @pl.when(seq % 2 == 1)
    def _():
        run(True)


def merge_rows(span, cache, own_part, other_part, dec, flat):
    steps, rows, columns = dec.shape
    half = columns // 2
    group = half // D_HEAD
    queries = group * span
    role = lax.axis_index("role")
    for index, (part, kv) in enumerate(((own_part, role), (other_part, 1 - role))):
        top = row_to_column(part[queries : queries + 1, :], queries)
        total = row_to_column(part[queries + 1 : queries + 2, :], queries)
        cache_sum, cache_top, cache_tot = (ref[index] for ref in cache)
        high = jnp.maximum(top, cache_top)
        one, two = jnp.exp2(cache_top - high), jnp.exp2(top - high)
        result = (one * cache_sum + two * part[:queries, :]) / (one * cache_tot + two * total)
        for head in range(group):
            start = pl.multiple_of(kv * half + head * D_HEAD, D_HEAD)
            flat[:, pl.ds(start, D_HEAD)] = result[head * span : (head + 1) * span]
    for step in range(steps):
        dec[step] = flat[step * rows : (step + 1) * rows, :].astype(jnp.bfloat16)


def joined(q, keys):
    return jnp.concatenate([scores_of(q, one) for one in keys], axis=1)


def add_keys(q, keys, wide, summed, total, top):
    scores = joined(q, keys)
    new = jnp.maximum(top, jnp.max(scores, axis=1, keepdims=True) * EXP2_SCALE)
    high = jnp.concatenate([new] * (scores.shape[1] // D_HEAD), axis=1)
    far = weighted(jnp.exp2(scores * EXP2_SCALE - high), wide)
    alpha = jnp.exp2(top - new)
    return summed * alpha + far[:, :D_HEAD], total * alpha + far[:, D_HEAD:], new


def add_keys_at(q, keys, wide, summed, total, top):
    scores = joined(q, keys)
    high = jnp.concatenate([top] * (scores.shape[1] // D_HEAD), axis=1)
    far = weighted(jnp.exp2(scores * EXP2_SCALE - high), wide)
    return summed + far[:, :D_HEAD], total + far[:, D_HEAD:]


def far_kernel(blocks, shift, last, info_ref, q_ref, k_one, v_one, k_two, v_two, _, *refs):
    prompts, length, columns = q_ref.shape
    count = 3 * len(blocks)
    states, outs, (wide, sem) = refs[:count], refs[count:-2], refs[-2:]
    seq = lax.axis_index("seq")
    position = seq * length + lax.broadcasted_iota(jnp.int32, (length, D_HEAD), 0)
    places = [
        (index, row, slice(head * D_HEAD, (head + 1) * D_HEAD), slice((head - start) * D_HEAD, (head - start + 1) * D_HEAD))
        for index, (row, start, stop) in enumerate(blocks)
        for head in range(start, stop)
    ]

    def state_of(index, at):
        return (states[3 * index][:, at], states[3 * index + 2][:, at], states[3 * index + 1][:, at])

    def emit(index, row, cols, at, summed, total, top):
        if last:
            live = position < info_ref[row : row + 1, :]
            outs[0][row, :, cols] = jnp.where(live, summed / total, 0.0).astype(jnp.bfloat16)
        else:
            for ref, value in zip(outs[3 * index : 3 * index + 3], (summed, top, total)):
                ref[:, at] = value

    @pl.when(seq // 2 >= shift)
    def _():
        wide[:, :length, :D_HEAD] = v_one[...]
        wide[:, length:, :D_HEAD] = v_two[...]
        wide[:, :, D_HEAD:] = jnp.ones((prompts, 2 * length, D_HEAD), jnp.bfloat16)
        worst = jnp.zeros((8, D_HEAD), jnp.float32)
        for index, row, cols, at in places:
            state = state_of(index, at)
            summed, total = add_keys_at(q_ref[row, :, cols], (k_one[row], k_two[row]), wide[row], *state)
            emit(index, row, cols, at, summed, total, state[2])
            peaks = [total[i : i + 8] for i in range(0, length, 8)]
            worst = functools.reduce(jnp.maximum, [functools.reduce(jnp.maximum, peaks[i::4]) for i in range(4)], worst)

        @pl.when(jnp.max(worst) > SUM_LIMIT)
        def _():
            for index, (row, start, stop) in enumerate(blocks):

                @pl.loop(0, stop - start)
                def _(head, index=index, row=row, start=start):
                    at = pl.ds(pl.multiple_of(head * D_HEAD, D_HEAD), D_HEAD)
                    cols = pl.ds(pl.multiple_of((start + head) * D_HEAD, D_HEAD), D_HEAD)
                    state = state_of(index, at)
                    new = add_keys(q_ref[row, :, cols], (k_one[row], k_two[row]), wide[row], *state)
                    emit(index, row, cols, at, *new)

    @pl.when(seq // 2 < shift)
    def _():
        for index, row, cols, at in places:
            emit(index, row, cols, at, *state_of(index, at))
        if last:
            copy = pltpu.make_async_copy(outs[0], outs[1], sem)
            copy.start()
            copy.wait()


def finish_kernel(
    shift, span, pre, cache_sum, cache_top, cache_tot, own_part, other_part, _, dec_hbm, pre_hbm, dec, flat, sems
):
    copy = pltpu.make_async_copy(pre, pre_hbm, sems.at[0])
    dec_copy = pltpu.make_async_copy(dec, dec_hbm, sems.at[1])
    late = lax.axis_index("seq") // 2 >= shift

    @pl.when(late)
    def _():
        copy.start()

    merge_rows(span, (cache_sum, cache_top, cache_tot), own_part, other_part, dec, flat)
    dec_copy.start()

    @pl.when(late)
    def _():
        copy.wait()

    dec_copy.wait()


VMEM = pl.BlockSpec(memory_space=pltpu.VMEM)
ANY = pl.BlockSpec(memory_space=pl.ANY)
SMEM = pl.BlockSpec(memory_space=pltpu.SMEM)


def in_hbm(x):
    return pltpu.with_memory_space_constraint(x, pltpu.HBM)


def call(kernel, args, outs, scratch=(), specs=None, out_specs=None, aliases=None, us=1.0):
    return pl.pallas_call(
        kernel,
        out_shape=outs,
        in_specs=specs or [VMEM] * len(args),
        out_specs=out_specs or [VMEM] * len(outs),
        scratch_shapes=list(scratch),
        input_output_aliases=aliases or {},
        compiler_params=pltpu.CompilerParams(vmem_limit_bytes=VMEM_BYTES),
        cost_estimate=pl.CostEstimate(flops=int(us * 1.1e9), bytes_accessed=int(us * 3e6), transcendentals=0),
    )(*args)


def body(
    prefill_queries,
    prefill_keys,
    prefill_values,
    prompt_len,
    assignment,
    cache_len,
    cache_keys,
    cache_values,
    decode_queries,
    new_keys,
    new_values,
):
    seqs = lax.axis_size("seq")
    prompts, length, columns = prefill_queries.shape
    steps, rows, dec_columns = decode_queries.shape
    group = columns // D_HEAD
    span = steps * rows
    queries = group * span
    f32, bf16, i32 = jnp.float32, jnp.bfloat16, jnp.int32
    shape = jax.ShapeDtypeStruct
    after = lax.optimization_barrier

    def near(x):
        return lax.ppermute(x, "seq", [(i, i ^ 1) for i in range(seqs)])

    def around(x, shift):
        return lax.ppermute(x, "seq", [(i, (i + 2 * shift) % seqs) for i in range(seqs)])

    def partner(x):
        moves = [(i * 2 + r, (i ^ 1) * 2 + 1 - r) for i in range(seqs) for r in range(2)]
        return lax.ppermute(x, ("seq", "role"), moves)

    shifts = range(1, seqs // 2)
    far_keys = [around(prefill_keys, s) for s in shifts]
    far_values = [around(prefill_values, s) for s in shifts]
    (first,) = call(first_kernel, [in_hbm(prompt_len)], [shape((span, 128), f32)], specs=[ANY], us=3.0)
    own_keys, own_values, first = after((prefill_keys, prefill_values, first))
    near_keys, near_values = near(own_keys), near(own_values)
    message = shape((queries + 2 * span, 128), bf16)
    state = shape((2, queries, 128), f32)
    own_msg, other_msg, info, *cache = call(
        own_kernel,
        [assignment, prompt_len, cache_len, decode_queries, new_keys, new_values, cache_keys, cache_values, first],
        [message] * 2 + [shape((span, 128), i32)] + [state] * 3,
        [
            pltpu.VMEM((span, dec_columns), f32),
            pltpu.VMEM((128, 2 * D_HEAD), f32),
            pltpu.VMEM((128, 2 * D_HEAD), f32),
        ],
        specs=[SMEM] * 3 + [VMEM] * 5 + [ANY],
        us=1.3,
    )
    partner_msg = partner(other_msg)
    blocks = [(row, 0, group) for row in range(prompts - 1)]
    blocks += [(prompts - 1, 0, group // 2), (prompts - 1, group // 2, group)]
    runs = [[shape((length, (stop - start) * D_HEAD), f32)] * 3 for _, start, stop in blocks]

    def local(some, outs, marker):
        return call(
            functools.partial(local_kernel, some),
            (prefill_queries, prefill_keys, prefill_values, near_keys, near_values, marker),
            sum(outs, []),
            [pltpu.VMEM((prompts, 2 * length, 2 * D_HEAD), bf16)],
            specs=[VMEM] * 5 + [ANY],
            us=0.2 * sum(stop - start for _, start, stop in some),
        )

    states = local(blocks[:-1], runs[:-1], info)
    far_keys, states = after((far_keys, states))
    far_near_keys = [near(k) for k in far_keys]
    far_values, partner_msg, states = after((far_values, partner_msg, states))
    far_near_values = [near(v) for v in far_values]
    states = [*states, *local(blocks[-1:], runs[-1:], states[0])]
    far = list(zip(far_keys, far_values, far_near_keys, far_near_values))
    chunks = [prefill_keys, prefill_values, near_keys, near_values] + sum([list(four) for four in far], [])
    part = shape((queries + 8, 128), f32)
    own_part, partner_part = call(
        functools.partial(prompt_kernel, span),
        (own_msg, partner_msg, info, *chunks, states[-1]),
        [part] * 2,
        specs=[VMEM] * (3 + len(chunks)) + [ANY],
        us=0.7,
    )
    other_part = partner(partner_part)
    for index, shift in enumerate(shifts):
        last = index == len(shifts) - 1
        outs, out_specs = sum(runs, []), [VMEM] * len(states)
        if last:
            outs, out_specs = [shape(prefill_queries.shape, bf16)] * 2, [VMEM, ANY]
        states = call(
            functools.partial(far_kernel, blocks, shift, last),
            (info, prefill_queries, *far[index], own_part, *states),
            outs,
            [pltpu.VMEM((prompts, 2 * length, 2 * D_HEAD), bf16), pltpu.SemaphoreType.DMA(())],
            specs=[VMEM] * 6 + [ANY] + [VMEM] * len(states),
            out_specs=out_specs,
            us=2.8,
        )
    pre, prefill_out = states
    decode_out, prefill_out = call(
        functools.partial(finish_kernel, shifts[-1], span),
        (pre, *cache, own_part, other_part, prefill_out),
        [shape(decode_queries.shape, bf16), shape(prefill_queries.shape, bf16)],
        [
            pltpu.VMEM(decode_queries.shape, bf16),
            pltpu.VMEM((span, dec_columns), f32),
            pltpu.SemaphoreType.DMA((2,)),
        ],
        specs=[VMEM] * 6 + [ANY],
        out_specs=[ANY, ANY],
        aliases={6: 1},
        us=0.7,
    )
    return prefill_out, decode_out


def solution(mesh):
    in_specs = (
        P(None, "seq", ("head", "role")),
        P(None, "seq", ("head", "role")),
        P(None, "seq", ("head", "role")),
        P(),
        P(("seq", "role")),
        P(("seq", "role")),
        P(("seq", "role"), None, "head"),
        P(("seq", "role"), None, "head"),
        P(None, ("seq", "role"), "head"),
        P(None, ("seq", "role"), "head"),
        P(None, ("seq", "role"), "head"),
    )
    out_specs = (P(None, "seq", ("head", "role")), P(None, ("seq", "role"), "head"))
    return jax.shard_map(body, mesh=mesh, in_specs=in_specs, out_specs=out_specs, check_vma=False)
```

```python
import functools
import math

import jax
import jax.numpy as jnp
from jax import lax
from jax.experimental import pallas as pl
from jax.experimental.pallas import tpu as pltpu
from jax.sharding import PartitionSpec as P

D_HEAD = 128
MASKED_SCORE = -1e30
EXP2_SCALE = D_HEAD**-0.5 * math.log2(math.e)
VMEM_BYTES = 40 * 2**20
SUM_LIMIT = 2.0**100
NT = (((1,), (1,)), ((), ()))


def scores_of(queries, keys):
    return lax.dot_general(queries, keys, NT, preferred_element_type=jnp.float32)


def weighted(weights, values):
    return jnp.dot(weights.astype(jnp.bfloat16), values, preferred_element_type=jnp.float32)


def eye_of(rows):
    shape = (rows, 128)
    return lax.broadcasted_iota(jnp.int32, shape, 0) == lax.broadcasted_iota(jnp.int32, shape, 1)


def column_to_row(column):
    spread = jnp.where(eye_of(column.shape[0]), column, 0.0)
    return jnp.sum(spread, axis=0, keepdims=True)


def row_to_column(row, rows):
    spread = jnp.where(eye_of(rows), jnp.broadcast_to(row, (rows, 128)), 0.0)
    return jnp.sum(spread, axis=1, keepdims=True)


def select_rows(index, parts):
    chosen = parts[-1]
    for number in range(len(parts) - 2, -1, -1):
        chosen = jnp.where(index == number, parts[number], chosen)
    return chosen


def lane_sum(x):
    tiles = [x[:, i : i + 128] for i in range(0, x.shape[1], 128)]
    return jnp.sum(functools.reduce(jnp.add, tiles), axis=1, keepdims=True)


def lane_max(x):
    tiles = [x[:, i : i + 128] for i in range(0, x.shape[1], 128)]
    return jnp.max(functools.reduce(jnp.maximum, tiles), axis=1, keepdims=True)


def first_kernel(_, out_ref):
    out_ref[...] = jnp.zeros_like(out_ref)


def own_kernel(
    asg, plen, clen, dq, nk, nv, ck_ref, cv_ref, _,
    own_ref, other_ref, info_ref, sum_ref, top_ref, tot_ref, flat, fk, fv,
):
    role = lax.axis_index("role")
    steps, rows, columns = dq.shape
    span = steps * rows
    half = columns // 2
    group = half // D_HEAD
    queries = group * span
    slots = ck_ref.shape[1]
    fk[...] = jnp.zeros_like(fk)
    fv[...] = jnp.zeros_like(fv)
    for step in range(steps):
        at = slice(step * rows, (step + 1) * rows)
        flat[at, :] = dq[step].astype(jnp.float32)
        fk[at, :] = nk[step].astype(jnp.float32)
        fv[at, :] = nv[step].astype(jnp.float32)
    q_index = lax.broadcasted_iota(jnp.int32, (queries, 1), 0) % span
    q_step, q_row = q_index // rows, q_index % rows
    lane = lax.broadcasted_iota(jnp.int32, (queries, 128), 1)
    fresh_mask = (lane < span) & (lane % rows == q_row) & (lane // rows <= q_step)
    sides = ((own_ref, role), (other_ref, 1 - role))
    slices = [pl.ds(pl.multiple_of(kv * D_HEAD, D_HEAD), D_HEAD) for _, kv in sides]
    scores = []
    for (out, kv), cols in zip(sides, slices):
        heads = [flat[:, pl.ds(pl.multiple_of(kv * half + i * D_HEAD, D_HEAD), D_HEAD)] for i in range(group)]
        q = jnp.concatenate(heads, axis=0).astype(jnp.bfloat16)
        out[:queries, :] = q
        fresh = scores_of(q, fk[:, cols].astype(jnp.bfloat16))
        fresh = jnp.where(fresh_mask, fresh * EXP2_SCALE, MASKED_SCORE)
        scores.append((fresh, select_rows(q_row, [scores_of(q, ck_ref[r, :, cols]) for r in range(rows)])))
    row_index = lax.broadcasted_iota(jnp.int32, (span, 128), 0)
    prompt = jnp.zeros((span, 128), jnp.float32)
    for row in range(rows):
        prompt = jnp.where(row_index % rows == row, asg[row].astype(jnp.float32), prompt)
    info = jnp.zeros((span, 128), jnp.int32)
    for row in range(plen.shape[0]):
        info = jnp.where(row_index == row, plen[row], info)
    info_ref[...] = info
    limit = select_rows(q_row, [clen[r] for r in range(rows)])
    live = lax.broadcasted_iota(jnp.int32, (queries, slots), 1) < limit
    for index, ((out, _), cols, (fresh, old)) in enumerate(zip(sides, slices, scores)):
        out[queries : queries + 2 * span, :] = jnp.concatenate([prompt, prompt], axis=0).astype(jnp.bfloat16)
        old = jnp.where(live, old * EXP2_SCALE, MASKED_SCORE)
        top = jnp.maximum(lane_max(fresh), lane_max(old))
        fresh = jnp.exp2(fresh - top)
        old = jnp.exp2(old - top)
        total = lane_sum(fresh) + lane_sum(old)
        summed = weighted(fresh, fv[:, cols].astype(jnp.bfloat16))
        for r in range(rows):
            summed = summed + weighted(jnp.where(q_row == r, old, 0.0), cv_ref[r, :, cols])
        sum_ref[index] = summed
        top_ref[index] = jnp.broadcast_to(top, (queries, 128))
        tot_ref[index] = jnp.broadcast_to(total, (queries, 128))


def prompt_kernel(span, *refs):
    messages, info_ref = refs[:2], refs[2]
    chunk_refs, outs = refs[3:-3], refs[-2:]
    queries = messages[0].shape[0] - 2 * span
    seqs, seq = lax.axis_size("seq"), lax.axis_index("seq")
    prompts, length, _ = chunk_refs[0].shape
    q = jnp.concatenate([m[:queries, :] for m in messages], axis=0)
    columns = []
    for m in messages:
        eight = m[queries : queries + 2 * span, :].astype(jnp.float32)[:span, :1]
        columns += [eight] * (queries // span)
    prompt = jnp.concatenate(columns, axis=0).astype(jnp.int32)
    limit = select_rows(prompt, [jnp.broadcast_to(info_ref[r : r + 1, :1], prompt.shape) for r in range(prompts)])
    parts = []
    for index in range(seqs):
        base = (seq + seqs - 2 * (index // 2)) % seqs
        chunk = base + (index % 2) * (1 - 2 * (seq % 2))
        keys = chunk_refs[2 * index]
        position = chunk * length + lax.broadcasted_iota(jnp.int32, (q.shape[0], length), 1)
        part = select_rows(prompt, [scores_of(q, keys[r]) for r in range(prompts)])
        parts.append(jnp.where(position < limit, part * EXP2_SCALE, MASKED_SCORE))
    top = lane_max(jnp.concatenate(parts, axis=1))
    summed = jnp.zeros((q.shape[0], D_HEAD), jnp.float32)
    total = jnp.zeros((q.shape[0], 1), jnp.float32)
    for index, part in enumerate(parts):
        weights = jnp.exp2(part - top)
        total = total + lane_sum(weights)
        for r in range(prompts):
            summed = summed + weighted(jnp.where(prompt == r, weights, 0.0), chunk_refs[2 * index + 1][r])
    for index, out in enumerate(outs):
        rows = slice(index * queries, (index + 1) * queries)
        out[:queries, :] = summed[rows]
        out[queries : queries + 8, :] = jnp.concatenate(
            [column_to_row(top[rows]), column_to_row(total[rows]), jnp.zeros((6, 128), jnp.float32)], axis=0
        )


def local_kernel(blocks, q_ref, k_own, v_own, k_near, v_near, _, *refs):
    outs, wide = refs[:-1], refs[-1]
    prompts, length, _ = q_ref.shape
    seq = lax.axis_index("seq")
    for row in sorted({row for row, _, _ in blocks}):
        wide[row, :length, :D_HEAD] = v_own[row]
        wide[row, length:, :D_HEAD] = v_near[row]
        wide[row, :, D_HEAD:] = jnp.ones((2 * length, D_HEAD), jnp.bfloat16)
    causal = lax.broadcasted_iota(jnp.int32, (length, length), 1) <= lax.broadcasted_iota(
        jnp.int32, (length, length), 0
    )

    def run(with_near):
        for index, (row, start, stop) in enumerate(blocks):
            sum_ref, top_ref, tot_ref = outs[3 * index : 3 * index + 3]
            for head in range(start, stop):
                cols = slice((head - start) * D_HEAD, (head - start + 1) * D_HEAD)
                q = q_ref[row, :, head * D_HEAD : (head + 1) * D_HEAD]
                scores = jnp.where(causal, scores_of(q, k_own[row]), MASKED_SCORE)
                if with_near:
                    scores = jnp.concatenate([scores, scores_of(q, k_near[row])], axis=1)
                top = jnp.max(scores, axis=1, keepdims=True) * EXP2_SCALE
                summed = weighted(jnp.exp2(scores * EXP2_SCALE - top), wide[row, : scores.shape[1], :])
                sum_ref[:, cols] = summed[:, :D_HEAD]
                tot_ref[:, cols] = summed[:, D_HEAD:]
                top_ref[:, cols] = jnp.broadcast_to(top, (length, D_HEAD))

    @pl.when(seq % 2 == 0)
    def _():
        run(False)

    @pl.when(seq % 2 == 1)
    def _():
        run(True)


def merge_rows(span, cache, own_part, other_part, dec, flat):
    steps, rows, columns = dec.shape
    half = columns // 2
    group = half // D_HEAD
    queries = group * span
    role = lax.axis_index("role")
    for index, (part, kv) in enumerate(((own_part, role), (other_part, 1 - role))):
        top = row_to_column(part[queries : queries + 1, :], queries)
        total = row_to_column(part[queries + 1 : queries + 2, :], queries)
        cache_sum, cache_top, cache_tot = (ref[index] for ref in cache)
        high = jnp.maximum(top, cache_top)
        one, two = jnp.exp2(cache_top - high), jnp.exp2(top - high)
        result = (one * cache_sum + two * part[:queries, :]) / (one * cache_tot + two * total)
        for head in range(group):
            start = pl.multiple_of(kv * half + head * D_HEAD, D_HEAD)
            flat[:, pl.ds(start, D_HEAD)] = result[head * span : (head + 1) * span]
    for step in range(steps):
        dec[step] = flat[step * rows : (step + 1) * rows, :].astype(jnp.bfloat16)


def joined(q, keys):
    return jnp.concatenate([scores_of(q, one) for one in keys], axis=1)


def add_keys(q, keys, wide, summed, total, top):
    scores = joined(q, keys)
    new = jnp.maximum(top, jnp.max(scores, axis=1, keepdims=True) * EXP2_SCALE)
    high = jnp.concatenate([new] * (scores.shape[1] // D_HEAD), axis=1)
    far = weighted(jnp.exp2(scores * EXP2_SCALE - high), wide)
    alpha = jnp.exp2(top - new)
    return summed * alpha + far[:, :D_HEAD], total * alpha + far[:, D_HEAD:], new


def add_keys_at(q, keys, wide, summed, total, top):
    scores = joined(q, keys)
    high = jnp.concatenate([top] * (scores.shape[1] // D_HEAD), axis=1)
    far = weighted(jnp.exp2(scores * EXP2_SCALE - high), wide)
    return summed + far[:, :D_HEAD], total + far[:, D_HEAD:]


def far_kernel(blocks, shift, last, info_ref, q_ref, k_one, v_one, k_two, v_two, _, *refs):
    prompts, length, columns = q_ref.shape
    count = 3 * len(blocks)
    states, outs, (wide, sem) = refs[:count], refs[count:-2], refs[-2:]
    seq = lax.axis_index("seq")
    position = seq * length + lax.broadcasted_iota(jnp.int32, (length, D_HEAD), 0)
    places = [
        (index, row, slice(head * D_HEAD, (head + 1) * D_HEAD), slice((head - start) * D_HEAD, (head - start + 1) * D_HEAD))
        for index, (row, start, stop) in enumerate(blocks)
        for head in range(start, stop)
    ]

    def state_of(index, at):
        return (states[3 * index][:, at], states[3 * index + 2][:, at], states[3 * index + 1][:, at])

    def emit(index, row, cols, at, summed, total, top):
        if last:
            live = position < info_ref[row : row + 1, :]
            outs[0][row, :, cols] = jnp.where(live, summed / total, 0.0).astype(jnp.bfloat16)
        else:
            for ref, value in zip(outs[3 * index : 3 * index + 3], (summed, top, total)):
                ref[:, at] = value

    @pl.when(seq // 2 >= shift)
    def _():
        wide[:, :length, :D_HEAD] = v_one[...]
        wide[:, length:, :D_HEAD] = v_two[...]
        wide[:, :, D_HEAD:] = jnp.ones((prompts, 2 * length, D_HEAD), jnp.bfloat16)
        worst = jnp.zeros((8, D_HEAD), jnp.float32)
        if last:
            first_copy = pltpu.make_async_copy(outs[0].at[0], outs[1].at[0], sem)
        for index, row, cols, at in places:
            state = state_of(index, at)
            summed, total = add_keys_at(q_ref[row, :, cols], (k_one[row], k_two[row]), wide[row], *state)
            emit(index, row, cols, at, summed, total, state[2])
            if last and row == 0 and cols.stop == columns:
                first_copy.start()
            peaks = [total[i : i + 8] for i in range(0, length, 8)]
            worst = functools.reduce(jnp.maximum, [functools.reduce(jnp.maximum, peaks[i::4]) for i in range(4)], worst)

        if last:
            first_copy.wait()

        @pl.when(jnp.max(worst) > SUM_LIMIT)
        def _():
            for index, (row, start, stop) in enumerate(blocks):

                @pl.loop(0, stop - start)
                def _(head, index=index, row=row, start=start):
                    at = pl.ds(pl.multiple_of(head * D_HEAD, D_HEAD), D_HEAD)
                    cols = pl.ds(pl.multiple_of((start + head) * D_HEAD, D_HEAD), D_HEAD)
                    state = state_of(index, at)
                    new = add_keys(q_ref[row, :, cols], (k_one[row], k_two[row]), wide[row], *state)
                    emit(index, row, cols, at, *new)

            if last:
                first_copy.start()
                first_copy.wait()

    @pl.when(seq // 2 < shift)
    def _():
        for index, row, cols, at in places:
            emit(index, row, cols, at, *state_of(index, at))
        if last:
            copy = pltpu.make_async_copy(outs[0], outs[1], sem)
            copy.start()
            copy.wait()


def finish_kernel(
    shift, span, pre, cache_sum, cache_top, cache_tot, own_part, other_part, _, dec_hbm, pre_hbm, dec, flat, sems
):
    copy = pltpu.make_async_copy(pre.at[1:], pre_hbm.at[1:], sems.at[0])
    dec_copy = pltpu.make_async_copy(dec, dec_hbm, sems.at[1])
    late = lax.axis_index("seq") // 2 >= shift

    @pl.when(late)
    def _():
        copy.start()

    merge_rows(span, (cache_sum, cache_top, cache_tot), own_part, other_part, dec, flat)
    dec_copy.start()

    @pl.when(late)
    def _():
        copy.wait()

    dec_copy.wait()


VMEM = pl.BlockSpec(memory_space=pltpu.VMEM)
ANY = pl.BlockSpec(memory_space=pl.ANY)
SMEM = pl.BlockSpec(memory_space=pltpu.SMEM)


def in_hbm(x):
    return pltpu.with_memory_space_constraint(x, pltpu.HBM)


def call(kernel, args, outs, scratch=(), specs=None, out_specs=None, aliases=None, us=1.0):
    return pl.pallas_call(
        kernel,
        out_shape=outs,
        in_specs=specs or [VMEM] * len(args),
        out_specs=out_specs or [VMEM] * len(outs),
        scratch_shapes=list(scratch),
        input_output_aliases=aliases or {},
        compiler_params=pltpu.CompilerParams(vmem_limit_bytes=VMEM_BYTES),
        cost_estimate=pl.CostEstimate(flops=int(us * 1.1e9), bytes_accessed=int(us * 3e6), transcendentals=0),
    )(*args)


def body(
    prefill_queries,
    prefill_keys,
    prefill_values,
    prompt_len,
    assignment,
    cache_len,
    cache_keys,
    cache_values,
    decode_queries,
    new_keys,
    new_values,
):
    seqs = lax.axis_size("seq")
    prompts, length, columns = prefill_queries.shape
    steps, rows, dec_columns = decode_queries.shape
    group = columns // D_HEAD
    span = steps * rows
    queries = group * span
    f32, bf16, i32 = jnp.float32, jnp.bfloat16, jnp.int32
    shape = jax.ShapeDtypeStruct
    after = lax.optimization_barrier

    def near(x):
        return lax.ppermute(x, "seq", [(i, i ^ 1) for i in range(seqs)])

    def around(x, shift):
        return lax.ppermute(x, "seq", [(i, (i + 2 * shift) % seqs) for i in range(seqs)])

    def partner(x):
        moves = [(i * 2 + r, (i ^ 1) * 2 + 1 - r) for i in range(seqs) for r in range(2)]
        return lax.ppermute(x, ("seq", "role"), moves)

    shifts = range(1, seqs // 2)
    far_keys = [around(prefill_keys, s) for s in shifts]
    far_values = [around(prefill_values, s) for s in shifts]
    (first,) = call(first_kernel, [in_hbm(prompt_len)], [shape((span, 128), f32)], specs=[ANY], us=3.0)
    own_keys, own_values, first = after((prefill_keys, prefill_values, first))
    near_keys, near_values = near(own_keys), near(own_values)
    message = shape((queries + 2 * span, 128), bf16)
    state = shape((2, queries, 128), f32)
    own_msg, other_msg, info, *cache = call(
        own_kernel,
        [assignment, prompt_len, cache_len, decode_queries, new_keys, new_values, cache_keys, cache_values, first],
        [message] * 2 + [shape((span, 128), i32)] + [state] * 3,
        [
            pltpu.VMEM((span, dec_columns), f32),
            pltpu.VMEM((128, 2 * D_HEAD), f32),
            pltpu.VMEM((128, 2 * D_HEAD), f32),
        ],
        specs=[SMEM] * 3 + [VMEM] * 5 + [ANY],
        us=1.3,
    )
    partner_msg = partner(other_msg)
    blocks = [(row, 0, group) for row in range(prompts - 1)]
    blocks += [(prompts - 1, 0, group // 2), (prompts - 1, group // 2, group)]
    runs = [[shape((length, (stop - start) * D_HEAD), f32)] * 3 for _, start, stop in blocks]

    def local(some, outs, marker):
        return call(
            functools.partial(local_kernel, some),
            (prefill_queries, prefill_keys, prefill_values, near_keys, near_values, marker),
            sum(outs, []),
            [pltpu.VMEM((prompts, 2 * length, 2 * D_HEAD), bf16)],
            specs=[VMEM] * 5 + [ANY],
            us=0.2 * sum(stop - start for _, start, stop in some),
        )

    states = local(blocks[:-1], runs[:-1], info)
    far_keys, states = after((far_keys, states))
    far_near_keys = [near(k) for k in far_keys]
    far_values, partner_msg, states = after((far_values, partner_msg, states))
    far_near_values = [near(v) for v in far_values]
    states = [*states, *local(blocks[-1:], runs[-1:], states[0])]
    far = list(zip(far_keys, far_values, far_near_keys, far_near_values))
    chunks = [prefill_keys, prefill_values, near_keys, near_values] + sum([list(four) for four in far], [])
    part = shape((queries + 8, 128), f32)
    own_part, partner_part = call(
        functools.partial(prompt_kernel, span),
        (own_msg, partner_msg, info, *chunks, states[-1]),
        [part] * 2,
        specs=[VMEM] * (3 + len(chunks)) + [ANY],
        us=0.7,
    )
    other_part = partner(partner_part)
    for index, shift in enumerate(shifts):
        last = index == len(shifts) - 1
        outs, out_specs = sum(runs, []), [VMEM] * len(states)
        if last:
            outs, out_specs = [shape(prefill_queries.shape, bf16)] * 2, [VMEM, ANY]
        states = call(
            functools.partial(far_kernel, blocks, shift, last),
            (info, prefill_queries, *far[index], own_part, *states),
            outs,
            [pltpu.VMEM((prompts, 2 * length, 2 * D_HEAD), bf16), pltpu.SemaphoreType.DMA(())],
            specs=[VMEM] * 6 + [ANY] + [VMEM] * len(states),
            out_specs=out_specs,
            us=2.8,
        )
    pre, prefill_out = states
    decode_out, prefill_out = call(
        functools.partial(finish_kernel, shifts[-1], span),
        (pre, *cache, own_part, other_part, prefill_out),
        [shape(decode_queries.shape, bf16), shape(prefill_queries.shape, bf16)],
        [
            pltpu.VMEM(decode_queries.shape, bf16),
            pltpu.VMEM((span, dec_columns), f32),
            pltpu.SemaphoreType.DMA((2,)),
        ],
        specs=[VMEM] * 6 + [ANY],
        out_specs=[ANY, ANY],
        aliases={6: 1},
        us=0.7,
    )
    return prefill_out, decode_out


def solution(mesh):
    in_specs = (
        P(None, "seq", ("head", "role")),
        P(None, "seq", ("head", "role")),
        P(None, "seq", ("head", "role")),
        P(),
        P(("seq", "role")),
        P(("seq", "role")),
        P(("seq", "role"), None, "head"),
        P(("seq", "role"), None, "head"),
        P(None, ("seq", "role"), "head"),
        P(None, ("seq", "role"), "head"),
        P(None, ("seq", "role"), "head"),
    )
    out_specs = (P(None, "seq", ("head", "role")), P(None, ("seq", "role"), "head"))
    return jax.shard_map(body, mesh=mesh, in_specs=in_specs, out_specs=out_specs, check_vma=False)
```

```python
import functools
import math

import jax
import jax.numpy as jnp
from jax import lax
from jax.experimental import pallas as pl
from jax.experimental.pallas import tpu as pltpu
from jax.sharding import PartitionSpec as P

D_HEAD = 128
MASKED_SCORE = -1e30
EXP2_SCALE = D_HEAD**-0.5 * math.log2(math.e)
VMEM_BYTES = 40 * 2**20
SUM_LIMIT = 2.0**100
NT = (((1,), (1,)), ((), ()))


def scores_of(queries, keys):
    return lax.dot_general(queries, keys, NT, preferred_element_type=jnp.float32)


def weighted(weights, values):
    return jnp.dot(weights.astype(jnp.bfloat16), values, preferred_element_type=jnp.float32)


def eye_of(rows):
    shape = (rows, 128)
    return lax.broadcasted_iota(jnp.int32, shape, 0) == lax.broadcasted_iota(jnp.int32, shape, 1)


def column_to_row(column):
    spread = jnp.where(eye_of(column.shape[0]), column, 0.0)
    return jnp.sum(spread, axis=0, keepdims=True)


def row_to_column(row, rows):
    spread = jnp.where(eye_of(rows), jnp.broadcast_to(row, (rows, 128)), 0.0)
    return jnp.sum(spread, axis=1, keepdims=True)


def select_rows(index, parts):
    chosen = parts[-1]
    for number in range(len(parts) - 2, -1, -1):
        chosen = jnp.where(index == number, parts[number], chosen)
    return chosen


def lane_sum(x):
    tiles = [x[:, i : i + 128] for i in range(0, x.shape[1], 128)]
    return jnp.sum(functools.reduce(jnp.add, tiles), axis=1, keepdims=True)


def lane_max(x):
    tiles = [x[:, i : i + 128] for i in range(0, x.shape[1], 128)]
    return jnp.max(functools.reduce(jnp.maximum, tiles), axis=1, keepdims=True)


def first_kernel(_, out_ref):
    out_ref[...] = jnp.zeros_like(out_ref)


def own_kernel(
    asg_hbm, plen_hbm, clen_hbm, dq_hbm, nk_hbm, nv_hbm, ck_ref, cv_ref, _,
    own_ref, other_ref, info_ref, sum_ref, top_ref, tot_ref, asg, plen, clen, dq, nk, nv, flat, fk, fv, sems,
):
    moves = [(dq_hbm, dq), (nk_hbm, nk), (nv_hbm, nv), (asg_hbm, asg), (plen_hbm, plen), (clen_hbm, clen)]
    copies = [pltpu.make_async_copy(a, b, sems.at[i]) for i, (a, b) in enumerate(moves)]
    for copy in copies:
        copy.start()
    role = lax.axis_index("role")
    steps, rows, columns = dq.shape
    span = steps * rows
    half = columns // 2
    group = half // D_HEAD
    queries = group * span
    slots = ck_ref.shape[1]
    fk[...] = jnp.zeros_like(fk)
    fv[...] = jnp.zeros_like(fv)
    for copy in copies:
        copy.wait()
    for step in range(steps):
        at = slice(step * rows, (step + 1) * rows)
        flat[at, :] = dq[step].astype(jnp.float32)
        fk[at, :] = nk[step].astype(jnp.float32)
        fv[at, :] = nv[step].astype(jnp.float32)
    q_index = lax.broadcasted_iota(jnp.int32, (queries, 1), 0) % span
    q_step, q_row = q_index // rows, q_index % rows
    lane = lax.broadcasted_iota(jnp.int32, (queries, 128), 1)
    fresh_mask = (lane < span) & (lane % rows == q_row) & (lane // rows <= q_step)
    sides = ((own_ref, role), (other_ref, 1 - role))
    slices = [pl.ds(pl.multiple_of(kv * D_HEAD, D_HEAD), D_HEAD) for _, kv in sides]
    scores = []
    for (out, kv), cols in zip(sides, slices):
        heads = [flat[:, pl.ds(pl.multiple_of(kv * half + i * D_HEAD, D_HEAD), D_HEAD)] for i in range(group)]
        q = jnp.concatenate(heads, axis=0).astype(jnp.bfloat16)
        out[:queries, :] = q
        fresh = scores_of(q, fk[:, cols].astype(jnp.bfloat16))
        fresh = jnp.where(fresh_mask, fresh * EXP2_SCALE, MASKED_SCORE)
        scores.append((fresh, select_rows(q_row, [scores_of(q, ck_ref[r, :, cols]) for r in range(rows)])))
    row_index = lax.broadcasted_iota(jnp.int32, (span, 128), 0)
    prompt = jnp.zeros((span, 128), jnp.float32)
    for row in range(rows):
        prompt = jnp.where(row_index % rows == row, asg[row].astype(jnp.float32), prompt)
    info = jnp.zeros((span, 128), jnp.int32)
    for row in range(plen.shape[0]):
        info = jnp.where(row_index == row, plen[row], info)
    info_ref[...] = info
    limit = select_rows(q_row, [clen[r] for r in range(rows)])
    live = lax.broadcasted_iota(jnp.int32, (queries, slots), 1) < limit
    for index, ((out, _), cols, (fresh, old)) in enumerate(zip(sides, slices, scores)):
        out[queries : queries + 2 * span, :] = jnp.concatenate([prompt, prompt], axis=0).astype(jnp.bfloat16)
        old = jnp.where(live, old * EXP2_SCALE, MASKED_SCORE)
        top = jnp.maximum(lane_max(fresh), lane_max(old))
        fresh = jnp.exp2(fresh - top)
        old = jnp.exp2(old - top)
        total = lane_sum(fresh) + lane_sum(old)
        summed = weighted(fresh, fv[:, cols].astype(jnp.bfloat16))
        for r in range(rows):
            summed = summed + weighted(jnp.where(q_row == r, old, 0.0), cv_ref[r, :, cols])
        sum_ref[index] = summed
        top_ref[index] = jnp.broadcast_to(top, (queries, 128))
        tot_ref[index] = jnp.broadcast_to(total, (queries, 128))


def prompt_kernel(span, *refs):
    messages, info_ref = refs[:2], refs[2]
    chunk_refs, outs = refs[3:-3], refs[-2:]
    queries = messages[0].shape[0] - 2 * span
    seqs, seq = lax.axis_size("seq"), lax.axis_index("seq")
    prompts, length, _ = chunk_refs[0].shape
    q = jnp.concatenate([m[:queries, :] for m in messages], axis=0)
    columns = []
    for m in messages:
        eight = m[queries : queries + 2 * span, :].astype(jnp.float32)[:span, :1]
        columns += [eight] * (queries // span)
    prompt = jnp.concatenate(columns, axis=0).astype(jnp.int32)
    limit = select_rows(prompt, [jnp.broadcast_to(info_ref[r : r + 1, :1], prompt.shape) for r in range(prompts)])
    parts = []
    for index in range(seqs):
        base = (seq + seqs - 2 * (index // 2)) % seqs
        chunk = base + (index % 2) * (1 - 2 * (seq % 2))
        keys = chunk_refs[2 * index]
        position = chunk * length + lax.broadcasted_iota(jnp.int32, (q.shape[0], length), 1)
        part = select_rows(prompt, [scores_of(q, keys[r]) for r in range(prompts)])
        parts.append(jnp.where(position < limit, part * EXP2_SCALE, MASKED_SCORE))
    top = lane_max(jnp.concatenate(parts, axis=1))
    summed = jnp.zeros((q.shape[0], D_HEAD), jnp.float32)
    total = jnp.zeros((q.shape[0], 1), jnp.float32)
    for index, part in enumerate(parts):
        weights = jnp.exp2(part - top)
        total = total + lane_sum(weights)
        for r in range(prompts):
            summed = summed + weighted(jnp.where(prompt == r, weights, 0.0), chunk_refs[2 * index + 1][r])
    for index, out in enumerate(outs):
        rows = slice(index * queries, (index + 1) * queries)
        out[:queries, :] = summed[rows]
        out[queries : queries + 8, :] = jnp.concatenate(
            [column_to_row(top[rows]), column_to_row(total[rows]), jnp.zeros((6, 128), jnp.float32)], axis=0
        )


def local_kernel(blocks, q_ref, k_own, v_own, k_near, v_near, _, *refs):
    outs, wide = refs[:-1], refs[-1]
    prompts, length, _ = q_ref.shape
    seq = lax.axis_index("seq")
    for row in sorted({row for row, _, _ in blocks}):
        wide[row, :length, :D_HEAD] = v_own[row]
        wide[row, length:, :D_HEAD] = v_near[row]
        wide[row, :, D_HEAD:] = jnp.ones((2 * length, D_HEAD), jnp.bfloat16)
    causal = lax.broadcasted_iota(jnp.int32, (length, length), 1) <= lax.broadcasted_iota(
        jnp.int32, (length, length), 0
    )

    def run(with_near):
        for index, (row, start, stop) in enumerate(blocks):
            sum_ref, top_ref, tot_ref = outs[3 * index : 3 * index + 3]
            for head in range(start, stop):
                cols = slice((head - start) * D_HEAD, (head - start + 1) * D_HEAD)
                q = q_ref[row, :, head * D_HEAD : (head + 1) * D_HEAD]
                scores = jnp.where(causal, scores_of(q, k_own[row]), MASKED_SCORE)
                if with_near:
                    scores = jnp.concatenate([scores, scores_of(q, k_near[row])], axis=1)
                top = jnp.max(scores, axis=1, keepdims=True) * EXP2_SCALE
                summed = weighted(jnp.exp2(scores * EXP2_SCALE - top), wide[row, : scores.shape[1], :])
                sum_ref[:, cols] = summed[:, :D_HEAD]
                tot_ref[:, cols] = summed[:, D_HEAD:]
                top_ref[:, cols] = jnp.broadcast_to(top, (length, D_HEAD))

    @pl.when(seq % 2 == 0)
    def _():
        run(False)

    @pl.when(seq % 2 == 1)
    def _():
        run(True)


def merge_rows(span, cache, own_part, other_part, dec, flat):
    steps, rows, columns = dec.shape
    half = columns // 2
    group = half // D_HEAD
    queries = group * span
    role = lax.axis_index("role")
    for index, (part, kv) in enumerate(((own_part, role), (other_part, 1 - role))):
        top = row_to_column(part[queries : queries + 1, :], queries)
        total = row_to_column(part[queries + 1 : queries + 2, :], queries)
        cache_sum, cache_top, cache_tot = (ref[index] for ref in cache)
        high = jnp.maximum(top, cache_top)
        one, two = jnp.exp2(cache_top - high), jnp.exp2(top - high)
        result = (one * cache_sum + two * part[:queries, :]) / (one * cache_tot + two * total)
        for head in range(group):
            start = pl.multiple_of(kv * half + head * D_HEAD, D_HEAD)
            flat[:, pl.ds(start, D_HEAD)] = result[head * span : (head + 1) * span]
    for step in range(steps):
        dec[step] = flat[step * rows : (step + 1) * rows, :].astype(jnp.bfloat16)


def joined(q, keys):
    return jnp.concatenate([scores_of(q, one) for one in keys], axis=1)


def add_keys(q, keys, wide, summed, total, top):
    scores = joined(q, keys)
    new = jnp.maximum(top, jnp.max(scores, axis=1, keepdims=True) * EXP2_SCALE)
    high = jnp.concatenate([new] * (scores.shape[1] // D_HEAD), axis=1)
    far = weighted(jnp.exp2(scores * EXP2_SCALE - high), wide)
    alpha = jnp.exp2(top - new)
    return summed * alpha + far[:, :D_HEAD], total * alpha + far[:, D_HEAD:], new


def add_keys_at(q, keys, wide, summed, total, top):
    scores = joined(q, keys)
    high = jnp.concatenate([top] * (scores.shape[1] // D_HEAD), axis=1)
    far = weighted(jnp.exp2(scores * EXP2_SCALE - high), wide)
    return summed + far[:, :D_HEAD], total + far[:, D_HEAD:]


def far_kernel(blocks, shift, last, info_ref, q_ref, k_one, v_one, k_two, v_two, _, *refs):
    prompts, length, columns = q_ref.shape
    count = 3 * len(blocks)
    states, outs, (wide, sem) = refs[:count], refs[count:-2], refs[-2:]
    seq = lax.axis_index("seq")
    position = seq * length + lax.broadcasted_iota(jnp.int32, (length, D_HEAD), 0)
    places = [
        (index, row, slice(head * D_HEAD, (head + 1) * D_HEAD), slice((head - start) * D_HEAD, (head - start + 1) * D_HEAD))
        for index, (row, start, stop) in enumerate(blocks)
        for head in range(start, stop)
    ]

    def state_of(index, at):
        return (states[3 * index][:, at], states[3 * index + 2][:, at], states[3 * index + 1][:, at])

    def emit(index, row, cols, at, summed, total, top):
        if last:
            live = position < info_ref[row : row + 1, :]
            outs[0][row, :, cols] = jnp.where(live, summed / total, 0.0).astype(jnp.bfloat16)
        else:
            for ref, value in zip(outs[3 * index : 3 * index + 3], (summed, top, total)):
                ref[:, at] = value

    @pl.when(seq // 2 >= shift)
    def _():
        wide[:, :length, :D_HEAD] = v_one[...]
        wide[:, length:, :D_HEAD] = v_two[...]
        wide[:, :, D_HEAD:] = jnp.ones((prompts, 2 * length, D_HEAD), jnp.bfloat16)
        worst = jnp.zeros((8, D_HEAD), jnp.float32)
        if last:
            first_copy = pltpu.make_async_copy(outs[0].at[0], outs[1].at[0], sem)
        for index, row, cols, at in places:
            state = state_of(index, at)
            summed, total = add_keys_at(q_ref[row, :, cols], (k_one[row], k_two[row]), wide[row], *state)
            emit(index, row, cols, at, summed, total, state[2])
            if last and row == 0 and cols.stop == columns:
                first_copy.start()
            peaks = [total[i : i + 8] for i in range(0, length, 8)]
            worst = functools.reduce(jnp.maximum, [functools.reduce(jnp.maximum, peaks[i::4]) for i in range(4)], worst)

        if last:
            first_copy.wait()

        @pl.when(jnp.max(worst) > SUM_LIMIT)
        def _():
            for index, (row, start, stop) in enumerate(blocks):

                @pl.loop(0, stop - start)
                def _(head, index=index, row=row, start=start):
                    at = pl.ds(pl.multiple_of(head * D_HEAD, D_HEAD), D_HEAD)
                    cols = pl.ds(pl.multiple_of((start + head) * D_HEAD, D_HEAD), D_HEAD)
                    state = state_of(index, at)
                    new = add_keys(q_ref[row, :, cols], (k_one[row], k_two[row]), wide[row], *state)
                    emit(index, row, cols, at, *new)

            if last:
                first_copy.start()
                first_copy.wait()

    @pl.when(seq // 2 < shift)
    def _():
        for index, row, cols, at in places:
            emit(index, row, cols, at, *state_of(index, at))
        if last:
            copy = pltpu.make_async_copy(outs[0], outs[1], sem)
            copy.start()
            copy.wait()


def finish_kernel(
    shift, span, pre, cache_sum, cache_top, cache_tot, own_part, other_part, _, dec_hbm, pre_hbm, dec, flat, sems
):
    copy = pltpu.make_async_copy(pre.at[1:], pre_hbm.at[1:], sems.at[0])
    dec_copy = pltpu.make_async_copy(dec, dec_hbm, sems.at[1])
    late = lax.axis_index("seq") // 2 >= shift

    @pl.when(late)
    def _():
        copy.start()

    merge_rows(span, (cache_sum, cache_top, cache_tot), own_part, other_part, dec, flat)
    dec_copy.start()

    @pl.when(late)
    def _():
        copy.wait()

    dec_copy.wait()


VMEM = pl.BlockSpec(memory_space=pltpu.VMEM)
ANY = pl.BlockSpec(memory_space=pl.ANY)


def in_hbm(x):
    return pltpu.with_memory_space_constraint(x, pltpu.HBM)


def call(kernel, args, outs, scratch=(), specs=None, out_specs=None, aliases=None, us=1.0):
    return pl.pallas_call(
        kernel,
        out_shape=outs,
        in_specs=specs or [VMEM] * len(args),
        out_specs=out_specs or [VMEM] * len(outs),
        scratch_shapes=list(scratch),
        input_output_aliases=aliases or {},
        compiler_params=pltpu.CompilerParams(vmem_limit_bytes=VMEM_BYTES),
        cost_estimate=pl.CostEstimate(flops=int(us * 1.1e9), bytes_accessed=int(us * 3e6), transcendentals=0),
    )(*args)


def body(
    prefill_queries,
    prefill_keys,
    prefill_values,
    prompt_len,
    assignment,
    cache_len,
    cache_keys,
    cache_values,
    decode_queries,
    new_keys,
    new_values,
):
    seqs = lax.axis_size("seq")
    prompts, length, columns = prefill_queries.shape
    steps, rows, dec_columns = decode_queries.shape
    group = columns // D_HEAD
    span = steps * rows
    queries = group * span
    f32, bf16, i32 = jnp.float32, jnp.bfloat16, jnp.int32
    shape = jax.ShapeDtypeStruct
    after = lax.optimization_barrier

    def near(x):
        return lax.ppermute(x, "seq", [(i, i ^ 1) for i in range(seqs)])

    def around(x, shift):
        return lax.ppermute(x, "seq", [(i, (i + 2 * shift) % seqs) for i in range(seqs)])

    def partner(x):
        moves = [(i * 2 + r, (i ^ 1) * 2 + 1 - r) for i in range(seqs) for r in range(2)]
        return lax.ppermute(x, ("seq", "role"), moves)

    shifts = range(1, seqs // 2)
    far_keys = [around(prefill_keys, s) for s in shifts]
    far_values = [around(prefill_values, s) for s in shifts]
    (first,) = call(first_kernel, [in_hbm(prompt_len)], [shape((span, 128), f32)], specs=[ANY], us=3.0)
    own_keys, own_values, first = after((prefill_keys, prefill_values, first))
    near_keys, near_values = near(own_keys), near(own_values)
    message = shape((queries + 2 * span, 128), bf16)
    state = shape((2, queries, 128), f32)
    own_msg, other_msg, info, *cache = call(
        own_kernel,
        [in_hbm(x) for x in (assignment, prompt_len, cache_len, decode_queries, new_keys, new_values)]
        + [cache_keys, cache_values, first],
        [message] * 2 + [shape((span, 128), i32)] + [state] * 3,
        [
            pltpu.SMEM(assignment.shape, i32),
            pltpu.SMEM(prompt_len.shape, i32),
            pltpu.SMEM(cache_len.shape, i32),
            pltpu.VMEM(decode_queries.shape, bf16),
            pltpu.VMEM(new_keys.shape, bf16),
            pltpu.VMEM(new_values.shape, bf16),
            pltpu.VMEM((span, dec_columns), f32),
            pltpu.VMEM((128, 2 * D_HEAD), f32),
            pltpu.VMEM((128, 2 * D_HEAD), f32),
            pltpu.SemaphoreType.DMA((6,)),
        ],
        specs=[ANY] * 6 + [VMEM] * 2 + [ANY],
        us=1.3,
    )
    partner_msg = partner(other_msg)
    blocks = [(row, 0, group) for row in range(prompts - 1)]
    blocks += [(prompts - 1, 0, group // 2), (prompts - 1, group // 2, group)]
    runs = [[shape((length, (stop - start) * D_HEAD), f32)] * 3 for _, start, stop in blocks]

    def local(some, outs, marker):
        return call(
            functools.partial(local_kernel, some),
            (prefill_queries, prefill_keys, prefill_values, near_keys, near_values, marker),
            sum(outs, []),
            [pltpu.VMEM((prompts, 2 * length, 2 * D_HEAD), bf16)],
            specs=[VMEM] * 5 + [ANY],
            us=0.2 * sum(stop - start for _, start, stop in some),
        )

    states = local(blocks[:-1], runs[:-1], info)
    far_values, partner_msg, states = after((far_values, partner_msg, states))
    far_near_values = [near(v) for v in far_values]
    far_keys, states = after((far_keys, states))
    far_near_keys = [near(k) for k in far_keys]
    states = [*states, *local(blocks[-1:], runs[-1:], states[0])]
    far = list(zip(far_keys, far_values, far_near_keys, far_near_values))
    chunks = [prefill_keys, prefill_values, near_keys, near_values] + sum([list(four) for four in far], [])
    part = shape((queries + 8, 128), f32)
    own_part, partner_part = call(
        functools.partial(prompt_kernel, span),
        (own_msg, partner_msg, info, *chunks, states[-1]),
        [part] * 2,
        specs=[VMEM] * (3 + len(chunks)) + [ANY],
        us=0.7,
    )
    other_part = partner(partner_part)
    for index, shift in enumerate(shifts):
        last = index == len(shifts) - 1
        outs, out_specs = sum(runs, []), [VMEM] * len(states)
        if last:
            outs, out_specs = [shape(prefill_queries.shape, bf16)] * 2, [VMEM, ANY]
        states = call(
            functools.partial(far_kernel, blocks, shift, last),
            (info, prefill_queries, *far[index], own_part, *states),
            outs,
            [pltpu.VMEM((prompts, 2 * length, 2 * D_HEAD), bf16), pltpu.SemaphoreType.DMA(())],
            specs=[VMEM] * 6 + [ANY] + [VMEM] * len(states),
            out_specs=out_specs,
            us=2.8,
        )
    pre, prefill_out = states
    decode_out, prefill_out = call(
        functools.partial(finish_kernel, shifts[-1], span),
        (pre, *cache, own_part, other_part, prefill_out),
        [shape(decode_queries.shape, bf16), shape(prefill_queries.shape, bf16)],
        [
            pltpu.VMEM(decode_queries.shape, bf16),
            pltpu.VMEM((span, dec_columns), f32),
            pltpu.SemaphoreType.DMA((2,)),
        ],
        specs=[VMEM] * 6 + [ANY],
        out_specs=[ANY, ANY],
        aliases={6: 1},
        us=0.7,
    )
    return prefill_out, decode_out


def solution(mesh):
    in_specs = (
        P(None, "seq", ("head", "role")),
        P(None, "seq", ("head", "role")),
        P(None, "seq", ("head", "role")),
        P(),
        P(("seq", "role")),
        P(("seq", "role")),
        P(("seq", "role"), None, "head"),
        P(("seq", "role"), None, "head"),
        P(None, ("seq", "role"), "head"),
        P(None, ("seq", "role"), "head"),
        P(None, ("seq", "role"), "head"),
    )
    out_specs = (P(None, "seq", ("head", "role")), P(None, ("seq", "role"), "head"))
    return jax.shard_map(body, mesh=mesh, in_specs=in_specs, out_specs=out_specs, check_vma=False)
```

```python
import functools
import math

import jax
import jax.numpy as jnp
from jax import lax
from jax.experimental import pallas as pl
from jax.experimental.pallas import tpu as pltpu
from jax.sharding import PartitionSpec as P

D_HEAD = 128
MASKED_SCORE = -1e30
EXP2_SCALE = D_HEAD**-0.5 * math.log2(math.e)
VMEM_BYTES = 40 * 2**20
SUM_LIMIT = 2.0**100
NT = (((1,), (1,)), ((), ()))


def scores_of(queries, keys):
    return lax.dot_general(queries, keys, NT, preferred_element_type=jnp.float32)


def weighted(weights, values):
    return jnp.dot(weights.astype(jnp.bfloat16), values, preferred_element_type=jnp.float32)


def eye_of(rows):
    shape = (rows, 128)
    return lax.broadcasted_iota(jnp.int32, shape, 0) == lax.broadcasted_iota(jnp.int32, shape, 1)


def column_to_row(column):
    spread = jnp.where(eye_of(column.shape[0]), column, 0.0)
    return jnp.sum(spread, axis=0, keepdims=True)


def row_to_column(row, rows):
    spread = jnp.where(eye_of(rows), jnp.broadcast_to(row, (rows, 128)), 0.0)
    return jnp.sum(spread, axis=1, keepdims=True)


def terms_of(x):
    terms = []
    for _ in range(3):
        terms.append(x.astype(jnp.bfloat16).astype(jnp.float32))
        x = x - terms[-1]
    return terms


def sum_of_terms(block, first):
    return block[first : first + 1] + block[first + 1 : first + 2] + block[first + 2 : first + 3]


def select_rows(index, parts):
    chosen = parts[-1]
    for number in range(len(parts) - 2, -1, -1):
        chosen = jnp.where(index == number, parts[number], chosen)
    return chosen


def lane_sum(x):
    tiles = [x[:, i : i + 128] for i in range(0, x.shape[1], 128)]
    return jnp.sum(functools.reduce(jnp.add, tiles), axis=1, keepdims=True)


def lane_max(x):
    tiles = [x[:, i : i + 128] for i in range(0, x.shape[1], 128)]
    return jnp.max(functools.reduce(jnp.maximum, tiles), axis=1, keepdims=True)


def first_kernel(_, out_ref):
    out_ref[...] = jnp.zeros_like(out_ref)


def own_kernel(
    asg_hbm, plen_hbm, clen_hbm, dq_hbm, nk_hbm, nv_hbm, ck_ref, cv_ref, _,
    own_ref, other_ref, info_ref, sum_ref, top_ref, tot_ref, asg, plen, clen, dq, nk, nv, flat, fk, fv, sems,
):
    moves = [(dq_hbm, dq), (nk_hbm, nk), (nv_hbm, nv), (asg_hbm, asg), (plen_hbm, plen), (clen_hbm, clen)]
    copies = [pltpu.make_async_copy(a, b, sems.at[i]) for i, (a, b) in enumerate(moves)]
    for copy in copies:
        copy.start()
    role = lax.axis_index("role")
    steps, rows, columns = dq.shape
    span = steps * rows
    half = columns // 2
    group = half // D_HEAD
    queries = group * span
    slots = ck_ref.shape[1]
    fk[...] = jnp.zeros_like(fk)
    fv[...] = jnp.zeros_like(fv)
    for copy in copies:
        copy.wait()
    for step in range(steps):
        at = slice(step * rows, (step + 1) * rows)
        flat[at, :] = dq[step].astype(jnp.float32)
        fk[at, :] = nk[step].astype(jnp.float32)
        fv[at, :] = nv[step].astype(jnp.float32)
    q_index = lax.broadcasted_iota(jnp.int32, (queries, 1), 0) % span
    q_step, q_row = q_index // rows, q_index % rows
    lane = lax.broadcasted_iota(jnp.int32, (queries, 128), 1)
    fresh_mask = (lane < span) & (lane % rows == q_row) & (lane // rows <= q_step)
    sides = ((own_ref, role), (other_ref, 1 - role))
    slices = [pl.ds(pl.multiple_of(kv * D_HEAD, D_HEAD), D_HEAD) for _, kv in sides]
    scores = []
    for (out, kv), cols in zip(sides, slices):
        heads = [flat[:, pl.ds(pl.multiple_of(kv * half + i * D_HEAD, D_HEAD), D_HEAD)] for i in range(group)]
        q = jnp.concatenate(heads, axis=0).astype(jnp.bfloat16)
        out[:queries, :] = q
        fresh = scores_of(q, fk[:, cols].astype(jnp.bfloat16))
        fresh = jnp.where(fresh_mask, fresh * EXP2_SCALE, MASKED_SCORE)
        scores.append((fresh, select_rows(q_row, [scores_of(q, ck_ref[r, :, cols]) for r in range(rows)])))
    row_index = lax.broadcasted_iota(jnp.int32, (span, 128), 0)
    prompt = jnp.zeros((span, 128), jnp.float32)
    for row in range(rows):
        prompt = jnp.where(row_index % rows == row, asg[row].astype(jnp.float32), prompt)
    info = jnp.zeros((span, 128), jnp.int32)
    for row in range(plen.shape[0]):
        info = jnp.where(row_index == row, plen[row], info)
    info_ref[...] = info
    limit = select_rows(q_row, [clen[r] for r in range(rows)])
    live = lax.broadcasted_iota(jnp.int32, (queries, slots), 1) < limit
    for index, ((out, _), cols, (fresh, old)) in enumerate(zip(sides, slices, scores)):
        out[queries : queries + 2 * span, :] = jnp.concatenate([prompt, prompt], axis=0).astype(jnp.bfloat16)
        old = jnp.where(live, old * EXP2_SCALE, MASKED_SCORE)
        top = jnp.maximum(lane_max(fresh), lane_max(old))
        fresh = jnp.exp2(fresh - top)
        old = jnp.exp2(old - top)
        total = lane_sum(fresh) + lane_sum(old)
        summed = weighted(fresh, fv[:, cols].astype(jnp.bfloat16))
        for r in range(rows):
            summed = summed + weighted(jnp.where(q_row == r, old, 0.0), cv_ref[r, :, cols])
        sum_ref[index] = summed
        top_ref[index] = jnp.broadcast_to(top, (queries, 128))
        tot_ref[index] = jnp.broadcast_to(total, (queries, 128))


def prompt_kernel(span, *refs):
    messages, info_ref = refs[:2], refs[2]
    chunk_refs, outs = refs[3:-3], refs[-2:]
    queries = messages[0].shape[0] - 2 * span
    seqs, seq = lax.axis_size("seq"), lax.axis_index("seq")
    prompts, length, _ = chunk_refs[0].shape
    q = jnp.concatenate([m[:queries, :] for m in messages], axis=0)
    columns = []
    for m in messages:
        eight = m[queries : queries + 2 * span, :].astype(jnp.float32)[:span, :1]
        columns += [eight] * (queries // span)
    prompt = jnp.concatenate(columns, axis=0).astype(jnp.int32)
    limit = select_rows(prompt, [jnp.broadcast_to(info_ref[r : r + 1, :1], prompt.shape) for r in range(prompts)])
    parts = []
    for index in range(seqs):
        base = (seq + seqs - 2 * (index // 2)) % seqs
        chunk = base + (index % 2) * (1 - 2 * (seq % 2))
        keys = chunk_refs[2 * index]
        position = chunk * length + lax.broadcasted_iota(jnp.int32, (q.shape[0], length), 1)
        part = select_rows(prompt, [scores_of(q, keys[r]) for r in range(prompts)])
        parts.append(jnp.where(position < limit, part * EXP2_SCALE, MASKED_SCORE))
    top = lane_max(jnp.concatenate(parts, axis=1))
    summed = jnp.zeros((q.shape[0], D_HEAD), jnp.float32)
    total = jnp.zeros((q.shape[0], 1), jnp.float32)
    for index, part in enumerate(parts):
        weights = jnp.exp2(part - top)
        total = total + lane_sum(weights)
        for r in range(prompts):
            summed = summed + weighted(jnp.where(prompt == r, weights, 0.0), chunk_refs[2 * index + 1][r])
    for index, out in enumerate(outs):
        rows = slice(index * queries, (index + 1) * queries)
        stats = terms_of(column_to_row(top[rows])) + terms_of(column_to_row(total[rows]))
        stats = jnp.concatenate(stats + [jnp.zeros((16 - len(stats), 128), jnp.float32)], axis=0)
        out[:queries, :] = summed[rows].astype(out.dtype)
        out[queries : queries + 16, :] = stats.astype(out.dtype)


def local_kernel(blocks, q_ref, k_own, v_own, k_near, v_near, _, *refs):
    outs, wide = refs[:-1], refs[-1]
    prompts, length, _ = q_ref.shape
    seq = lax.axis_index("seq")
    for row in sorted({row for row, _, _ in blocks}):
        wide[row, :length, :D_HEAD] = v_own[row]
        wide[row, length:, :D_HEAD] = v_near[row]
        wide[row, :, D_HEAD:] = jnp.ones((2 * length, D_HEAD), jnp.bfloat16)
    causal = lax.broadcasted_iota(jnp.int32, (length, length), 1) <= lax.broadcasted_iota(
        jnp.int32, (length, length), 0
    )

    def run(with_near):
        for index, (row, start, stop) in enumerate(blocks):
            sum_ref, top_ref, tot_ref = outs[3 * index : 3 * index + 3]
            for head in range(start, stop):
                cols = slice((head - start) * D_HEAD, (head - start + 1) * D_HEAD)
                q = q_ref[row, :, head * D_HEAD : (head + 1) * D_HEAD]
                scores = jnp.where(causal, scores_of(q, k_own[row]), MASKED_SCORE)
                if with_near:
                    scores = jnp.concatenate([scores, scores_of(q, k_near[row])], axis=1)
                top = jnp.max(scores, axis=1, keepdims=True) * EXP2_SCALE
                summed = weighted(jnp.exp2(scores * EXP2_SCALE - top), wide[row, : scores.shape[1], :])
                sum_ref[:, cols] = summed[:, :D_HEAD]
                tot_ref[:, cols] = summed[:, D_HEAD:]
                top_ref[:, cols] = jnp.broadcast_to(top, (length, D_HEAD))

    @pl.when(seq % 2 == 0)
    def _():
        run(False)

    @pl.when(seq % 2 == 1)
    def _():
        run(True)


def merged(span, group, cache_sum, cache_top, cache_tot, part):
    queries = group * span
    stats = part[queries : queries + 16, :].astype(jnp.float32)
    top = row_to_column(sum_of_terms(stats, 0), queries)
    total = row_to_column(sum_of_terms(stats, 3), queries)
    high = jnp.maximum(top, cache_top)
    one, two = jnp.exp2(cache_top - high), jnp.exp2(top - high)
    result = (one * cache_sum + two * part[:queries, :].astype(jnp.float32)) / (one * cache_tot + two * total)
    return jnp.concatenate([result[head * span : (head + 1) * span] for head in range(group)], axis=1)


def joined(q, keys):
    return jnp.concatenate([scores_of(q, one) for one in keys], axis=1)


def add_keys(q, keys, wide, summed, total, top):
    scores = joined(q, keys)
    new = jnp.maximum(top, jnp.max(scores, axis=1, keepdims=True) * EXP2_SCALE)
    high = jnp.concatenate([new] * (scores.shape[1] // D_HEAD), axis=1)
    far = weighted(jnp.exp2(scores * EXP2_SCALE - high), wide)
    alpha = jnp.exp2(top - new)
    return summed * alpha + far[:, :D_HEAD], total * alpha + far[:, D_HEAD:], new


def add_keys_at(q, keys, wide, summed, total, top):
    scores = joined(q, keys)
    high = jnp.concatenate([top] * (scores.shape[1] // D_HEAD), axis=1)
    far = weighted(jnp.exp2(scores * EXP2_SCALE - high), wide)
    return summed + far[:, :D_HEAD], total + far[:, D_HEAD:]


def far_kernel(blocks, shift, last, span, info_ref, q_ref, k_one, v_one, k_two, v_two, _, *refs):
    prompts, length, columns = q_ref.shape
    group = columns // D_HEAD
    count = 3 * len(blocks)
    states, outs, (wide, sem) = refs[:count], refs[count:-2], refs[-2:]
    if last:
        (cache_sum, cache_top, cache_tot, own_part), outs = outs[:4], outs[4:]
        outs[2][...] = merged(span, group, cache_sum[0], cache_top[0], cache_tot[0], own_part)
    seq = lax.axis_index("seq")
    position = seq * length + lax.broadcasted_iota(jnp.int32, (length, D_HEAD), 0)
    places = [
        (index, row, slice(head * D_HEAD, (head + 1) * D_HEAD), slice((head - start) * D_HEAD, (head - start + 1) * D_HEAD))
        for index, (row, start, stop) in enumerate(blocks)
        for head in range(start, stop)
    ]

    def state_of(index, at):
        return (states[3 * index][:, at], states[3 * index + 2][:, at], states[3 * index + 1][:, at])

    def emit(index, row, cols, at, summed, total, top):
        if last:
            live = position < info_ref[row : row + 1, :]
            outs[0][row, :, cols] = jnp.where(live, summed / total, 0.0).astype(jnp.bfloat16)
        else:
            for ref, value in zip(outs[3 * index : 3 * index + 3], (summed, top, total)):
                ref[:, at] = value

    @pl.when(seq // 2 >= shift)
    def _():
        wide[:, :length, :D_HEAD] = v_one[...]
        wide[:, length:, :D_HEAD] = v_two[...]
        wide[:, :, D_HEAD:] = jnp.ones((prompts, 2 * length, D_HEAD), jnp.bfloat16)
        worst = jnp.zeros((8, D_HEAD), jnp.float32)
        if last:
            first_copy = pltpu.make_async_copy(outs[0].at[0], outs[1].at[0], sem)
        for index, row, cols, at in places:
            state = state_of(index, at)
            summed, total = add_keys_at(q_ref[row, :, cols], (k_one[row], k_two[row]), wide[row], *state)
            emit(index, row, cols, at, summed, total, state[2])
            if last and row == 0 and cols.stop == columns:
                first_copy.start()
            peaks = [total[i : i + 8] for i in range(0, length, 8)]
            worst = functools.reduce(jnp.maximum, [functools.reduce(jnp.maximum, peaks[i::4]) for i in range(4)], worst)

        if last:
            first_copy.wait()

        @pl.when(jnp.max(worst) > SUM_LIMIT)
        def _():
            for index, (row, start, stop) in enumerate(blocks):

                @pl.loop(0, stop - start)
                def _(head, index=index, row=row, start=start):
                    at = pl.ds(pl.multiple_of(head * D_HEAD, D_HEAD), D_HEAD)
                    cols = pl.ds(pl.multiple_of((start + head) * D_HEAD, D_HEAD), D_HEAD)
                    state = state_of(index, at)
                    new = add_keys(q_ref[row, :, cols], (k_one[row], k_two[row]), wide[row], *state)
                    emit(index, row, cols, at, *new)

            if last:
                first_copy.start()
                first_copy.wait()

    @pl.when(seq // 2 < shift)
    def _():
        for index, row, cols, at in places:
            emit(index, row, cols, at, *state_of(index, at))
        if last:
            copy = pltpu.make_async_copy(outs[0], outs[1], sem)
            copy.start()
            copy.wait()


def finish_kernel(
    shift, span, pre, own_rows, cache_sum, cache_top, cache_tot, other_part, _, dec_hbm, pre_hbm, dec, flat, sems
):
    copy = pltpu.make_async_copy(pre.at[1:], pre_hbm.at[1:], sems.at[0])
    dec_copy = pltpu.make_async_copy(dec, dec_hbm, sems.at[1])
    late = lax.axis_index("seq") // 2 >= shift
    role = lax.axis_index("role")

    @pl.when(late)
    def _():
        copy.start()

    steps, rows, columns = dec.shape
    half = columns // 2
    flat[:, pl.ds(pl.multiple_of(role * half, half), half)] = own_rows[...]
    other = merged(span, half // D_HEAD, cache_sum[1], cache_top[1], cache_tot[1], other_part)
    flat[:, pl.ds(pl.multiple_of((1 - role) * half, half), half)] = other
    for step in range(steps):
        dec[step] = flat[step * rows : (step + 1) * rows, :].astype(jnp.bfloat16)
    dec_copy.start()

    @pl.when(late)
    def _():
        copy.wait()

    dec_copy.wait()


VMEM = pl.BlockSpec(memory_space=pltpu.VMEM)
ANY = pl.BlockSpec(memory_space=pl.ANY)


def in_hbm(x):
    return pltpu.with_memory_space_constraint(x, pltpu.HBM)


def call(kernel, args, outs, scratch=(), specs=None, out_specs=None, aliases=None, us=1.0):
    return pl.pallas_call(
        kernel,
        out_shape=outs,
        in_specs=specs or [VMEM] * len(args),
        out_specs=out_specs or [VMEM] * len(outs),
        scratch_shapes=list(scratch),
        input_output_aliases=aliases or {},
        compiler_params=pltpu.CompilerParams(vmem_limit_bytes=VMEM_BYTES),
        cost_estimate=pl.CostEstimate(flops=int(us * 1.1e9), bytes_accessed=int(us * 3e6), transcendentals=0),
    )(*args)


def body(
    prefill_queries,
    prefill_keys,
    prefill_values,
    prompt_len,
    assignment,
    cache_len,
    cache_keys,
    cache_values,
    decode_queries,
    new_keys,
    new_values,
):
    seqs = lax.axis_size("seq")
    prompts, length, columns = prefill_queries.shape
    steps, rows, dec_columns = decode_queries.shape
    group = columns // D_HEAD
    span = steps * rows
    queries = group * span
    f32, bf16, i32 = jnp.float32, jnp.bfloat16, jnp.int32
    shape = jax.ShapeDtypeStruct
    after = lax.optimization_barrier

    def near(x):
        return lax.ppermute(x, "seq", [(i, i ^ 1) for i in range(seqs)])

    def around(x, shift):
        return lax.ppermute(x, "seq", [(i, (i + 2 * shift) % seqs) for i in range(seqs)])

    def partner(x):
        moves = [(i * 2 + r, (i ^ 1) * 2 + 1 - r) for i in range(seqs) for r in range(2)]
        return lax.ppermute(x, ("seq", "role"), moves)

    shifts = range(1, seqs // 2)
    far_keys = [around(prefill_keys, s) for s in shifts]
    far_values = [around(prefill_values, s) for s in shifts]
    (first,) = call(first_kernel, [in_hbm(prompt_len)], [shape((span, 128), f32)], specs=[ANY], us=3.0)
    own_keys, own_values, first = after((prefill_keys, prefill_values, first))
    near_keys, near_values = near(own_keys), near(own_values)
    message = shape((queries + 2 * span, 128), bf16)
    state = shape((2, queries, 128), f32)
    own_msg, other_msg, info, *cache = call(
        own_kernel,
        [in_hbm(x) for x in (assignment, prompt_len, cache_len, decode_queries, new_keys, new_values)]
        + [cache_keys, cache_values, first],
        [message] * 2 + [shape((span, 128), i32)] + [state] * 3,
        [
            pltpu.SMEM(assignment.shape, i32),
            pltpu.SMEM(prompt_len.shape, i32),
            pltpu.SMEM(cache_len.shape, i32),
            pltpu.VMEM(decode_queries.shape, bf16),
            pltpu.VMEM(new_keys.shape, bf16),
            pltpu.VMEM(new_values.shape, bf16),
            pltpu.VMEM((span, dec_columns), f32),
            pltpu.VMEM((128, 2 * D_HEAD), f32),
            pltpu.VMEM((128, 2 * D_HEAD), f32),
            pltpu.SemaphoreType.DMA((6,)),
        ],
        specs=[ANY] * 6 + [VMEM] * 2 + [ANY],
        us=1.3,
    )
    partner_msg = partner(other_msg)
    blocks = [(row, 0, group) for row in range(prompts - 1)]
    blocks += [(prompts - 1, 0, group // 2), (prompts - 1, group // 2, group)]
    runs = [[shape((length, (stop - start) * D_HEAD), f32)] * 3 for _, start, stop in blocks]

    def local(some, outs, marker):
        return call(
            functools.partial(local_kernel, some),
            (prefill_queries, prefill_keys, prefill_values, near_keys, near_values, marker),
            sum(outs, []),
            [pltpu.VMEM((prompts, 2 * length, 2 * D_HEAD), bf16)],
            specs=[VMEM] * 5 + [ANY],
            us=0.2 * sum(stop - start for _, start, stop in some),
        )

    states = local(blocks[:-1], runs[:-1], info)
    far_values, partner_msg, states = after((far_values, partner_msg, states))
    far_near_values = [near(v) for v in far_values]
    far_keys, states = after((far_keys, states))
    far_near_keys = [near(k) for k in far_keys]
    states = [*states, *local(blocks[-1:], runs[-1:], states[0])]
    far = list(zip(far_keys, far_values, far_near_keys, far_near_values))
    chunks = [prefill_keys, prefill_values, near_keys, near_values] + sum([list(four) for four in far], [])
    parts = [shape((queries + 16, 128), f32), shape((queries + 16, 128), bf16)]
    own_part, partner_part = call(
        functools.partial(prompt_kernel, span),
        (own_msg, partner_msg, info, *chunks, states[-1]),
        parts,
        specs=[VMEM] * (3 + len(chunks)) + [ANY],
        us=0.7,
    )
    other_part = partner(partner_part)
    for index, shift in enumerate(shifts):
        last = index == len(shifts) - 1
        outs, out_specs, extra = sum(runs, []), [VMEM] * len(states), []
        if last:
            outs = [shape(prefill_queries.shape, bf16)] * 2 + [shape((span, dec_columns // 2), f32)]
            out_specs, extra = [VMEM, ANY, VMEM], [*cache, own_part]
        states = call(
            functools.partial(far_kernel, blocks, shift, last, span),
            (info, prefill_queries, *far[index], own_part, *states, *extra),
            outs,
            [pltpu.VMEM((prompts, 2 * length, 2 * D_HEAD), bf16), pltpu.SemaphoreType.DMA(())],
            specs=[VMEM] * 6 + [ANY] + [VMEM] * (len(states) + len(extra)),
            out_specs=out_specs,
            us=2.8,
        )
    pre, prefill_out, own_rows = states
    decode_out, prefill_out = call(
        functools.partial(finish_kernel, shifts[-1], span),
        (pre, own_rows, *cache, other_part, prefill_out),
        [shape(decode_queries.shape, bf16), shape(prefill_queries.shape, bf16)],
        [
            pltpu.VMEM(decode_queries.shape, bf16),
            pltpu.VMEM((span, dec_columns), f32),
            pltpu.SemaphoreType.DMA((2,)),
        ],
        specs=[VMEM] * 6 + [ANY],
        out_specs=[ANY, ANY],
        aliases={6: 1},
        us=0.7,
    )
    return prefill_out, decode_out


def solution(mesh):
    in_specs = (
        P(None, "seq", ("head", "role")),
        P(None, "seq", ("head", "role")),
        P(None, "seq", ("head", "role")),
        P(),
        P(("seq", "role")),
        P(("seq", "role")),
        P(("seq", "role"), None, "head"),
        P(("seq", "role"), None, "head"),
        P(None, ("seq", "role"), "head"),
        P(None, ("seq", "role"), "head"),
        P(None, ("seq", "role"), "head"),
    )
    out_specs = (P(None, "seq", ("head", "role")), P(None, ("seq", "role"), "head"))
    return jax.shard_map(body, mesh=mesh, in_specs=in_specs, out_specs=out_specs, check_vma=False)
```

```python
import functools
import math

import jax
import jax.numpy as jnp
from jax import lax
from jax.experimental import pallas as pl
from jax.experimental.pallas import tpu as pltpu
from jax.sharding import PartitionSpec as P

D_HEAD = 128
MASKED_SCORE = -1e30
EXP2_SCALE = D_HEAD**-0.5 * math.log2(math.e)
VMEM_BYTES = 40 * 2**20
SUM_LIMIT = 2.0**100
NT = (((1,), (1,)), ((), ()))


def scores_of(queries, keys):
    return lax.dot_general(queries, keys, NT, preferred_element_type=jnp.float32)


def weighted(weights, values):
    return jnp.dot(weights.astype(jnp.bfloat16), values, preferred_element_type=jnp.float32)


def eye_of(rows):
    shape = (rows, 128)
    return lax.broadcasted_iota(jnp.int32, shape, 0) == lax.broadcasted_iota(jnp.int32, shape, 1)


def column_to_row(column):
    spread = jnp.where(eye_of(column.shape[0]), column, 0.0)
    return jnp.sum(spread, axis=0, keepdims=True)


def row_to_column(row, rows):
    spread = jnp.where(eye_of(rows), jnp.broadcast_to(row, (rows, 128)), 0.0)
    return jnp.sum(spread, axis=1, keepdims=True)


def terms_of(x):
    terms = []
    for _ in range(3):
        terms.append(x.astype(jnp.bfloat16).astype(jnp.float32))
        x = x - terms[-1]
    return terms


def sum_of_terms(block, first):
    return block[first : first + 1] + block[first + 1 : first + 2] + block[first + 2 : first + 3]


def select_rows(index, parts):
    chosen = parts[-1]
    for number in range(len(parts) - 2, -1, -1):
        chosen = jnp.where(index == number, parts[number], chosen)
    return chosen


def lane_sum(x):
    tiles = [x[:, i : i + 128] for i in range(0, x.shape[1], 128)]
    return jnp.sum(functools.reduce(jnp.add, tiles), axis=1, keepdims=True)


def lane_max(x):
    tiles = [x[:, i : i + 128] for i in range(0, x.shape[1], 128)]
    return jnp.max(functools.reduce(jnp.maximum, tiles), axis=1, keepdims=True)


def first_kernel(_, out_ref):
    out_ref[...] = jnp.zeros_like(out_ref)


def own_kernel(
    asg_hbm, plen_hbm, clen_hbm, dq_hbm, nk_hbm, nv_hbm, ck_ref, cv_ref, _,
    own_ref, other_ref, info_ref, sum_ref, top_ref, tot_ref, asg, plen, clen, dq, nk, nv, flat, fk, fv, sems,
):
    moves = [(dq_hbm, dq), (nk_hbm, nk), (nv_hbm, nv), (asg_hbm, asg), (plen_hbm, plen), (clen_hbm, clen)]
    copies = [pltpu.make_async_copy(a, b, sems.at[i]) for i, (a, b) in enumerate(moves)]
    for copy in copies:
        copy.start()
    role = lax.axis_index("role")
    steps, rows, columns = dq.shape
    span = steps * rows
    half = columns // 2
    group = half // D_HEAD
    queries = group * span
    slots = ck_ref.shape[1]
    fk[...] = jnp.zeros_like(fk)
    fv[...] = jnp.zeros_like(fv)
    for copy in copies:
        copy.wait()
    for step in range(steps):
        at = slice(step * rows, (step + 1) * rows)
        flat[at, :] = dq[step].astype(jnp.float32)
        fk[at, :] = nk[step].astype(jnp.float32)
        fv[at, :] = nv[step].astype(jnp.float32)
    q_index = lax.broadcasted_iota(jnp.int32, (queries, 1), 0) % span
    q_step, q_row = q_index // rows, q_index % rows
    lane = lax.broadcasted_iota(jnp.int32, (queries, 128), 1)
    fresh_mask = (lane < span) & (lane % rows == q_row) & (lane // rows <= q_step)
    sides = ((own_ref, role), (other_ref, 1 - role))
    slices = [pl.ds(pl.multiple_of(kv * D_HEAD, D_HEAD), D_HEAD) for _, kv in sides]
    scores = []
    for (out, kv), cols in zip(sides, slices):
        heads = [flat[:, pl.ds(pl.multiple_of(kv * half + i * D_HEAD, D_HEAD), D_HEAD)] for i in range(group)]
        q = jnp.concatenate(heads, axis=0).astype(jnp.bfloat16)
        out[:queries, :] = q
        fresh = scores_of(q, fk[:, cols].astype(jnp.bfloat16))
        fresh = jnp.where(fresh_mask, fresh * EXP2_SCALE, MASKED_SCORE)
        scores.append((fresh, select_rows(q_row, [scores_of(q, ck_ref[r, :, cols]) for r in range(rows)])))
    row_index = lax.broadcasted_iota(jnp.int32, (span, 128), 0)
    prompt = jnp.zeros((span, 128), jnp.float32)
    for row in range(rows):
        prompt = jnp.where(row_index % rows == row, asg[row].astype(jnp.float32), prompt)
    info = jnp.zeros((span, 128), jnp.int32)
    for row in range(plen.shape[0]):
        info = jnp.where(row_index == row, plen[row], info)
    info_ref[...] = info
    limit = select_rows(q_row, [clen[r] for r in range(rows)])
    live = lax.broadcasted_iota(jnp.int32, (queries, slots), 1) < limit
    for index, ((out, _), cols, (fresh, old)) in enumerate(zip(sides, slices, scores)):
        out[queries : queries + 2 * span, :] = jnp.concatenate([prompt, prompt], axis=0).astype(jnp.bfloat16)
        old = jnp.where(live, old * EXP2_SCALE, MASKED_SCORE)
        top = jnp.maximum(lane_max(fresh), lane_max(old))
        fresh = jnp.exp2(fresh - top)
        old = jnp.exp2(old - top)
        total = lane_sum(fresh) + lane_sum(old)
        summed = weighted(fresh, fv[:, cols].astype(jnp.bfloat16))
        for r in range(rows):
            summed = summed + weighted(jnp.where(q_row == r, old, 0.0), cv_ref[r, :, cols])
        sum_ref[index] = summed
        top_ref[index] = jnp.broadcast_to(top, (queries, 128))
        tot_ref[index] = jnp.broadcast_to(total, (queries, 128))


def prompt_kernel(span, *refs):
    messages, info_ref = refs[:2], refs[2]
    chunk_refs, outs = refs[3:-3], refs[-2:]
    queries = messages[0].shape[0] - 2 * span
    seqs, seq = lax.axis_size("seq"), lax.axis_index("seq")
    prompts, length, _ = chunk_refs[0].shape
    q = jnp.concatenate([m[:queries, :] for m in messages], axis=0)
    columns = []
    for m in messages:
        eight = m[queries : queries + 2 * span, :].astype(jnp.float32)[:span, :1]
        columns += [eight] * (queries // span)
    prompt = jnp.concatenate(columns, axis=0).astype(jnp.int32)
    limit = select_rows(prompt, [jnp.broadcast_to(info_ref[r : r + 1, :1], prompt.shape) for r in range(prompts)])
    parts = []
    for index in range(seqs):
        base = (seq + seqs - 2 * (index // 2)) % seqs
        chunk = base + (index % 2) * (1 - 2 * (seq % 2))
        keys = chunk_refs[2 * index]
        position = chunk * length + lax.broadcasted_iota(jnp.int32, (q.shape[0], length), 1)
        part = select_rows(prompt, [scores_of(q, keys[r]) for r in range(prompts)])
        parts.append(jnp.where(position < limit, part * EXP2_SCALE, MASKED_SCORE))
    top = lane_max(jnp.concatenate(parts, axis=1))
    summed = jnp.zeros((q.shape[0], D_HEAD), jnp.float32)
    total = jnp.zeros((q.shape[0], 1), jnp.float32)
    for index, part in enumerate(parts):
        weights = jnp.exp2(part - top)
        total = total + lane_sum(weights)
        for r in range(prompts):
            summed = summed + weighted(jnp.where(prompt == r, weights, 0.0), chunk_refs[2 * index + 1][r])
    for index, out in enumerate(outs):
        rows = slice(index * queries, (index + 1) * queries)
        stats = terms_of(column_to_row(top[rows])) + terms_of(column_to_row(total[rows]))
        stats = jnp.concatenate(stats + [jnp.zeros((16 - len(stats), 128), jnp.float32)], axis=0)
        out[:queries, :] = summed[rows].astype(out.dtype)
        out[queries : queries + 16, :] = stats.astype(out.dtype)


def local_heads(block, with_near, q_ref, k_own, k_near, wide, outs):
    row, start, stop = block
    length = q_ref.shape[1]
    sum_ref, top_ref, tot_ref = outs
    causal = lax.broadcasted_iota(jnp.int32, (length, length), 1) <= lax.broadcasted_iota(
        jnp.int32, (length, length), 0
    )
    for head in range(start, stop):
        cols = slice((head - start) * D_HEAD, (head - start + 1) * D_HEAD)
        q = q_ref[row, :, head * D_HEAD : (head + 1) * D_HEAD]
        scores = jnp.where(causal, scores_of(q, k_own[row]), MASKED_SCORE)
        if with_near:
            scores = jnp.concatenate([scores, scores_of(q, k_near[row])], axis=1)
        top = jnp.max(scores, axis=1, keepdims=True) * EXP2_SCALE
        summed = weighted(jnp.exp2(scores * EXP2_SCALE - top), wide[row, : scores.shape[1], :])
        sum_ref[:, cols] = summed[:, :D_HEAD]
        tot_ref[:, cols] = summed[:, D_HEAD:]
        top_ref[:, cols] = jnp.broadcast_to(top, (length, D_HEAD))


def widen(rows, v_one, v_two, wide):
    length = v_one.shape[1]
    for row in rows:
        wide[row, :length, :D_HEAD] = v_one[row]
        wide[row, length:, :D_HEAD] = v_two[row]
        wide[row, :, D_HEAD:] = jnp.ones((2 * length, D_HEAD), jnp.bfloat16)


def local_kernel(blocks, shift, q_ref, k_own, v_own, k_near, v_near, _, *refs):
    outs, wide = refs[:-1], refs[-1]
    prompts = q_ref.shape[0]
    seq = lax.axis_index("seq")
    widen(range(prompts), v_own, v_near, wide)

    def run(some, with_near):
        for index in some:
            local_heads(blocks[index], with_near, q_ref, k_own, k_near, wide, outs[3 * index : 3 * index + 3])

    for core in range(2):

        @pl.when(seq % 2 == core)
        def _(core=core):
            run(range(len(blocks) - 1), core == 1)

            @pl.when(seq // 2 >= shift)
            def _():
                run([len(blocks) - 1], core == 1)


def window_kernel(blocks, shift, keep, q_ref, k_own, v_own, k_near, v_near, k_one, v_one, _, *refs):
    first_in, last_in, first_out, last_out = (refs[3 * i : 3 * i + 3] for i in range(4))
    wide = refs[-1]
    seq = lax.axis_index("seq")
    length = q_ref.shape[1]
    late = seq // 2 >= shift

    def emit(index, row, cols, at, summed, total, top):
        for ref, value in zip(first_out, (summed, top, total)):
            ref[:, at] = value

    @pl.when(late)
    def _():
        widen([0], v_one, v_one, wide)
        add_blocks([(0, *blocks[0])], lambda row: ([k_one[row]], wide[row, :length]), q_ref, first_in, emit)
        if keep:
            for ref, value in zip(last_out, last_in):
                ref[...] = value[...]

    @pl.when(jnp.logical_not(late))
    def _():
        widen([blocks[-1][0]], v_own, v_near, wide)
        for core in range(2):

            @pl.when(seq % 2 == core)
            def _(core=core):
                local_heads(blocks[-1], core == 1, q_ref, k_own, k_near, wide, last_out)

        if keep:
            for ref, value in zip(first_out, first_in):
                ref[...] = value[...]


def merged(span, group, cache_sum, cache_top, cache_tot, part):
    queries = group * span
    stats = part[queries : queries + 16, :].astype(jnp.float32)
    top = row_to_column(sum_of_terms(stats, 0), queries)
    total = row_to_column(sum_of_terms(stats, 3), queries)
    high = jnp.maximum(top, cache_top)
    one, two = jnp.exp2(cache_top - high), jnp.exp2(top - high)
    result = (one * cache_sum + two * part[:queries, :].astype(jnp.float32)) / (one * cache_tot + two * total)
    return jnp.concatenate([result[head * span : (head + 1) * span] for head in range(group)], axis=1)


def joined(q, keys):
    return jnp.concatenate([scores_of(q, one) for one in keys], axis=1)


def add_keys(q, keys, wide, summed, total, top):
    scores = joined(q, keys)
    new = jnp.maximum(top, jnp.max(scores, axis=1, keepdims=True) * EXP2_SCALE)
    high = jnp.concatenate([new] * (scores.shape[1] // D_HEAD), axis=1)
    far = weighted(jnp.exp2(scores * EXP2_SCALE - high), wide)
    alpha = jnp.exp2(top - new)
    return summed * alpha + far[:, :D_HEAD], total * alpha + far[:, D_HEAD:], new


def add_keys_at(q, keys, wide, summed, total, top):
    scores = joined(q, keys)
    high = jnp.concatenate([top] * (scores.shape[1] // D_HEAD), axis=1)
    far = weighted(jnp.exp2(scores * EXP2_SCALE - high), wide)
    return summed + far[:, :D_HEAD], total + far[:, D_HEAD:]


def add_blocks(blocks, far_of, q_ref, states, emit, row_done=None, before=None, after=None):
    length = q_ref.shape[1]

    def state_of(index, at):
        return (states[3 * index][:, at], states[3 * index + 2][:, at], states[3 * index + 1][:, at])

    worst = jnp.zeros((8, D_HEAD), jnp.float32)
    for index, row, start, stop in blocks:
        for head in range(start, stop):
            cols = slice(head * D_HEAD, (head + 1) * D_HEAD)
            at = slice((head - start) * D_HEAD, (head - start + 1) * D_HEAD)
            state = state_of(index, at)
            summed, total = add_keys_at(q_ref[row, :, cols], *far_of(row), *state)
            emit(index, row, cols, at, summed, total, state[2])
            if row_done and cols.stop == q_ref.shape[2]:
                row_done(row)
            peaks = [total[i : i + 8] for i in range(0, length, 8)]
            worst = functools.reduce(jnp.maximum, [functools.reduce(jnp.maximum, peaks[i::4]) for i in range(4)], worst)

    if before:
        before()

    @pl.when(jnp.max(worst) > SUM_LIMIT)
    def _():
        for index, row, start, stop in blocks:

            @pl.loop(0, stop - start)
            def _(head, index=index, row=row, start=start):
                at = pl.ds(pl.multiple_of(head * D_HEAD, D_HEAD), D_HEAD)
                cols = pl.ds(pl.multiple_of((start + head) * D_HEAD, D_HEAD), D_HEAD)
                new = add_keys(q_ref[row, :, cols], *far_of(row), *state_of(index, at))
                emit(index, row, cols, at, *new)

        if after:
            after()


def far_kernel(blocks, chosen, shift, last, span, info_ref, q_ref, k_one, v_one, k_two, v_two, _, *refs):
    _, length, columns = q_ref.shape
    group = columns // D_HEAD
    count = 3 * len(blocks)
    states, others, outs, (wide, sem) = refs[:count], refs[count : 2 * count], refs[2 * count : -2], refs[-2:]
    if last:
        (cache_sum, cache_top, cache_tot, own_part), outs = outs[:4], outs[4:]
        outs[2][...] = merged(span, group, cache_sum[0], cache_top[0], cache_tot[0], own_part)
    seq = lax.axis_index("seq")
    position = seq * length + lax.broadcasted_iota(jnp.int32, (length, D_HEAD), 0)
    places = [(index, *block) for index, block in enumerate(blocks)]

    def far_of(row):
        first, stop = chosen[row][0] * length, (chosen[row][-1] + 1) * length
        return [(k_one, k_two)[i][row] for i in chosen[row]], wide[row, first:stop]

    def emit(index, row, cols, at, summed, total, top):
        if last:
            live = position < info_ref[row : row + 1, :]
            outs[0][row, :, cols] = jnp.where(live, summed / total, 0.0).astype(jnp.bfloat16)
        else:
            for ref, value in zip(outs[3 * index : 3 * index + 3], (summed, top, total)):
                ref[:, at] = value

    hooks = {}
    if last:
        first_copy = pltpu.make_async_copy(outs[0].at[0], outs[1].at[0], sem)

        def row_done(row):
            if row == 0:
                first_copy.start()

        def after():
            first_copy.start()
            first_copy.wait()

        hooks = {"row_done": row_done, "before": first_copy.wait, "after": after}

    @pl.when(seq // 2 >= shift)
    def _():
        widen(range(q_ref.shape[0]), v_one, v_two, wide)
        add_blocks(places, far_of, q_ref, states, emit, **hooks)

    @pl.when(seq // 2 < shift)
    def _():
        for index, row, start, stop in places:

            @pl.loop(0, stop - start)
            def _(head, index=index, row=row, start=start):
                at = pl.ds(pl.multiple_of(head * D_HEAD, D_HEAD), D_HEAD)
                cols = pl.ds(pl.multiple_of((start + head) * D_HEAD, D_HEAD), D_HEAD)
                kept = others[3 * index : 3 * index + 3]
                emit(index, row, cols, at, kept[0][:, at], kept[2][:, at], kept[1][:, at])

        if last:
            copy = pltpu.make_async_copy(outs[0], outs[1], sem)
            copy.start()
            copy.wait()


def finish_kernel(
    shift, span, pre, own_rows, cache_sum, cache_top, cache_tot, other_part, _, dec_hbm, pre_hbm, dec, flat, sems
):
    copy = pltpu.make_async_copy(pre.at[1:], pre_hbm.at[1:], sems.at[0])
    dec_copy = pltpu.make_async_copy(dec, dec_hbm, sems.at[1])
    late = lax.axis_index("seq") // 2 >= shift
    role = lax.axis_index("role")

    @pl.when(late)
    def _():
        copy.start()

    steps, rows, columns = dec.shape
    half = columns // 2
    flat[:, pl.ds(pl.multiple_of(role * half, half), half)] = own_rows[...]
    other = merged(span, half // D_HEAD, cache_sum[1], cache_top[1], cache_tot[1], other_part)
    flat[:, pl.ds(pl.multiple_of((1 - role) * half, half), half)] = other
    for step in range(steps):
        dec[step] = flat[step * rows : (step + 1) * rows, :].astype(jnp.bfloat16)
    dec_copy.start()

    @pl.when(late)
    def _():
        copy.wait()

    dec_copy.wait()


VMEM = pl.BlockSpec(memory_space=pltpu.VMEM)
ANY = pl.BlockSpec(memory_space=pl.ANY)


def in_hbm(x):
    return pltpu.with_memory_space_constraint(x, pltpu.HBM)


def call(kernel, args, outs, scratch=(), specs=None, out_specs=None, aliases=None, us=1.0):
    return pl.pallas_call(
        kernel,
        out_shape=outs,
        in_specs=specs or [VMEM] * len(args),
        out_specs=out_specs or [VMEM] * len(outs),
        scratch_shapes=list(scratch),
        input_output_aliases=aliases or {},
        compiler_params=pltpu.CompilerParams(vmem_limit_bytes=VMEM_BYTES),
        cost_estimate=pl.CostEstimate(flops=int(us * 1.1e9), bytes_accessed=int(us * 3e6), transcendentals=0),
    )(*args)


def body(
    prefill_queries,
    prefill_keys,
    prefill_values,
    prompt_len,
    assignment,
    cache_len,
    cache_keys,
    cache_values,
    decode_queries,
    new_keys,
    new_values,
):
    seqs = lax.axis_size("seq")
    prompts, length, columns = prefill_queries.shape
    steps, rows, dec_columns = decode_queries.shape
    group = columns // D_HEAD
    span = steps * rows
    queries = group * span
    f32, bf16, i32 = jnp.float32, jnp.bfloat16, jnp.int32
    shape = jax.ShapeDtypeStruct
    after = lax.optimization_barrier

    def near(x):
        return lax.ppermute(x, "seq", [(i, i ^ 1) for i in range(seqs)])

    def around(x, shift):
        return lax.ppermute(x, "seq", [(i, (i + 2 * shift) % seqs) for i in range(seqs)])

    def partner(x):
        moves = [(i * 2 + r, (i ^ 1) * 2 + 1 - r) for i in range(seqs) for r in range(2)]
        return lax.ppermute(x, ("seq", "role"), moves)

    shifts = range(1, seqs // 2)
    far_keys = [around(prefill_keys, s) for s in shifts]
    far_values = [around(prefill_values, s) for s in shifts]
    (first,) = call(first_kernel, [in_hbm(prompt_len)], [shape((span, 128), f32)], specs=[ANY], us=3.0)
    own_keys, own_values, first = after((prefill_keys, prefill_values, first))
    near_keys, near_values = near(own_keys), near(own_values)
    message = shape((queries + 2 * span, 128), bf16)
    state = shape((2, queries, 128), f32)
    own_msg, other_msg, info, *cache = call(
        own_kernel,
        [in_hbm(x) for x in (assignment, prompt_len, cache_len, decode_queries, new_keys, new_values)]
        + [cache_keys, cache_values, first],
        [message] * 2 + [shape((span, 128), i32)] + [state] * 3,
        [
            pltpu.SMEM(assignment.shape, i32),
            pltpu.SMEM(prompt_len.shape, i32),
            pltpu.SMEM(cache_len.shape, i32),
            pltpu.VMEM(decode_queries.shape, bf16),
            pltpu.VMEM(new_keys.shape, bf16),
            pltpu.VMEM(new_values.shape, bf16),
            pltpu.VMEM((span, dec_columns), f32),
            pltpu.VMEM((128, 2 * D_HEAD), f32),
            pltpu.VMEM((128, 2 * D_HEAD), f32),
            pltpu.SemaphoreType.DMA((6,)),
        ],
        specs=[ANY] * 6 + [VMEM] * 2 + [ANY],
        us=1.3,
    )
    partner_msg = partner(other_msg)
    blocks = [(row, 0, group) for row in range(prompts - 1)]
    blocks += [(prompts - 1, 0, group // 2), (prompts - 1, group // 2, group)]
    runs = [[shape((length, (stop - start) * D_HEAD), f32)] * 3 for _, start, stop in blocks]

    last_shift = shifts[-1]
    wide = pltpu.VMEM((prompts, 2 * length, 2 * D_HEAD), bf16)
    mine = (prefill_queries, prefill_keys, prefill_values, near_keys, near_values)
    states = call(
        functools.partial(local_kernel, blocks, last_shift),
        (*mine, info),
        sum(runs, []),
        [wide],
        specs=[VMEM] * 5 + [ANY],
        us=2.6,
    )
    far_values, partner_msg, states = after((far_values, partner_msg, states))
    far_near_values = [near(v) for v in far_values]
    far_keys, states = after((far_keys, states))
    far_near_keys = [near(k) for k in far_keys]
    keep = len(shifts) > 1
    window = call(
        functools.partial(window_kernel, blocks, last_shift, keep),
        (*mine, far_keys[-1], far_values[-1], info, *states[:3], *states[-3:]),
        runs[0] + runs[-1],
        [wide],
        specs=[VMEM] * 7 + [ANY] + [VMEM] * 6,
        us=1.0,
    )
    others = [*states[:-3], *window[3:]]
    states = [*window[:3], *states[3:]]
    if keep:
        states = others = [*window[:3], *states[3:-3], *window[3:]]
    far = list(zip(far_keys, far_values, far_near_keys, far_near_values))
    chunks = [prefill_keys, prefill_values, near_keys, near_values] + sum([list(four) for four in far], [])
    parts = [shape((queries + 16, 128), f32), shape((queries + 16, 128), bf16)]
    own_part, partner_part = call(
        functools.partial(prompt_kernel, span),
        (own_msg, partner_msg, info, *chunks, window[0]),
        parts,
        specs=[VMEM] * (3 + len(chunks)) + [ANY],
        us=0.7,
    )
    other_part = partner(partner_part)
    for index, shift in enumerate(shifts):
        last = index == len(shifts) - 1
        chosen = {row: (1,) if last and row == 0 else (0, 1) for row in range(prompts)}
        outs, out_specs, extra = sum(runs, []), [VMEM] * len(states), []
        if last:
            outs = [shape(prefill_queries.shape, bf16)] * 2 + [shape((span, dec_columns // 2), f32)]
            out_specs, extra = [VMEM, ANY, VMEM], [*cache, own_part]
        states = others = call(
            functools.partial(far_kernel, blocks, chosen, shift, last, span),
            (info, prefill_queries, *far[index], own_part, *states, *others, *extra),
            outs,
            [wide, pltpu.SemaphoreType.DMA(())],
            specs=[VMEM] * 6 + [ANY] + [VMEM] * (2 * len(states) + len(extra)),
            out_specs=out_specs,
            us=2.4,
        )
    pre, prefill_out, own_rows = states
    decode_out, prefill_out = call(
        functools.partial(finish_kernel, shifts[-1], span),
        (pre, own_rows, *cache, other_part, prefill_out),
        [shape(decode_queries.shape, bf16), shape(prefill_queries.shape, bf16)],
        [
            pltpu.VMEM(decode_queries.shape, bf16),
            pltpu.VMEM((span, dec_columns), f32),
            pltpu.SemaphoreType.DMA((2,)),
        ],
        specs=[VMEM] * 6 + [ANY],
        out_specs=[ANY, ANY],
        aliases={6: 1},
        us=0.7,
    )
    return prefill_out, decode_out


def solution(mesh):
    in_specs = (
        P(None, "seq", ("head", "role")),
        P(None, "seq", ("head", "role")),
        P(None, "seq", ("head", "role")),
        P(),
        P(("seq", "role")),
        P(("seq", "role")),
        P(("seq", "role"), None, "head"),
        P(("seq", "role"), None, "head"),
        P(None, ("seq", "role"), "head"),
        P(None, ("seq", "role"), "head"),
        P(None, ("seq", "role"), "head"),
    )
    out_specs = (P(None, "seq", ("head", "role")), P(None, ("seq", "role"), "head"))
    return jax.shard_map(body, mesh=mesh, in_specs=in_specs, out_specs=out_specs, check_vma=False)
```

```python
import functools
import math

import jax
import jax.numpy as jnp
from jax import lax
from jax.experimental import pallas as pl
from jax.experimental.pallas import tpu as pltpu
from jax.sharding import PartitionSpec as P

D_HEAD = 128
MASKED_SCORE = -1e30
EXP2_SCALE = D_HEAD**-0.5 * math.log2(math.e)
VMEM_BYTES = 40 * 2**20
SUM_LIMIT = 2.0**100
NT = (((1,), (1,)), ((), ()))


def scores_of(queries, keys):
    return lax.dot_general(queries, keys, NT, preferred_element_type=jnp.float32)


def weighted(weights, values):
    return jnp.dot(weights.astype(jnp.bfloat16), values, preferred_element_type=jnp.float32)


def eye_of(rows):
    shape = (rows, 128)
    return lax.broadcasted_iota(jnp.int32, shape, 0) == lax.broadcasted_iota(jnp.int32, shape, 1)


def column_to_row(column):
    spread = jnp.where(eye_of(column.shape[0]), column, 0.0)
    return jnp.sum(spread, axis=0, keepdims=True)


def row_to_column(row, rows):
    spread = jnp.where(eye_of(rows), jnp.broadcast_to(row, (rows, 128)), 0.0)
    return jnp.sum(spread, axis=1, keepdims=True)


def terms_of(x):
    terms = []
    for _ in range(3):
        terms.append(x.astype(jnp.bfloat16).astype(jnp.float32))
        x = x - terms[-1]
    return terms


def sum_of_terms(block, first):
    return block[first : first + 1] + block[first + 1 : first + 2] + block[first + 2 : first + 3]


def select_rows(index, parts):
    chosen = parts[-1]
    for number in range(len(parts) - 2, -1, -1):
        chosen = jnp.where(index == number, parts[number], chosen)
    return chosen


def lane_sum(x):
    tiles = [x[:, i : i + 128] for i in range(0, x.shape[1], 128)]
    return jnp.sum(functools.reduce(jnp.add, tiles), axis=1, keepdims=True)


def lane_max(x):
    tiles = [x[:, i : i + 128] for i in range(0, x.shape[1], 128)]
    return jnp.max(functools.reduce(jnp.maximum, tiles), axis=1, keepdims=True)


def first_kernel(_, out_ref):
    out_ref[...] = jnp.zeros_like(out_ref)


def own_kernel(
    asg_hbm, plen_hbm, clen_hbm, dq_hbm, nk_hbm, nv_hbm, ck_ref, cv_ref, _,
    own_ref, other_ref, info_ref, sum_ref, top_ref, tot_ref, asg, plen, clen, dq, nk, nv, flat, fk, fv, sems,
):
    moves = [(dq_hbm, dq), (nk_hbm, nk), (nv_hbm, nv), (asg_hbm, asg), (plen_hbm, plen), (clen_hbm, clen)]
    copies = [pltpu.make_async_copy(a, b, sems.at[i]) for i, (a, b) in enumerate(moves)]
    for copy in copies:
        copy.start()
    role = lax.axis_index("role")
    steps, rows, columns = dq.shape
    span = steps * rows
    half = columns // 2
    group = half // D_HEAD
    queries = group * span
    slots = ck_ref.shape[1]
    fk[...] = jnp.zeros_like(fk)
    fv[...] = jnp.zeros_like(fv)
    for copy in copies:
        copy.wait()
    for step in range(steps):
        at = slice(step * rows, (step + 1) * rows)
        flat[at, :] = dq[step].astype(jnp.float32)
        fk[at, :] = nk[step].astype(jnp.float32)
        fv[at, :] = nv[step].astype(jnp.float32)
    q_index = lax.broadcasted_iota(jnp.int32, (queries, 1), 0) % span
    q_step, q_row = q_index // rows, q_index % rows
    lane = lax.broadcasted_iota(jnp.int32, (queries, 128), 1)
    fresh_mask = (lane < span) & (lane % rows == q_row) & (lane // rows <= q_step)
    sides = ((own_ref, role), (other_ref, 1 - role))
    slices = [pl.ds(pl.multiple_of(kv * D_HEAD, D_HEAD), D_HEAD) for _, kv in sides]
    scores = []
    for (out, kv), cols in zip(sides, slices):
        heads = [flat[:, pl.ds(pl.multiple_of(kv * half + i * D_HEAD, D_HEAD), D_HEAD)] for i in range(group)]
        q = jnp.concatenate(heads, axis=0).astype(jnp.bfloat16)
        out[:queries, :] = q
        fresh = scores_of(q, fk[:, cols].astype(jnp.bfloat16))
        fresh = jnp.where(fresh_mask, fresh * EXP2_SCALE, MASKED_SCORE)
        scores.append((fresh, select_rows(q_row, [scores_of(q, ck_ref[r, :, cols]) for r in range(rows)])))
    row_index = lax.broadcasted_iota(jnp.int32, (span, 128), 0)
    prompt = jnp.zeros((span, 128), jnp.float32)
    for row in range(rows):
        prompt = jnp.where(row_index % rows == row, asg[row].astype(jnp.float32), prompt)
    info = jnp.zeros((span, 128), jnp.int32)
    for row in range(plen.shape[0]):
        info = jnp.where(row_index == row, plen[row], info)
    info_ref[...] = info
    limit = select_rows(q_row, [clen[r] for r in range(rows)])
    live = lax.broadcasted_iota(jnp.int32, (queries, slots), 1) < limit
    for index, ((out, _), cols, (fresh, old)) in enumerate(zip(sides, slices, scores)):
        out[queries : queries + 2 * span, :] = jnp.concatenate([prompt, prompt], axis=0).astype(jnp.bfloat16)
        old = jnp.where(live, old * EXP2_SCALE, MASKED_SCORE)
        top = jnp.maximum(lane_max(fresh), lane_max(old))
        fresh = jnp.exp2(fresh - top)
        old = jnp.exp2(old - top)
        total = lane_sum(fresh) + lane_sum(old)
        summed = weighted(fresh, fv[:, cols].astype(jnp.bfloat16))
        for r in range(rows):
            summed = summed + weighted(jnp.where(q_row == r, old, 0.0), cv_ref[r, :, cols])
        sum_ref[index] = summed
        top_ref[index] = jnp.broadcast_to(top, (queries, 128))
        tot_ref[index] = jnp.broadcast_to(total, (queries, 128))


def prompt_kernel(span, *refs):
    messages, info_ref = refs[:2], refs[2]
    chunk_refs, outs = refs[3:-3], refs[-2:]
    queries = messages[0].shape[0] - 2 * span
    seqs, seq = lax.axis_size("seq"), lax.axis_index("seq")
    prompts, length, _ = chunk_refs[0].shape
    q = jnp.concatenate([m[:queries, :] for m in messages], axis=0)
    columns = []
    for m in messages:
        eight = m[queries : queries + 2 * span, :].astype(jnp.float32)[:span, :1]
        columns += [eight] * (queries // span)
    prompt = jnp.concatenate(columns, axis=0).astype(jnp.int32)
    limit = select_rows(prompt, [jnp.broadcast_to(info_ref[r : r + 1, :1], prompt.shape) for r in range(prompts)])
    parts = []
    for index in range(seqs):
        base = (seq + seqs - 2 * (index // 2)) % seqs
        chunk = base + (index % 2) * (1 - 2 * (seq % 2))
        keys = chunk_refs[2 * index]
        position = chunk * length + lax.broadcasted_iota(jnp.int32, (q.shape[0], length), 1)
        part = select_rows(prompt, [scores_of(q, keys[r]) for r in range(prompts)])
        parts.append(jnp.where(position < limit, part * EXP2_SCALE, MASKED_SCORE))
    top = lane_max(jnp.concatenate(parts, axis=1))
    summed = jnp.zeros((q.shape[0], D_HEAD), jnp.float32)
    total = jnp.zeros((q.shape[0], 1), jnp.float32)
    for index, part in enumerate(parts):
        weights = jnp.exp2(part - top)
        total = total + lane_sum(weights)
        for r in range(prompts):
            summed = summed + weighted(jnp.where(prompt == r, weights, 0.0), chunk_refs[2 * index + 1][r])
    for index, out in enumerate(outs):
        rows = slice(index * queries, (index + 1) * queries)
        stats = terms_of(column_to_row(top[rows])) + terms_of(column_to_row(total[rows]))
        stats = jnp.concatenate(stats + [jnp.zeros((16 - len(stats), 128), jnp.float32)], axis=0)
        out[:queries, :] = summed[rows].astype(out.dtype)
        out[queries : queries + 16, :] = stats.astype(out.dtype)


def local_heads(block, with_near, q_ref, k_own, k_near, wide, outs):
    row, start, stop = block
    length = q_ref.shape[1]
    sum_ref, top_ref, tot_ref = outs
    causal = lax.broadcasted_iota(jnp.int32, (length, length), 1) <= lax.broadcasted_iota(
        jnp.int32, (length, length), 0
    )
    for head in range(start, stop):
        cols = slice((head - start) * D_HEAD, (head - start + 1) * D_HEAD)
        q = q_ref[row, :, head * D_HEAD : (head + 1) * D_HEAD]
        scores = jnp.where(causal, scores_of(q, k_own[row]), MASKED_SCORE)
        if with_near:
            scores = jnp.concatenate([scores, scores_of(q, k_near[row])], axis=1)
        top = jnp.max(scores, axis=1, keepdims=True) * EXP2_SCALE
        summed = weighted(jnp.exp2(scores * EXP2_SCALE - top), wide[row, : scores.shape[1], :])
        sum_ref[:, cols] = summed[:, :D_HEAD]
        tot_ref[:, cols] = summed[:, D_HEAD:]
        top_ref[:, cols] = jnp.broadcast_to(top, (length, D_HEAD))


def widen(rows, v_one, v_two, wide):
    length = v_one.shape[1]
    for row in rows:
        wide[row, :length, :D_HEAD] = v_one[row]
        wide[row, length:, :D_HEAD] = v_two[row]
        wide[row, :, D_HEAD:] = jnp.ones((2 * length, D_HEAD), jnp.bfloat16)


def local_kernel(blocks, shift, q_ref, k_own, v_own, k_near, v_near, _, *refs):
    outs, wide = refs[:-1], refs[-1]
    prompts = q_ref.shape[0]
    seq = lax.axis_index("seq")
    widen(range(prompts), v_own, v_near, wide)

    def run(some, with_near):
        for index in some:
            local_heads(blocks[index], with_near, q_ref, k_own, k_near, wide, outs[3 * index : 3 * index + 3])

    for core in range(2):

        @pl.when(seq % 2 == core)
        def _(core=core):
            run(range(len(blocks) - 1), core == 1)

            @pl.when(seq // 2 >= shift)
            def _():
                run([len(blocks) - 1], core == 1)


def window_kernel(blocks, shift, keep, q_ref, k_own, v_own, k_near, v_near, k_one, v_one, _, *refs):
    first_in, last_in, first_out, last_out = (refs[3 * i : 3 * i + 3] for i in range(4))
    wide = refs[-1]
    seq = lax.axis_index("seq")
    length = q_ref.shape[1]
    late = seq // 2 >= shift

    def emit(index, row, cols, at, summed, total, top):
        for ref, value in zip(first_out, (summed, top, total)):
            ref[:, at] = value

    @pl.when(late)
    def _():
        widen([0], v_one, v_one, wide)
        add_blocks([(0, *blocks[0])], lambda index, row: ([k_one[row]], wide[row, :length]), q_ref, first_in, emit)
        if keep:
            for ref, value in zip(last_out, last_in):
                ref[...] = value[...]

    @pl.when(jnp.logical_not(late))
    def _():
        widen([blocks[-1][0]], v_own, v_near, wide)
        for core in range(2):

            @pl.when(seq % 2 == core)
            def _(core=core):
                local_heads(blocks[-1], core == 1, q_ref, k_own, k_near, wide, last_out)

        if keep:
            for ref, value in zip(first_out, first_in):
                ref[...] = value[...]


def merged(span, group, cache_sum, cache_top, cache_tot, part):
    queries = group * span
    stats = part[queries : queries + 16, :].astype(jnp.float32)
    top = row_to_column(sum_of_terms(stats, 0), queries)
    total = row_to_column(sum_of_terms(stats, 3), queries)
    high = jnp.maximum(top, cache_top)
    one, two = jnp.exp2(cache_top - high), jnp.exp2(top - high)
    result = (one * cache_sum + two * part[:queries, :].astype(jnp.float32)) / (one * cache_tot + two * total)
    return jnp.concatenate([result[head * span : (head + 1) * span] for head in range(group)], axis=1)


def joined(q, keys):
    return jnp.concatenate([scores_of(q, one) for one in keys], axis=1)


def add_keys(q, keys, wide, summed, total, top):
    scores = joined(q, keys)
    new = jnp.maximum(top, jnp.max(scores, axis=1, keepdims=True) * EXP2_SCALE)
    high = jnp.concatenate([new] * (scores.shape[1] // D_HEAD), axis=1)
    far = weighted(jnp.exp2(scores * EXP2_SCALE - high), wide)
    alpha = jnp.exp2(top - new)
    return summed * alpha + far[:, :D_HEAD], total * alpha + far[:, D_HEAD:], new


def add_keys_at(q, keys, wide, summed, total, top):
    scores = joined(q, keys)
    high = jnp.concatenate([top] * (scores.shape[1] // D_HEAD), axis=1)
    far = weighted(jnp.exp2(scores * EXP2_SCALE - high), wide)
    return summed + far[:, :D_HEAD], total + far[:, D_HEAD:]


def add_blocks(blocks, far_of, q_ref, states, emit, row_done=None, before=None, after=None):
    length = q_ref.shape[1]

    def state_of(index, at):
        return (states[3 * index][:, at], states[3 * index + 2][:, at], states[3 * index + 1][:, at])

    worst = jnp.zeros((8, D_HEAD), jnp.float32)
    for index, row, start, stop in blocks:
        for head in range(start, stop):
            cols = slice(head * D_HEAD, (head + 1) * D_HEAD)
            at = slice((head - start) * D_HEAD, (head - start + 1) * D_HEAD)
            state = state_of(index, at)
            summed, total = add_keys_at(q_ref[row, :, cols], *far_of(index, row), *state)
            emit(index, row, cols, at, summed, total, state[2])
            if row_done and cols.stop == q_ref.shape[2]:
                row_done(row)
            peaks = [total[i : i + 8] for i in range(0, length, 8)]
            worst = functools.reduce(jnp.maximum, [functools.reduce(jnp.maximum, peaks[i::4]) for i in range(4)], worst)

    if before:
        before()

    @pl.when(jnp.max(worst) > SUM_LIMIT)
    def _():
        for index, row, start, stop in blocks:

            @pl.loop(0, stop - start)
            def _(head, index=index, row=row, start=start):
                at = pl.ds(pl.multiple_of(head * D_HEAD, D_HEAD), D_HEAD)
                cols = pl.ds(pl.multiple_of((start + head) * D_HEAD, D_HEAD), D_HEAD)
                new = add_keys(q_ref[row, :, cols], *far_of(index, row), *state_of(index, at))
                emit(index, row, cols, at, *new)

        if after:
            after()


def far_kernel(blocks, chosen, shift, last, span, info_ref, q_ref, k_one, v_one, k_two, v_two, _, *refs):
    _, length, columns = q_ref.shape
    group = columns // D_HEAD
    count = 3 * len(blocks)
    states, others, outs, (wide, sem) = refs[:count], refs[count : 2 * count], refs[2 * count : -2], refs[-2:]
    if last:
        (cache_sum, cache_top, cache_tot, own_part), outs = outs[:4], outs[4:]
        outs[2][...] = merged(span, group, cache_sum[0], cache_top[0], cache_tot[0], own_part)
    seq = lax.axis_index("seq")
    position = seq * length + lax.broadcasted_iota(jnp.int32, (length, D_HEAD), 0)
    places = [(index, *block) for index, block in enumerate(blocks)]

    def far_of(index, row):
        first, stop = chosen[index][0] * length, (chosen[index][-1] + 1) * length
        return [(k_one, k_two)[i][row] for i in chosen[index]], wide[row, first:stop]

    def emit(index, row, cols, at, summed, total, top):
        if last:
            live = position < info_ref[row : row + 1, :]
            outs[0][row, :, cols] = jnp.where(live, summed / total, 0.0).astype(jnp.bfloat16)
        else:
            for ref, value in zip(outs[3 * index : 3 * index + 3], (summed, top, total)):
                ref[:, at] = value

    hooks = {}
    if last:
        first_copy = pltpu.make_async_copy(outs[0].at[0], outs[1].at[0], sem)

        def row_done(row):
            if row == 0:
                first_copy.start()

        def after():
            first_copy.start()
            first_copy.wait()

        hooks = {"row_done": row_done, "before": first_copy.wait, "after": after}

    @pl.when(seq // 2 >= shift)
    def _():
        widen(range(q_ref.shape[0]), v_one, v_two, wide)
        add_blocks(places, far_of, q_ref, states, emit, **hooks)

    @pl.when(seq // 2 < shift)
    def _():
        for index, row, start, stop in places:

            @pl.loop(0, stop - start)
            def _(head, index=index, row=row, start=start):
                at = pl.ds(pl.multiple_of(head * D_HEAD, D_HEAD), D_HEAD)
                cols = pl.ds(pl.multiple_of((start + head) * D_HEAD, D_HEAD), D_HEAD)
                kept = others[3 * index : 3 * index + 3]
                emit(index, row, cols, at, kept[0][:, at], kept[2][:, at], kept[1][:, at])

        if last:
            copy = pltpu.make_async_copy(outs[0], outs[1], sem)
            copy.start()
            copy.wait()


def finish_kernel(
    shift, span, pre, own_rows, cache_sum, cache_top, cache_tot, other_part, _, dec_hbm, pre_hbm, dec, flat, sems
):
    copy = pltpu.make_async_copy(pre.at[1:], pre_hbm.at[1:], sems.at[0])
    dec_copy = pltpu.make_async_copy(dec, dec_hbm, sems.at[1])
    late = lax.axis_index("seq") // 2 >= shift
    role = lax.axis_index("role")

    @pl.when(late)
    def _():
        copy.start()

    steps, rows, columns = dec.shape
    half = columns // 2
    flat[:, pl.ds(pl.multiple_of(role * half, half), half)] = own_rows[...]
    other = merged(span, half // D_HEAD, cache_sum[1], cache_top[1], cache_tot[1], other_part)
    flat[:, pl.ds(pl.multiple_of((1 - role) * half, half), half)] = other
    for step in range(steps):
        dec[step] = flat[step * rows : (step + 1) * rows, :].astype(jnp.bfloat16)
    dec_copy.start()

    @pl.when(late)
    def _():
        copy.wait()

    dec_copy.wait()


VMEM = pl.BlockSpec(memory_space=pltpu.VMEM)
ANY = pl.BlockSpec(memory_space=pl.ANY)


def in_hbm(x):
    return pltpu.with_memory_space_constraint(x, pltpu.HBM)


def call(kernel, args, outs, scratch=(), specs=None, out_specs=None, aliases=None, us=1.0):
    return pl.pallas_call(
        kernel,
        out_shape=outs,
        in_specs=specs or [VMEM] * len(args),
        out_specs=out_specs or [VMEM] * len(outs),
        scratch_shapes=list(scratch),
        input_output_aliases=aliases or {},
        compiler_params=pltpu.CompilerParams(vmem_limit_bytes=VMEM_BYTES),
        cost_estimate=pl.CostEstimate(flops=int(us * 1.1e9), bytes_accessed=int(us * 3e6), transcendentals=0),
    )(*args)


def body(
    prefill_queries,
    prefill_keys,
    prefill_values,
    prompt_len,
    assignment,
    cache_len,
    cache_keys,
    cache_values,
    decode_queries,
    new_keys,
    new_values,
):
    seqs = lax.axis_size("seq")
    prompts, length, columns = prefill_queries.shape
    steps, rows, dec_columns = decode_queries.shape
    group = columns // D_HEAD
    span = steps * rows
    queries = group * span
    f32, bf16, i32 = jnp.float32, jnp.bfloat16, jnp.int32
    shape = jax.ShapeDtypeStruct
    after = lax.optimization_barrier

    def near(x):
        return lax.ppermute(x, "seq", [(i, i ^ 1) for i in range(seqs)])

    def around(x, shift):
        return lax.ppermute(x, "seq", [(i, (i + 2 * shift) % seqs) for i in range(seqs)])

    def partner(x):
        moves = [(i * 2 + r, (i ^ 1) * 2 + 1 - r) for i in range(seqs) for r in range(2)]
        return lax.ppermute(x, ("seq", "role"), moves)

    shifts = range(1, seqs // 2)
    far_keys = [around(prefill_keys, s) for s in shifts]
    far_values = [around(prefill_values, s) for s in shifts]
    (first,) = call(first_kernel, [in_hbm(prompt_len)], [shape((span, 128), f32)], specs=[ANY], us=3.0)
    own_keys, own_values, first = after((prefill_keys, prefill_values, first))
    near_keys, near_values = near(own_keys), near(own_values)
    message = shape((queries + 2 * span, 128), bf16)
    state = shape((2, queries, 128), f32)
    own_msg, other_msg, info, *cache = call(
        own_kernel,
        [in_hbm(x) for x in (assignment, prompt_len, cache_len, decode_queries, new_keys, new_values)]
        + [cache_keys, cache_values, first],
        [message] * 2 + [shape((span, 128), i32)] + [state] * 3,
        [
            pltpu.SMEM(assignment.shape, i32),
            pltpu.SMEM(prompt_len.shape, i32),
            pltpu.SMEM(cache_len.shape, i32),
            pltpu.VMEM(decode_queries.shape, bf16),
            pltpu.VMEM(new_keys.shape, bf16),
            pltpu.VMEM(new_values.shape, bf16),
            pltpu.VMEM((span, dec_columns), f32),
            pltpu.VMEM((128, 2 * D_HEAD), f32),
            pltpu.VMEM((128, 2 * D_HEAD), f32),
            pltpu.SemaphoreType.DMA((6,)),
        ],
        specs=[ANY] * 6 + [VMEM] * 2 + [ANY],
        us=1.3,
    )
    partner_msg = partner(other_msg)
    blocks = []
    for row in range(prompts):
        cut = row == 0 or row == prompts - 1
        blocks += [(row, 0, group // 2), (row, group // 2, group)] if cut else [(row, 0, group)]
    runs = [[shape((length, (stop - start) * D_HEAD), f32)] * 3 for _, start, stop in blocks]

    last_shift = shifts[-1]
    wide = pltpu.VMEM((prompts, 2 * length, 2 * D_HEAD), bf16)
    mine = (prefill_queries, prefill_keys, prefill_values, near_keys, near_values)
    states = call(
        functools.partial(local_kernel, blocks, last_shift),
        (*mine, info),
        sum(runs, []),
        [wide],
        specs=[VMEM] * 5 + [ANY],
        us=2.6,
    )
    far_values, partner_msg, states = after((far_values, partner_msg, states))
    far_near_values = [near(v) for v in far_values]
    far_keys, states = after((far_keys, states))
    far_near_keys = [near(k) for k in far_keys]
    keep = len(shifts) > 1
    window = call(
        functools.partial(window_kernel, blocks, last_shift, keep),
        (*mine, far_keys[-1], far_values[-1], info, *states[:3], *states[-3:]),
        runs[0] + runs[-1],
        [wide],
        specs=[VMEM] * 7 + [ANY] + [VMEM] * 6,
        us=1.0,
    )
    others = [*states[:-3], *window[3:]]
    states = [*window[:3], *states[3:]]
    if keep:
        states = others = [*window[:3], *states[3:-3], *window[3:]]
    far = list(zip(far_keys, far_values, far_near_keys, far_near_values))
    chunks = [prefill_keys, prefill_values, near_keys, near_values] + sum([list(four) for four in far], [])
    parts = [shape((queries + 16, 128), f32), shape((queries + 16, 128), bf16)]
    own_part, partner_part = call(
        functools.partial(prompt_kernel, span),
        (own_msg, partner_msg, info, *chunks, window[0]),
        parts,
        specs=[VMEM] * (3 + len(chunks)) + [ANY],
        us=0.7,
    )
    other_part = partner(partner_part)
    for index, shift in enumerate(shifts):
        last = index == len(shifts) - 1
        chosen = [(1,) if last and number == 0 else (0, 1) for number in range(len(blocks))]
        outs, out_specs, extra = sum(runs, []), [VMEM] * len(states), []
        if last:
            outs = [shape(prefill_queries.shape, bf16)] * 2 + [shape((span, dec_columns // 2), f32)]
            out_specs, extra = [VMEM, ANY, VMEM], [*cache, own_part]
        states = others = call(
            functools.partial(far_kernel, blocks, chosen, shift, last, span),
            (info, prefill_queries, *far[index], own_part, *states, *others, *extra),
            outs,
            [wide, pltpu.SemaphoreType.DMA(())],
            specs=[VMEM] * 6 + [ANY] + [VMEM] * (2 * len(states) + len(extra)),
            out_specs=out_specs,
            us=2.4,
        )
    pre, prefill_out, own_rows = states
    decode_out, prefill_out = call(
        functools.partial(finish_kernel, shifts[-1], span),
        (pre, own_rows, *cache, other_part, prefill_out),
        [shape(decode_queries.shape, bf16), shape(prefill_queries.shape, bf16)],
        [
            pltpu.VMEM(decode_queries.shape, bf16),
            pltpu.VMEM((span, dec_columns), f32),
            pltpu.SemaphoreType.DMA((2,)),
        ],
        specs=[VMEM] * 6 + [ANY],
        out_specs=[ANY, ANY],
        aliases={6: 1},
        us=0.7,
    )
    return prefill_out, decode_out


def solution(mesh):
    in_specs = (
        P(None, "seq", ("head", "role")),
        P(None, "seq", ("head", "role")),
        P(None, "seq", ("head", "role")),
        P(),
        P(("seq", "role")),
        P(("seq", "role")),
        P(("seq", "role"), None, "head"),
        P(("seq", "role"), None, "head"),
        P(None, ("seq", "role"), "head"),
        P(None, ("seq", "role"), "head"),
        P(None, ("seq", "role"), "head"),
    )
    out_specs = (P(None, "seq", ("head", "role")), P(None, ("seq", "role"), "head"))
    return jax.shard_map(body, mesh=mesh, in_specs=in_specs, out_specs=out_specs, check_vma=False)
```

```python
import functools
import math

import jax
import jax.numpy as jnp
from jax import lax
from jax.experimental import pallas as pl
from jax.experimental.pallas import tpu as pltpu
from jax.sharding import PartitionSpec as P

D_HEAD = 128
MASKED_SCORE = -1e30
EXP2_SCALE = D_HEAD**-0.5 * math.log2(math.e)
VMEM_BYTES = 40 * 2**20
SUM_LIMIT = 2.0**100
NT = (((1,), (1,)), ((), ()))


def scores_of(queries, keys):
    return lax.dot_general(queries, keys, NT, preferred_element_type=jnp.float32)


def weighted(weights, values):
    return jnp.dot(weights.astype(jnp.bfloat16), values, preferred_element_type=jnp.float32)


def eye_of(rows):
    shape = (rows, 128)
    return lax.broadcasted_iota(jnp.int32, shape, 0) == lax.broadcasted_iota(jnp.int32, shape, 1)


def column_to_row(column):
    spread = jnp.where(eye_of(column.shape[0]), column, 0.0)
    return jnp.sum(spread, axis=0, keepdims=True)


def row_to_column(row, rows):
    spread = jnp.where(eye_of(rows), jnp.broadcast_to(row, (rows, 128)), 0.0)
    return jnp.sum(spread, axis=1, keepdims=True)


def terms_of(x):
    terms = []
    for _ in range(3):
        terms.append(x.astype(jnp.bfloat16).astype(jnp.float32))
        x = x - terms[-1]
    return terms


def sum_of_terms(block, first):
    return block[first : first + 1] + block[first + 1 : first + 2] + block[first + 2 : first + 3]


def select_rows(index, parts):
    chosen = parts[-1]
    for number in range(len(parts) - 2, -1, -1):
        chosen = jnp.where(index == number, parts[number], chosen)
    return chosen


def lane_sum(x):
    tiles = [x[:, i : i + 128] for i in range(0, x.shape[1], 128)]
    return jnp.sum(functools.reduce(jnp.add, tiles), axis=1, keepdims=True)


def lane_max(x):
    tiles = [x[:, i : i + 128] for i in range(0, x.shape[1], 128)]
    return jnp.max(functools.reduce(jnp.maximum, tiles), axis=1, keepdims=True)


def first_kernel(_, out_ref):
    out_ref[...] = jnp.zeros_like(out_ref)


def own_kernel(
    asg_hbm, plen_hbm, clen_hbm, dq_hbm, nk_hbm, nv_hbm, ck_ref, cv_ref, _,
    own_ref, other_ref, info_ref, sum_ref, top_ref, tot_ref, asg, plen, clen, dq, nk, nv, flat, fk, fv, sems,
):
    moves = [(dq_hbm, dq), (nk_hbm, nk), (nv_hbm, nv), (asg_hbm, asg), (plen_hbm, plen), (clen_hbm, clen)]
    copies = [pltpu.make_async_copy(a, b, sems.at[i]) for i, (a, b) in enumerate(moves)]
    for copy in copies:
        copy.start()
    role = lax.axis_index("role")
    steps, rows, columns = dq.shape
    span = steps * rows
    half = columns // 2
    group = half // D_HEAD
    queries = group * span
    slots = ck_ref.shape[1]
    fk[...] = jnp.zeros_like(fk)
    fv[...] = jnp.zeros_like(fv)
    for copy in copies:
        copy.wait()
    for step in range(steps):
        at = slice(step * rows, (step + 1) * rows)
        flat[at, :] = dq[step].astype(jnp.float32)
        fk[at, :] = nk[step].astype(jnp.float32)
        fv[at, :] = nv[step].astype(jnp.float32)
    q_index = lax.broadcasted_iota(jnp.int32, (queries, 1), 0) % span
    q_step, q_row = q_index // rows, q_index % rows
    lane = lax.broadcasted_iota(jnp.int32, (queries, 128), 1)
    fresh_mask = (lane < span) & (lane % rows == q_row) & (lane // rows <= q_step)
    sides = ((own_ref, role), (other_ref, 1 - role))
    slices = [pl.ds(pl.multiple_of(kv * D_HEAD, D_HEAD), D_HEAD) for _, kv in sides]
    scores = []
    for (out, kv), cols in zip(sides, slices):
        heads = [flat[:, pl.ds(pl.multiple_of(kv * half + i * D_HEAD, D_HEAD), D_HEAD)] for i in range(group)]
        q = jnp.concatenate(heads, axis=0).astype(jnp.bfloat16)
        out[:queries, :] = q
        fresh = scores_of(q, fk[:, cols].astype(jnp.bfloat16))
        fresh = jnp.where(fresh_mask, fresh * EXP2_SCALE, MASKED_SCORE)
        scores.append((fresh, select_rows(q_row, [scores_of(q, ck_ref[r, :, cols]) for r in range(rows)])))
    row_index = lax.broadcasted_iota(jnp.int32, (span, 128), 0)
    prompt = jnp.zeros((span, 128), jnp.float32)
    for row in range(rows):
        prompt = jnp.where(row_index % rows == row, asg[row].astype(jnp.float32), prompt)
    info = jnp.zeros((span, 128), jnp.int32)
    for row in range(plen.shape[0]):
        info = jnp.where(row_index == row, plen[row], info)
    info_ref[...] = info
    limit = select_rows(q_row, [clen[r] for r in range(rows)])
    live = lax.broadcasted_iota(jnp.int32, (queries, slots), 1) < limit
    for index, ((out, _), cols, (fresh, old)) in enumerate(zip(sides, slices, scores)):
        out[queries : queries + 2 * span, :] = jnp.concatenate([prompt, prompt], axis=0).astype(jnp.bfloat16)
        old = jnp.where(live, old * EXP2_SCALE, MASKED_SCORE)
        top = jnp.maximum(lane_max(fresh), lane_max(old))
        fresh = jnp.exp2(fresh - top)
        old = jnp.exp2(old - top)
        total = lane_sum(fresh) + lane_sum(old)
        summed = weighted(fresh, fv[:, cols].astype(jnp.bfloat16))
        for r in range(rows):
            summed = summed + weighted(jnp.where(q_row == r, old, 0.0), cv_ref[r, :, cols])
        sum_ref[index] = summed
        top_ref[index] = jnp.broadcast_to(top, (queries, 128))
        tot_ref[index] = jnp.broadcast_to(total, (queries, 128))


def prompt_kernel(span, *refs):
    messages, info_ref = refs[:2], refs[2]
    chunk_refs, outs = refs[3:-3], refs[-2:]
    queries = messages[0].shape[0] - 2 * span
    seqs, seq = lax.axis_size("seq"), lax.axis_index("seq")
    prompts, length, _ = chunk_refs[0].shape
    q = jnp.concatenate([m[:queries, :] for m in messages], axis=0)
    columns = []
    for m in messages:
        eight = m[queries : queries + 2 * span, :].astype(jnp.float32)[:span, :1]
        columns += [eight] * (queries // span)
    prompt = jnp.concatenate(columns, axis=0).astype(jnp.int32)
    limit = select_rows(prompt, [jnp.broadcast_to(info_ref[r : r + 1, :1], prompt.shape) for r in range(prompts)])
    parts = []
    for index in range(seqs):
        base = (seq + seqs - 2 * (index // 2)) % seqs
        chunk = base + (index % 2) * (1 - 2 * (seq % 2))
        keys = chunk_refs[2 * index]
        position = chunk * length + lax.broadcasted_iota(jnp.int32, (q.shape[0], length), 1)
        part = select_rows(prompt, [scores_of(q, keys[r]) for r in range(prompts)])
        parts.append(jnp.where(position < limit, part * EXP2_SCALE, MASKED_SCORE))
    top = lane_max(jnp.concatenate(parts, axis=1))
    summed = jnp.zeros((q.shape[0], D_HEAD), jnp.float32)
    total = jnp.zeros((q.shape[0], 1), jnp.float32)
    for index, part in enumerate(parts):
        weights = jnp.exp2(part - top)
        total = total + lane_sum(weights)
        for r in range(prompts):
            summed = summed + weighted(jnp.where(prompt == r, weights, 0.0), chunk_refs[2 * index + 1][r])
    for index, out in enumerate(outs):
        rows = slice(index * queries, (index + 1) * queries)
        stats = terms_of(column_to_row(top[rows])) + terms_of(column_to_row(total[rows]))
        stats = jnp.concatenate(stats + [jnp.zeros((16 - len(stats), 128), jnp.float32)], axis=0)
        out[:queries, :] = summed[rows].astype(out.dtype)
        out[queries : queries + 16, :] = stats.astype(out.dtype)


def local_heads(block, with_near, q_ref, k_own, k_near, wide, outs):
    row, start, stop = block
    length = q_ref.shape[1]
    sum_ref, top_ref, tot_ref = outs
    causal = lax.broadcasted_iota(jnp.int32, (length, length), 1) <= lax.broadcasted_iota(
        jnp.int32, (length, length), 0
    )
    for head in range(start, stop):
        cols = slice((head - start) * D_HEAD, (head - start + 1) * D_HEAD)
        q = q_ref[row, :, head * D_HEAD : (head + 1) * D_HEAD]
        scores = jnp.where(causal, scores_of(q, k_own[row]), MASKED_SCORE)
        if with_near:
            scores = jnp.concatenate([scores, scores_of(q, k_near[row])], axis=1)
        top = jnp.max(scores, axis=1, keepdims=True) * EXP2_SCALE
        summed = weighted(jnp.exp2(scores * EXP2_SCALE - top), wide[row, : scores.shape[1], :])
        sum_ref[:, cols] = summed[:, :D_HEAD]
        tot_ref[:, cols] = summed[:, D_HEAD:]
        top_ref[:, cols] = jnp.broadcast_to(top, (length, D_HEAD))


def widen(rows, v_one, v_two, wide):
    length = v_one.shape[1]
    for row in rows:
        wide[row, :length, :D_HEAD] = v_one[row]
        wide[row, length:, :D_HEAD] = v_two[row]
        wide[row, :, D_HEAD:] = jnp.ones((2 * length, D_HEAD), jnp.bfloat16)


def local_kernel(blocks, shift, q_ref, k_own, v_own, k_near, v_near, _, *refs):
    outs, wide = refs[:-1], refs[-1]
    prompts = q_ref.shape[0]
    seq = lax.axis_index("seq")
    widen(range(prompts), v_own, v_near, wide)

    def run(some, with_near):
        for index in some:
            local_heads(blocks[index], with_near, q_ref, k_own, k_near, wide, outs[3 * index : 3 * index + 3])

    for core in range(2):

        @pl.when(seq % 2 == core)
        def _(core=core):
            run(range(len(blocks) - 1), core == 1)

            @pl.when(seq // 2 >= shift)
            def _():
                run([len(blocks) - 1], core == 1)


def window_kernel(blocks, shift, keep, q_ref, k_own, v_own, k_near, v_near, k_one, v_one, _, *refs):
    first_in, last_in, first_out, last_out = (refs[3 * i : 3 * i + 3] for i in range(4))
    wide = refs[-1]
    seq = lax.axis_index("seq")
    length = q_ref.shape[1]
    late = seq // 2 >= shift

    def emit(index, row, cols, at, summed, total, top):
        for ref, value in zip(first_out, (summed, top, total)):
            ref[:, at] = value

    @pl.when(late)
    def _():
        widen([0], v_one, v_one, wide)
        add_blocks([(0, *blocks[0])], lambda index, row: ([k_one[row]], wide[row, :length]), q_ref, first_in, emit)
        if keep:
            for ref, value in zip(last_out, last_in):
                ref[...] = value[...]

    @pl.when(jnp.logical_not(late))
    def _():
        widen([blocks[-1][0]], v_own, v_near, wide)
        for core in range(2):

            @pl.when(seq % 2 == core)
            def _(core=core):
                local_heads(blocks[-1], core == 1, q_ref, k_own, k_near, wide, last_out)

        if keep:
            for ref, value in zip(first_out, first_in):
                ref[...] = value[...]


def merged(span, group, cache_sum, cache_top, cache_tot, part):
    queries = group * span
    stats = part[queries : queries + 16, :].astype(jnp.float32)
    top = row_to_column(sum_of_terms(stats, 0), queries)
    total = row_to_column(sum_of_terms(stats, 3), queries)
    high = jnp.maximum(top, cache_top)
    one, two = jnp.exp2(cache_top - high), jnp.exp2(top - high)
    result = (one * cache_sum + two * part[:queries, :].astype(jnp.float32)) / (one * cache_tot + two * total)
    return jnp.concatenate([result[head * span : (head + 1) * span] for head in range(group)], axis=1)


def joined(q, keys):
    return jnp.concatenate([scores_of(q, one) for one in keys], axis=1)


def add_keys(q, keys, wide, summed, total, top):
    scores = joined(q, keys)
    new = jnp.maximum(top, jnp.max(scores, axis=1, keepdims=True) * EXP2_SCALE)
    high = jnp.concatenate([new] * (scores.shape[1] // D_HEAD), axis=1)
    far = weighted(jnp.exp2(scores * EXP2_SCALE - high), wide)
    alpha = jnp.exp2(top - new)
    return summed * alpha + far[:, :D_HEAD], total * alpha + far[:, D_HEAD:], new


def add_keys_at(q, keys, wide, summed, total, top):
    scores = joined(q, keys)
    high = jnp.concatenate([top] * (scores.shape[1] // D_HEAD), axis=1)
    far = weighted(jnp.exp2(scores * EXP2_SCALE - high), wide)
    return summed + far[:, :D_HEAD], total + far[:, D_HEAD:]


def add_blocks(blocks, far_of, q_ref, states, emit, row_done=None, before=None, after=None):
    length = q_ref.shape[1]

    def state_of(index, at):
        return (states[3 * index][:, at], states[3 * index + 2][:, at], states[3 * index + 1][:, at])

    worst = jnp.zeros((8, D_HEAD), jnp.float32)
    for index, row, start, stop in blocks:
        for head in range(start, stop):
            cols = slice(head * D_HEAD, (head + 1) * D_HEAD)
            at = slice((head - start) * D_HEAD, (head - start + 1) * D_HEAD)
            state = state_of(index, at)
            summed, total = add_keys_at(q_ref[row, :, cols], *far_of(index, row), *state)
            emit(index, row, cols, at, summed, total, state[2])
            if row_done and cols.stop == q_ref.shape[2]:
                row_done(row)
            peaks = [total[i : i + 8] for i in range(0, length, 8)]
            worst = functools.reduce(jnp.maximum, [functools.reduce(jnp.maximum, peaks[i::4]) for i in range(4)], worst)

    if before:
        before()

    @pl.when(jnp.max(worst) > SUM_LIMIT)
    def _():
        for index, row, start, stop in blocks:

            @pl.loop(0, stop - start)
            def _(head, index=index, row=row, start=start):
                at = pl.ds(pl.multiple_of(head * D_HEAD, D_HEAD), D_HEAD)
                cols = pl.ds(pl.multiple_of((start + head) * D_HEAD, D_HEAD), D_HEAD)
                new = add_keys(q_ref[row, :, cols], *far_of(index, row), *state_of(index, at))
                emit(index, row, cols, at, *new)

        if after:
            after()


def far_kernel(blocks, chosen, shift, last, span, info_ref, q_ref, k_one, v_one, k_two, v_two, _, *refs):
    _, length, columns = q_ref.shape
    group = columns // D_HEAD
    count = 3 * len(blocks)
    states, others, outs, (wide, sem) = refs[:count], refs[count : 2 * count], refs[2 * count : -2], refs[-2:]
    if last:
        (cache_sum, cache_top, cache_tot, own_part), outs = outs[:4], outs[4:]
        outs[2][...] = merged(span, group, cache_sum[0], cache_top[0], cache_tot[0], own_part)
    seq = lax.axis_index("seq")
    position = seq * length + lax.broadcasted_iota(jnp.int32, (length, D_HEAD), 0)
    places = [(index, *block) for index, block in enumerate(blocks)]

    def far_of(index, row):
        first, stop = chosen[index][0] * length, (chosen[index][-1] + 1) * length
        return [(k_one, k_two)[i][row] for i in chosen[index]], wide[row, first:stop]

    def emit(index, row, cols, at, summed, total, top):
        if last:
            live = position < info_ref[row : row + 1, :]
            outs[0][row, :, cols] = jnp.where(live, summed / total, 0.0).astype(jnp.bfloat16)
        else:
            for ref, value in zip(outs[3 * index : 3 * index + 3], (summed, top, total)):
                ref[:, at] = value

    hooks = {}
    if last:
        first_copy = pltpu.make_async_copy(outs[0].at[0], outs[1].at[0], sem)

        def row_done(row):
            if row == 0:
                first_copy.start()

        def after():
            first_copy.start()
            first_copy.wait()

        hooks = {"row_done": row_done, "before": first_copy.wait, "after": after}

    @pl.when(seq // 2 >= shift)
    def _():
        widen(range(q_ref.shape[0]), v_one, v_two, wide)
        add_blocks(places, far_of, q_ref, states, emit, **hooks)

    @pl.when(seq // 2 < shift)
    def _():
        for index, row, start, stop in places:

            @pl.loop(0, stop - start)
            def _(head, index=index, row=row, start=start):
                at = pl.ds(pl.multiple_of(head * D_HEAD, D_HEAD), D_HEAD)
                cols = pl.ds(pl.multiple_of((start + head) * D_HEAD, D_HEAD), D_HEAD)
                kept = others[3 * index : 3 * index + 3]
                emit(index, row, cols, at, kept[0][:, at], kept[2][:, at], kept[1][:, at])

        if last:
            copy = pltpu.make_async_copy(outs[0], outs[1], sem)
            copy.start()
            copy.wait()


def finish_kernel(
    shift, span, pre, own_rows, cache_sum, cache_top, cache_tot, other_part, _, dec_hbm, pre_hbm, dec, flat, sems
):
    copy = pltpu.make_async_copy(pre.at[1:], pre_hbm.at[1:], sems.at[0])
    dec_copy = pltpu.make_async_copy(dec, dec_hbm, sems.at[1])
    late = lax.axis_index("seq") // 2 >= shift
    role = lax.axis_index("role")

    @pl.when(late)
    def _():
        copy.start()

    steps, rows, columns = dec.shape
    half = columns // 2
    flat[:, pl.ds(pl.multiple_of(role * half, half), half)] = own_rows[...]
    other = merged(span, half // D_HEAD, cache_sum[1], cache_top[1], cache_tot[1], other_part)
    flat[:, pl.ds(pl.multiple_of((1 - role) * half, half), half)] = other
    for step in range(steps):
        dec[step] = flat[step * rows : (step + 1) * rows, :].astype(jnp.bfloat16)
    dec_copy.start()

    @pl.when(late)
    def _():
        copy.wait()

    dec_copy.wait()


VMEM = pl.BlockSpec(memory_space=pltpu.VMEM)
ANY = pl.BlockSpec(memory_space=pl.ANY)


def in_hbm(x):
    return pltpu.with_memory_space_constraint(x, pltpu.HBM)


def call(kernel, args, outs, scratch=(), specs=None, out_specs=None, aliases=None, us=1.0):
    return pl.pallas_call(
        kernel,
        out_shape=outs,
        in_specs=specs or [VMEM] * len(args),
        out_specs=out_specs or [VMEM] * len(outs),
        scratch_shapes=list(scratch),
        input_output_aliases=aliases or {},
        compiler_params=pltpu.CompilerParams(vmem_limit_bytes=VMEM_BYTES),
        cost_estimate=pl.CostEstimate(flops=int(us * 1.1e9), bytes_accessed=int(us * 3e6), transcendentals=0),
    )(*args)


def body(
    prefill_queries,
    prefill_keys,
    prefill_values,
    prompt_len,
    assignment,
    cache_len,
    cache_keys,
    cache_values,
    decode_queries,
    new_keys,
    new_values,
):
    seqs = lax.axis_size("seq")
    prompts, length, columns = prefill_queries.shape
    steps, rows, dec_columns = decode_queries.shape
    group = columns // D_HEAD
    span = steps * rows
    queries = group * span
    f32, bf16, i32 = jnp.float32, jnp.bfloat16, jnp.int32
    shape = jax.ShapeDtypeStruct
    after = lax.optimization_barrier

    def near(x):
        return lax.ppermute(x, "seq", [(i, i ^ 1) for i in range(seqs)])

    def around(x, shift):
        return lax.ppermute(x, "seq", [(i, (i + 2 * shift) % seqs) for i in range(seqs)])

    def partner(x):
        moves = [(i * 2 + r, (i ^ 1) * 2 + 1 - r) for i in range(seqs) for r in range(2)]
        return lax.ppermute(x, ("seq", "role"), moves)

    shifts = range(1, seqs // 2)
    far_keys = [around(prefill_keys, s) for s in shifts]
    far_values = [around(prefill_values, s) for s in shifts]
    (first,) = call(first_kernel, [in_hbm(prompt_len)], [shape((span, 128), f32)], specs=[ANY], us=3.0)
    own_keys, own_values, first = after((prefill_keys, prefill_values, first))
    near_keys, near_values = near(own_keys), near(own_values)
    message = shape((queries + 2 * span, 128), bf16)
    state = shape((2, queries, 128), f32)
    own_msg, other_msg, info, *cache = call(
        own_kernel,
        [in_hbm(x) for x in (assignment, prompt_len, cache_len, decode_queries, new_keys, new_values)]
        + [cache_keys, cache_values, first],
        [message] * 2 + [shape((span, 128), i32)] + [state] * 3,
        [
            pltpu.SMEM(assignment.shape, i32),
            pltpu.SMEM(prompt_len.shape, i32),
            pltpu.SMEM(cache_len.shape, i32),
            pltpu.VMEM(decode_queries.shape, bf16),
            pltpu.VMEM(new_keys.shape, bf16),
            pltpu.VMEM(new_values.shape, bf16),
            pltpu.VMEM((span, dec_columns), f32),
            pltpu.VMEM((128, 2 * D_HEAD), f32),
            pltpu.VMEM((128, 2 * D_HEAD), f32),
            pltpu.SemaphoreType.DMA((6,)),
        ],
        specs=[ANY] * 6 + [VMEM] * 2 + [ANY],
        us=1.3,
    )
    partner_msg = partner(other_msg)
    blocks = []
    for row in range(prompts):
        cut = {prompts - 1: group // 2, 0: group // 4}.get(row)
        blocks += [(row, 0, cut), (row, cut, group)] if cut else [(row, 0, group)]
    runs = [[shape((length, (stop - start) * D_HEAD), f32)] * 3 for _, start, stop in blocks]

    last_shift = shifts[-1]
    wide = pltpu.VMEM((prompts, 2 * length, 2 * D_HEAD), bf16)
    mine = (prefill_queries, prefill_keys, prefill_values, near_keys, near_values)
    states = call(
        functools.partial(local_kernel, blocks, last_shift),
        (*mine, info),
        sum(runs, []),
        [wide],
        specs=[VMEM] * 5 + [ANY],
        us=2.6,
    )
    far_values, partner_msg, states = after((far_values, partner_msg, states))
    far_near_values = [near(v) for v in far_values]
    far_keys, states = after((far_keys, states))
    far_near_keys = [near(k) for k in far_keys]
    keep = len(shifts) > 1
    window = call(
        functools.partial(window_kernel, blocks, last_shift, keep),
        (*mine, far_keys[-1], far_values[-1], info, *states[:3], *states[-3:]),
        runs[0] + runs[-1],
        [wide],
        specs=[VMEM] * 7 + [ANY] + [VMEM] * 6,
        us=1.0,
    )
    others = [*states[:-3], *window[3:]]
    states = [*window[:3], *states[3:]]
    if keep:
        states = others = [*window[:3], *states[3:-3], *window[3:]]
    far = list(zip(far_keys, far_values, far_near_keys, far_near_values))
    chunks = [prefill_keys, prefill_values, near_keys, near_values] + sum([list(four) for four in far], [])
    parts = [shape((queries + 16, 128), f32), shape((queries + 16, 128), bf16)]
    own_part, partner_part = call(
        functools.partial(prompt_kernel, span),
        (own_msg, partner_msg, info, *chunks, window[0]),
        parts,
        specs=[VMEM] * (3 + len(chunks)) + [ANY],
        us=0.7,
    )
    other_part = partner(partner_part)
    for index, shift in enumerate(shifts):
        last = index == len(shifts) - 1
        chosen = [(1,) if last and number == 0 else (0, 1) for number in range(len(blocks))]
        outs, out_specs, extra = sum(runs, []), [VMEM] * len(states), []
        if last:
            outs = [shape(prefill_queries.shape, bf16)] * 2 + [shape((span, dec_columns // 2), f32)]
            out_specs, extra = [VMEM, ANY, VMEM], [*cache, own_part]
        states = others = call(
            functools.partial(far_kernel, blocks, chosen, shift, last, span),
            (info, prefill_queries, *far[index], own_part, *states, *others, *extra),
            outs,
            [wide, pltpu.SemaphoreType.DMA(())],
            specs=[VMEM] * 6 + [ANY] + [VMEM] * (2 * len(states) + len(extra)),
            out_specs=out_specs,
            us=2.4,
        )
    pre, prefill_out, own_rows = states
    decode_out, prefill_out = call(
        functools.partial(finish_kernel, shifts[-1], span),
        (pre, own_rows, *cache, other_part, prefill_out),
        [shape(decode_queries.shape, bf16), shape(prefill_queries.shape, bf16)],
        [
            pltpu.VMEM(decode_queries.shape, bf16),
            pltpu.VMEM((span, dec_columns), f32),
            pltpu.SemaphoreType.DMA((2,)),
        ],
        specs=[VMEM] * 6 + [ANY],
        out_specs=[ANY, ANY],
        aliases={6: 1},
        us=0.7,
    )
    return prefill_out, decode_out


def solution(mesh):
    in_specs = (
        P(None, "seq", ("head", "role")),
        P(None, "seq", ("head", "role")),
        P(None, "seq", ("head", "role")),
        P(),
        P(("seq", "role")),
        P(("seq", "role")),
        P(("seq", "role"), None, "head"),
        P(("seq", "role"), None, "head"),
        P(None, ("seq", "role"), "head"),
        P(None, ("seq", "role"), "head"),
        P(None, ("seq", "role"), "head"),
    )
    out_specs = (P(None, "seq", ("head", "role")), P(None, ("seq", "role"), "head"))
    return jax.shard_map(body, mesh=mesh, in_specs=in_specs, out_specs=out_specs, check_vma=False)
```
